32 devices in a mesh: tok: 8 (over y, x, core), head: 4 (over z).
Axes of the slice: x: 2, y: 2, z: 4, core: 2. Of those that a mesh axis runs over, the one named last changes fastest.
Arguments:
- patches: bfloat16 [8192, 768], P(('tok', 'head')), may hold values from -6 to 6
- classes: bfloat16 [2400, 768], P(('tok', 'head')), may hold values from -6 to 6
- slot_lengths: int32 [8, 2], P('tok'), may hold values from 64 to 960, as said below
- w_qkv: bfloat16 [768, 2304], P(('tok', 'head')), may hold values from -0.21875 to 0.21875
- w_out: bfloat16 [768, 768], P(('tok', 'head')), may hold values from -4 to 4
- w_up: bfloat16 [768, 3072], P(('tok', 'head')), may hold values from -0.21875 to 0.21875
- w_down: bfloat16 [3072, 768], P(('tok', 'head')), may hold values from -0.109375 to 0.109375
- w_patch: bfloat16 [768, 768], P(('tok', 'head')), may hold values from -0.21875 to 0.21875
- w_class: bfloat16 [768, 768], P(('tok', 'head')), may hold values from -0.21875 to 0.21875
- norm1: bfloat16 [768], P(('tok', 'head')), may hold values from 0.099609375 to 1.8984375
- norm2: bfloat16 [768], P(('tok', 'head')), may hold values from 0.099609375 to 1.8984375
- mask_gain: float32 [150], replicated, may hold values from 0.1 to 1.9
- d_masks: float32 [8192, 150], P(('tok', 'head')), may hold values from -6 to 6
Outputs:
- masks: float32 [8192, 150], P(('tok', 'head'))
- grad_patches: float32 [8192, 768], P(('tok', 'head'))
- grad_classes: float32 [2400, 768], P(('tok', 'head'))
- grad_qkv: float32 [768, 2304], P(('tok', 'head'))
- grad_out: float32 [768, 768], P(('tok', 'head'))
- grad_up: float32 [768, 3072], P(('tok', 'head'))
- grad_down: float32 [3072, 768], P(('tok', 'head'))
- grad_patch_proj: float32 [768, 768], P(('tok', 'head'))
- grad_class_proj: float32 [768, 768], P(('tok', 'head'))
- grad_norm1: float32 [768], P(('tok', 'head'))
- grad_norm2: float32 [768], P(('tok', 'head'))
- grad_mask_gain: float32 [150], replicated
The draws below stay inside these ranges and needn't reach their ends.
Inputs may be any that keep to these rules, and one draw needn't show every extreme that they name: `slot_lengths`: each slot holds two images, one of 64 to 255 patches and one of more than 768 patches, in either order, together at most 1024; in some slot they fill it exactly.
All inputs are finite; a program needn't handle non-finite values.
Results may differ from the reference program's by a relative error of at most 0.022.
Values may be sent and summed in bfloat16 or wider, within the bound.
A program may use at most 128 MiB of HBM per device.

```python
import jax
import jax.numpy as jnp
from jax import lax

D = 768
HEADS = 12
FF = 3072
NCLS = 150
TOK_DEV = 256
HEAD_DIM = 64
SLOT = 1024
SLOTS = 8
TOKENS = 8192
CLASS_ROWS = 2400


def draw_slot_lengths(key, part):
    key = jax.random.fold_in(key, 11)
    key_short, key_long, key_order, key_full = jax.random.split(key, 4)
    short_len = jax.random.randint(key_short, (SLOTS,), TOK_DEV // 4, TOK_DEV)
    full_slot = jax.random.randint(key_full, (), 0, SLOTS)
    picked = jnp.arange(SLOTS) == full_slot
    short_len = jnp.where(picked, TOK_DEV // 4, short_len)
    long_len = jax.random.randint(key_long, (SLOTS,), SLOT - TOK_DEV + 1, SLOT - short_len + 1)
    long_len = jnp.where(picked, SLOT - short_len, long_len)
    order = jax.random.randint(key_order, (SLOTS,), 0, 2)
    lead_len = jnp.where(order == 0, long_len, short_len)
    tail_len = jnp.where(order == 0, short_len, long_len)
    return jnp.stack([lead_len, tail_len], axis=1).astype(jnp.int32)


def block_scale(stream_key, shape, cuts, smallest, top_value):
    level = 1.0
    for dim, blocks in cuts:
        draws = jax.random.uniform(jax.random.fold_in(jax.random.fold_in(stream_key, 6), dim), (blocks,), jnp.float32, smallest / len(cuts), top_value / len(cuts))
        level = level * jnp.repeat(jnp.exp(draws), shape[dim] // blocks).reshape((-1,) + (1,) * (len(shape) - 1 - dim))
    return level


def noise(stream_key, shape, scale, most, pieces=(), held_as=jnp.bfloat16):
    values = scale * jax.random.normal(stream_key, shape, jnp.float32)
    if pieces:
        values = values * block_scale(stream_key, shape, pieces, -0.22, 0.18)
    return jnp.clip(values, -most, most).astype(held_as)


def setup_inputs(seed: int = 0) -> dict:
    key_of = jax.random.split(jax.random.key(seed), 14)
    patches = noise(key_of[0], (TOKENS, D), 1.0, 6.0, ((0, 32),))
    classes = noise(key_of[1], (CLASS_ROWS, D), 1.0, 6.0, ((0, 32),))
    slot_lengths = draw_slot_lengths(jax.random.fold_in(key_of[13], 71), 0)
    w_qkv = noise(key_of[3], (D, 3 * D), D ** -0.5, 0.21875, ((0, 32),))
    w_out = noise(key_of[4], (D, D), 2 ** -0.5, 4.0, ((0, 32),))
    w_up = noise(key_of[5], (D, FF), D ** -0.5, 0.21875, ((0, 32),))
    w_down = noise(key_of[6], (FF, D), FF ** -0.5, 0.109375, ((0, 32),))
    w_patch = noise(key_of[7], (D, D), D ** -0.5, 0.21875, ((0, 32),))
    w_class = noise(key_of[8], (D, D), D ** -0.5, 0.21875, ((0, 32),))
    norm1 = jnp.clip(1.0 + 0.18 * jax.random.normal(key_of[9], (D,), jnp.float32), 0.099609375, 1.8984375).astype(jnp.bfloat16)
    norm2 = jnp.clip(1.0 + 0.18 * jax.random.normal(key_of[10], (D,), jnp.float32), 0.099609375, 1.8984375).astype(jnp.bfloat16)
    mask_gain = jnp.clip(1.0 + 0.18 * jax.random.normal(key_of[11], (NCLS,), jnp.float32), 0.1, 1.9)
    d_masks = noise(key_of[12], (TOKENS, NCLS), 1.0, 6.0, ((0, 32),), jnp.float32)
    return dict(patches=patches, classes=classes, slot_lengths=slot_lengths, w_qkv=w_qkv, w_out=w_out, w_up=w_up, w_down=w_down, w_patch=w_patch, w_class=w_class, norm1=norm1, norm2=norm2, mask_gain=mask_gain, d_masks=d_masks)


@jax.custom_vjp
def low(v):
    return lax.optimization_barrier(v.astype(jnp.bfloat16)).astype(jnp.float32)

@jax.custom_vjp
def low_back(v):
    return v

def low_keep(v):
    return (low(v), None)

def low_pass(kept, grad):
    return (grad,)

def back_keep(v):
    return (v, None)

def back_low(kept, grad):
    return (low(grad),)
low.defvjp(low_keep, low_pass)
low_back.defvjp(back_keep, back_low)
HIGH = lax.Precision.HIGHEST

def matmul(left, right):
    return jnp.dot(left, right, precision=HIGH)

def layer_norm(values, gain):
    centre = values - lax.optimization_barrier(jnp.mean(values, axis=-1, keepdims=True))
    spread = lax.optimization_barrier(jnp.mean(centre * centre, axis=-1, keepdims=True))
    return centre * lax.rsqrt(spread + 1e-05) * gain

def unit_rows(values):
    return values * lax.rsqrt(lax.optimization_barrier(jnp.sum(values * values, axis=-1, keepdims=True)) + 1e-06)

def slot_masks(params, patch_rows, class_rows, lengths):
    w_q, w_o, w_u, w_d, w_p, w_c, gain_one, gain_two, gain_mask = params
    place = jnp.arange(SLOT).astype(jnp.int32)
    patch_seg = jnp.where(place < lengths[0], 0, jnp.where(place < lengths[0] + lengths[1], 1, -1)).astype(jnp.int32)
    class_seg = (jnp.arange(2 * NCLS) // NCLS).astype(jnp.int32)
    segment = jnp.concatenate([patch_seg, class_seg])
    allowed = (segment[:, None] == segment[None, :]) & (segment[None, :] >= 0)
    stacked = jnp.concatenate([patch_rows, class_rows], axis=0)
    total_rows = stacked.shape[0]
    first_in = low(layer_norm(stacked, gain_one))
    qkv = low(low_back(matmul(first_in, w_q))).reshape(total_rows, 3, HEADS, HEAD_DIM)
    queries = jnp.transpose(qkv[:, 0], (1, 0, 2))
    key_rows = jnp.transpose(qkv[:, 1], (1, 0, 2))
    value_rows = jnp.transpose(qkv[:, 2], (1, 0, 2))

    def one_head(parts):
        query, key_part, value_part = parts
        scores = low_back(matmul(query, key_part.T) * 0.125)
        scores = jnp.where(allowed, scores, -1e+30)
        top_score = lax.optimization_barrier(jnp.max(scores, axis=1, keepdims=True))
        expo = jnp.exp(scores - top_score)
        probs = expo / lax.optimization_barrier(jnp.sum(expo, axis=1, keepdims=True))
        return low(low_back(matmul(low(probs), value_part)))
    attended = lax.map(jax.checkpoint(one_head), (queries, key_rows, value_rows))
    attended = jnp.transpose(attended, (1, 0, 2)).reshape(total_rows, D)
    hidden = stacked + low_back(matmul(attended, w_o))
    second_in = low(layer_norm(hidden, gain_two))
    up_rows = low_back(matmul(second_in, w_u))
    gelu_rows = low(jax.nn.gelu(up_rows, approximate=False))
    after = low(hidden + low_back(matmul(gelu_rows, w_d)))
    patch_proj = low_back(matmul(after[:SLOT], w_p))
    class_proj = low_back(matmul(after[SLOT:], w_c))
    patch_unit = low(unit_rows(patch_proj))
    class_unit = low(unit_rows(class_proj))
    raw_both = low_back(matmul(patch_unit, class_unit.T))
    raw = jnp.where(patch_seg[:, None] == 0, raw_both[:, :NCLS], raw_both[:, NCLS:])
    valid = (patch_seg >= 0).astype(jnp.float32)[:, None]
    return layer_norm(raw, gain_mask) * valid

def reference(patches, classes, slot_lengths, w_qkv, w_out, w_up, w_down, w_patch, w_class, norm1, norm2, mask_gain, d_masks):
    params = tuple((item.astype(jnp.float32) for item in (w_qkv, w_out, w_up, w_down, w_patch, w_class, norm1, norm2, mask_gain)))
    patch_in = patches.astype(jnp.float32).reshape(SLOTS, SLOT, D)
    class_in = classes.astype(jnp.float32).reshape(SLOTS, 2 * NCLS, D)
    one_slot = jax.checkpoint(slot_masks)

    def forward(w_q, w_o, w_u, w_d, w_p, w_c, gain_one, gain_two, gain_mask, patch_all, class_all):
        weights = (w_q, w_o, w_u, w_d, w_p, w_c, gain_one, gain_two, gain_mask)

        def step(carry, item):
            return (carry, one_slot(weights, item[0], item[1], item[2]))
        _, result = lax.scan(step, jnp.zeros((), jnp.float32), (patch_all, class_all, slot_lengths))
        return result.reshape(TOKENS, NCLS)
    masks, pull = jax.vjp(forward, *params, patch_in, class_in)
    grads = pull(d_masks.astype(jnp.float32))
    return (masks, grads[9].reshape(TOKENS, D), grads[10].reshape(CLASS_ROWS, D), grads[0], grads[1], grads[2], grads[3], grads[4], grads[5], grads[6], grads[7], grads[8])
```

```python
import jax
import jax.numpy as jnp
from jax import lax
from jax.experimental import pallas as pl
from jax.experimental.pallas import tpu as pltpu
from jax.sharding import PartitionSpec as P

HEADS = 12
NCLS = 150


def layer_norm(values, gain):
    centre = values - jnp.mean(values, axis=-1, keepdims=True)
    spread = jnp.mean(centre * centre, axis=-1, keepdims=True)
    return centre * lax.rsqrt(spread + 1e-05) * gain


def unit_rows(values):
    return values * lax.rsqrt(jnp.sum(values * values, axis=-1, keepdims=True) + 1e-06)


def exact_gelu(values):
    return jax.nn.gelu(values, approximate=False)


def dot_plain(left, right):
    return jnp.dot(left, right, preferred_element_type=jnp.float32)


def dot_left_t(left, right):
    return lax.dot_general(
        left, right, (((0,), (0,)), ((), ())), preferred_element_type=jnp.float32
    )


def dot_right_t(left, right):
    return lax.dot_general(
        left, right, (((1,), (1,)), ((), ())), preferred_element_type=jnp.float32
    )


def flat_rows(matrix):
    return matrix.reshape(-1, 128)


def per_device(
    patches,
    classes,
    slot_lengths,
    w_qkv,
    w_out,
    w_up,
    w_down,
    w_patch,
    w_class,
    norm1,
    norm2,
    mask_gain,
    d_masks,
):
    tok_rows = patches.shape[0]
    cls_rows = classes.shape[0]
    all_rows = tok_rows + cls_rows
    width = patches.shape[1]
    groups = lax.axis_size("head")
    my_group = lax.axis_index("head")
    local_heads = HEADS // groups
    head_size = width // HEADS
    lead_len = slot_lengths[0, 0]
    tail_len = slot_lengths[0, 1]

    def segment_of(source, offset):
        place = source * tok_rows + offset
        patch_seg = jnp.where(place < lead_len, 0, jnp.where(place < lead_len + tail_len, 1, -1))
        class_seg = (source * cls_rows + offset - tok_rows) // NCLS
        return jnp.where(offset < tok_rows, patch_seg, class_seg)

    tok_seg = segment_of(my_group, jnp.arange(tok_rows))
    spread_rows = jnp.arange(groups * all_rows)
    head_seg = segment_of(spread_rows // all_rows, spread_rows % all_rows)
    allowed = (head_seg[:, None] == head_seg[None, :]) & (head_seg[None, :] >= 0)
    shards = (w_qkv, w_out, w_up, w_down, w_patch, w_class, norm1, norm2)
    gathered = (
        lax.all_gather(shards[0], ("tok", "head"), axis=0, tiled=True),
        lax.all_gather(shards[1], ("tok", "head"), axis=0, tiled=True),
        lax.all_gather(shards[2], ("tok", "head"), axis=0, tiled=True),
        lax.all_gather(shards[3], ("tok", "head"), axis=0, tiled=True),
        lax.all_gather(shards[4], ("tok", "head"), axis=0, tiled=True),
        lax.all_gather(shards[5], ("tok", "head"), axis=0, tiled=True),
        lax.all_gather(shards[6], ("tok", "head"), axis=0, tiled=True),
        lax.all_gather(shards[7], ("tok", "head"), axis=0, tiled=True),
    )
    full_qkv, full_out, full_up, full_down, full_patch, full_class, gain_one, gain_two = gathered
    stacked = jnp.concatenate([patches, classes], axis=0).astype(jnp.float32)
    first_in = layer_norm(stacked, gain_one.astype(jnp.float32)).astype(jnp.bfloat16)
    qkv_rows = (
        dot_plain(first_in, full_qkv)
        .astype(jnp.bfloat16)
        .reshape(all_rows, 3, groups, local_heads * head_size)
    )
    moved = lax.all_to_all(qkv_rows, "head", split_axis=2, concat_axis=0, tiled=True)
    moved = moved.reshape(groups * all_rows, 3, local_heads, head_size)
    queries = jnp.transpose(moved[:, 0], (1, 0, 2))
    key_rows = jnp.transpose(moved[:, 1], (1, 0, 2))
    value_rows = jnp.transpose(moved[:, 2], (1, 0, 2))

    def attend(parts):
        query, key_part, value_part = parts
        scores = jnp.where(allowed, dot_right_t(query, key_part) * 0.125, -1e30)
        top_score = jnp.max(scores, axis=1, keepdims=True)
        expo = jnp.exp(scores - top_score)
        total = jnp.sum(expo, axis=1, keepdims=True)
        probs = (expo / total).astype(jnp.bfloat16)
        result = dot_plain(probs, value_part).astype(jnp.bfloat16)
        return (result, top_score[:, 0] + jnp.log(total[:, 0]))

    head_out, log_total = lax.map(attend, (queries, key_rows, value_rows))
    sending = jnp.transpose(head_out, (1, 0, 2)).reshape(
        groups * all_rows, 1, local_heads * head_size
    )
    attended = lax.all_to_all(sending, "head", split_axis=0, concat_axis=1, tiled=True).reshape(
        all_rows, width
    )
    hidden = stacked + dot_plain(attended, full_out)
    second_in = layer_norm(hidden, gain_two.astype(jnp.float32)).astype(jnp.bfloat16)
    up_rows = dot_plain(second_in, full_up)
    gelu_rows = exact_gelu(up_rows).astype(jnp.bfloat16)
    after = (hidden + dot_plain(gelu_rows, full_down)).astype(jnp.bfloat16)
    patch_proj = dot_plain(after[:tok_rows], full_patch)
    class_proj = dot_plain(after[tok_rows:], full_class)
    patch_unit = unit_rows(patch_proj).astype(jnp.bfloat16)
    class_unit = unit_rows(class_proj).astype(jnp.bfloat16)
    slot_classes = lax.all_gather(class_unit, "head", axis=0, tiled=True)
    raw_both = dot_right_t(patch_unit, slot_classes)
    first_image = tok_seg[:, None] == 0
    raw = jnp.where(first_image, raw_both[:, :NCLS], raw_both[:, NCLS:])
    centre = raw - jnp.mean(raw, axis=1, keepdims=True)
    inv_sigma = lax.rsqrt(jnp.mean(centre * centre, axis=1, keepdims=True) + 1e-05)
    normed = centre * inv_sigma
    valid = (tok_seg >= 0).astype(jnp.float32)[:, None]
    masks = normed * mask_gain * valid
    regathered = (
        lax.all_gather(shards[0], ("tok", "head"), axis=0, tiled=True),
        lax.all_gather(shards[1], ("tok", "head"), axis=0, tiled=True),
        lax.all_gather(shards[2], ("tok", "head"), axis=0, tiled=True),
        lax.all_gather(shards[3], ("tok", "head"), axis=0, tiled=True),
        lax.all_gather(shards[4], ("tok", "head"), axis=0, tiled=True),
        lax.all_gather(shards[5], ("tok", "head"), axis=0, tiled=True),
        lax.all_gather(shards[6], ("tok", "head"), axis=0, tiled=True),
        lax.all_gather(shards[7], ("tok", "head"), axis=0, tiled=True),
    )
    back_qkv, back_out, back_up, back_down, back_patch, back_class, back_one, back_two = regathered
    mask_cot = d_masks * valid
    grad_mask = lax.psum(jnp.sum(mask_cot * normed, axis=0), ("tok", "head"))
    scaled = mask_cot * mask_gain
    d_raw = inv_sigma * (
        scaled
        - jnp.mean(scaled, axis=1, keepdims=True)
        - normed * jnp.mean(scaled * normed, axis=1, keepdims=True)
    )
    zero_part = jnp.zeros_like(d_raw)
    d_raw_both = jnp.concatenate(
        [jnp.where(first_image, d_raw, zero_part), jnp.where(first_image, zero_part, d_raw)], axis=1
    ).astype(jnp.bfloat16)
    d_patch_unit = dot_plain(d_raw_both, slot_classes)
    d_slot_classes = dot_left_t(d_raw_both, patch_unit)
    d_class_unit = lax.psum_scatter(
        d_slot_classes.astype(jnp.bfloat16), "head", scatter_dimension=0, tiled=True
    ).astype(jnp.float32)
    _, patch_pull = jax.vjp(unit_rows, patch_proj)
    d_patch_proj = patch_pull(d_patch_unit)[0].astype(jnp.bfloat16)
    _, class_pull = jax.vjp(unit_rows, class_proj)
    d_class_proj = class_pull(d_class_unit)[0].astype(jnp.bfloat16)
    grad_patch_w = dot_left_t(after[:tok_rows], d_patch_proj)
    grad_class_w = dot_left_t(after[tok_rows:], d_class_proj)
    d_after = jnp.concatenate(
        [dot_right_t(d_patch_proj, back_patch), dot_right_t(d_class_proj, back_class)], axis=0
    )
    d_after_low = d_after.astype(jnp.bfloat16)
    grad_down_w = dot_left_t(gelu_rows, d_after_low)
    d_gelu = dot_right_t(d_after_low, back_down)
    _, gelu_pull = jax.vjp(exact_gelu, up_rows)
    d_up_rows = gelu_pull(d_gelu)[0].astype(jnp.bfloat16)
    grad_up_w = dot_left_t(second_in, d_up_rows)
    d_second_in = dot_right_t(d_up_rows, back_up)
    _, norm_two_pull = jax.vjp(layer_norm, hidden, back_two.astype(jnp.float32))
    d_hidden_norm, grad_gain_two = norm_two_pull(d_second_in)
    d_hidden = d_after + d_hidden_norm
    d_hidden_low = d_hidden.astype(jnp.bfloat16)
    grad_out_w = dot_left_t(attended, d_hidden_low)
    d_attended = (
        dot_right_t(d_hidden_low, back_out)
        .astype(jnp.bfloat16)
        .reshape(all_rows, groups, local_heads * head_size)
    )
    d_head_out = lax.all_to_all(d_attended, "head", split_axis=1, concat_axis=0, tiled=True)
    d_head_out = jnp.transpose(
        d_head_out.reshape(groups * all_rows, local_heads, head_size), (1, 0, 2)
    )

    def attend_back(parts):
        query, key_part, value_part, log_row, d_result = parts
        scores = jnp.where(allowed, dot_right_t(query, key_part) * 0.125, -1e30)
        probs = jnp.exp(scores - log_row[:, None])
        d_probs = dot_right_t(d_result, value_part)
        inner = jnp.sum(probs * d_probs, axis=1, keepdims=True)
        d_scores = jnp.where(allowed, probs * (d_probs - inner), 0.0).astype(jnp.bfloat16)
        d_query = (dot_plain(d_scores, key_part) * 0.125).astype(jnp.bfloat16)
        d_key = (dot_left_t(d_scores, query) * 0.125).astype(jnp.bfloat16)
        d_value = dot_left_t(probs.astype(jnp.bfloat16), d_result).astype(jnp.bfloat16)
        return jnp.stack([d_query, d_key, d_value], axis=0)

    d_moved = lax.map(attend_back, (queries, key_rows, value_rows, log_total, d_head_out))
    d_moved = jnp.transpose(d_moved, (2, 1, 0, 3)).reshape(
        groups * all_rows, 3, 1, local_heads * head_size
    )
    d_qkv = lax.all_to_all(d_moved, "head", split_axis=0, concat_axis=2, tiled=True).reshape(
        all_rows, 3 * width
    )
    grad_qkv_w = dot_left_t(first_in, d_qkv)
    d_first_in = dot_right_t(d_qkv, back_qkv)
    _, norm_one_pull = jax.vjp(layer_norm, stacked, back_one.astype(jnp.float32))
    d_stacked_norm, grad_gain_one = norm_one_pull(d_first_in)
    d_stacked = d_hidden + d_stacked_norm
    every_sum = (
        lax.psum_scatter(flat_rows(grad_qkv_w), ("tok", "head"), scatter_dimension=0, tiled=True),
        lax.psum_scatter(flat_rows(grad_out_w), ("tok", "head"), scatter_dimension=0, tiled=True),
        lax.psum_scatter(flat_rows(grad_up_w), ("tok", "head"), scatter_dimension=0, tiled=True),
        lax.psum_scatter(flat_rows(grad_down_w), ("tok", "head"), scatter_dimension=0, tiled=True),
        lax.psum_scatter(flat_rows(grad_patch_w), ("tok", "head"), scatter_dimension=0, tiled=True),
        lax.psum_scatter(flat_rows(grad_class_w), ("tok", "head"), scatter_dimension=0, tiled=True),
        lax.psum_scatter(grad_gain_one, ("tok", "head"), scatter_dimension=0, tiled=True),
        lax.psum_scatter(grad_gain_two, ("tok", "head"), scatter_dimension=0, tiled=True),
    )
    sum_qkv, sum_out, sum_up, sum_down, sum_patch, sum_class, sum_one, sum_two = every_sum
    sum_qkv = sum_qkv.reshape(-1, 3 * width)
    sum_out = sum_out.reshape(-1, width)
    sum_up = sum_up.reshape(-1, grad_up_w.shape[1])
    sum_down = sum_down.reshape(-1, width)
    sum_patch = sum_patch.reshape(-1, width)
    sum_class = sum_class.reshape(-1, width)
    return (
        masks,
        d_stacked[:tok_rows],
        d_stacked[tok_rows:],
        sum_qkv,
        sum_out,
        sum_up,
        sum_down,
        sum_patch,
        sum_class,
        sum_one,
        sum_two,
        grad_mask,
    )


ROWS = 336
SLOT_ROWS = 4 * ROWS
PATCH = 256
CLS = 80
REAL = 75
PIECE = 80
LEAD = 16
MESH = pl.DeviceIdType.MESH
BF = jnp.bfloat16
F32 = jnp.float32


def position():
    tok = lax.axis_index("tok")
    return lax.div(tok, 4), lax.rem(lax.div(tok, 2), 2), lax.rem(tok, 2), lax.axis_index("head")


def device(y, x, c, z):
    return {"tok": y * 4 + x * 2 + c, "head": z}


def enter(y, x, c, z):
    barrier = pltpu.get_barrier_semaphore()
    others = [device(1 - y, x, c, z)]
    for turn in range(1, 16):
        flip_x, flip_c, step = turn // 8, (turn // 4) % 2, turn % 4
        others.append(
            device(
                y,
                1 - x if flip_x else x,
                1 - c if flip_c else c,
                lax.rem(z + step, 4),
            )
        )
    for other in others:
        pl.semaphore_signal(barrier, inc=1, device_id=other, device_id_type=MESH)
    pl.semaphore_wait(barrier, len(others))


class Net:
    def __init__(self, send_sem, recv_sem, here):
        self.send_sem, self.recv_sem, self.here = send_sem, recv_sem, here
        self.sends, self.recvs, self.open = 0, 0, []

    def land(self, count=1):
        first = self.recvs
        self.recvs += count
        return first

    def send(self, src, dst, to, slot, skip=None):
        index = self.sends
        self.sends += 1
        copy = pltpu.make_async_remote_copy(
            src_ref=src,
            dst_ref=dst,
            send_sem=self.send_sem.at[index],
            recv_sem=self.recv_sem.at[slot],
            device_id=to,
            device_id_type=MESH,
        )
        if skip is None:
            copy.start()
            self.open.append((copy, None))
        else:
            pl.when(jnp.logical_not(skip))(copy.start)
            self.open.append((copy, skip))

            @pl.when(skip)
            def _():
                pltpu.make_async_copy(src, dst, self.recv_sem.at[slot]).start()

    def local(self, src, dst, slot):
        pltpu.make_async_copy(src, dst, self.recv_sem.at[slot]).start()

    def wait(self, ref, slot):
        pltpu.make_async_copy(ref, ref, self.recv_sem.at[slot]).wait()

    def finish(self):
        for copy, skip in self.open:
            if skip is None:
                copy.wait_send()
            else:
                pl.when(jnp.logical_not(skip))(copy.wait_send)
        self.open = []


def rows_of(start, size):
    return pl.ds(pl.multiple_of(start, 16), size)


def lanes_of(start, size):
    return pl.ds(pl.multiple_of(start, 128), size)


def gather_kernel(
    xin, dmx, aux, wqa, wra, wd, xs, dmh, auxh, wq, wr, wdn, stq, str_, bq, br, send_sem, recv_sem
):
    y, x, c, z = position()
    tok = y * 4 + x * 2 + c
    quarter = 2 * x + c
    enter(y, x, c, z)
    net = Net(send_sem, recv_sem, None)
    sib, xdev, ydev = device(y, x, 1 - c, z), device(y, 1 - x, c, z), device(1 - y, x, c, z)
    half = wra.shape[1] // 2
    h1, h2 = pl.ds(0, half), pl.ds(half, half)
    d1, d2 = pl.ds(0, 384), pl.ds(384, 384)

    home = 2 * c + x
    got_lead, got_piece, got_dm, got_aux = net.land(4), net.land(4), net.land(), net.land()
    for q in range(4):
        to = device(y, q // 2, q % 2, home)
        mine = (z == home) & (quarter == q)
        off = LEAD + PIECE * q
        net.send(
            xin.at[pl.ds(off, PIECE)],
            xs.at[rows_of(z * ROWS + off, PIECE)],
            to,
            got_piece + z,
            mine,
        )
        net.send(
            xin.at[pl.ds(0, LEAD)], xs.at[rows_of(z * ROWS, LEAD)], to, got_lead + z, mine
        )
    to = device(y, lax.div(z, 2), lax.rem(z, 2), home)
    mine = (z == home) & (quarter == z)
    net.send(aux, auxh, to, got_aux, mine)

    got_q, got_r, got_d = net.land(4), net.land(4), net.land(4)
    net.local(wqa, stq.at[z], got_q + z)
    net.local(wra, str_.at[z], got_r + z)
    own_d = wdn.at[rows_of((tok * 4 + z) * 96, 96)]
    net.local(wd, own_d, got_d + z)
    peers = [device(y, x, c, lax.rem(z + step, 4)) for step in (1, 3, 2)]
    for peer in peers:
        net.send(wqa, stq.at[z], peer, got_q + z)
    for peer in peers:
        net.send(wra, str_.at[z], peer, got_r + z)
    for peer in peers:
        net.send(wd, own_d, peer, got_d + z)
    net.send(dmx, dmh, to, got_dm, mine)

    def piece(source, owner):
        return xs.at[rows_of(source * ROWS + LEAD + PIECE * owner, PIECE)]

    fwd_s, fwd_x, fwd_xs = net.land(4), net.land(4), net.land(4)
    for src in range(4):
        net.wait(piece(src, quarter), got_piece + src)
        net.send(piece(src, quarter), piece(src, quarter), xdev, fwd_x + src)
        net.send(piece(src, quarter), piece(src, quarter), sib, fwd_s + src)

    def blk(t):
        return rows_of(t * 96, 96)

    def big(t):
        return rows_of(t * 384, 384)

    for src in range(4):
        net.wait(stq.at[src], got_q + src)

    def join(stage, block, width):
        def body(i, carry):
            cols = lanes_of(i * width, width)
            parts = [stage[src, :, cols].astype(F32) for src in range(4)]
            block[:, cols] = jnp.concatenate(parts, axis=0).astype(BF)
            return carry

        lax.fori_loop(0, block.shape[1] // width, body, 0)

    join(stq, bq, 384)
    t_x, t_y = tok + 2 - 4 * x, tok + 4 - 8 * y
    t_xy = t_x + 4 - 8 * y
    own_half, other_half = lanes_of(1152 * x, 1152), lanes_of(1152 * (1 - x), 1152)
    q_own, q_x, q_y, q_xy, q_s = net.land(), net.land(), net.land(), net.land(), net.land(4)
    net.send(bq.at[:, other_half], wq.at[blk(tok)], xdev, q_x)
    net.send(bq.at[:, own_half], wq.at[blk(tok)], ydev, q_y)
    net.local(bq.at[:, own_half], wq.at[blk(tok)], q_own)
    net.send(bq.at[:, own_half], wq.at[blk(tok)], sib, q_s)

    other = quarter + 2 - 4 * x
    for src in range(4):
        net.wait(piece(src, other), fwd_x + src)
        net.send(piece(src, other), piece(src, other), sib, fwd_xs + src)
    net.wait(wq.at[blk(t_x)], q_x)
    net.send(wq.at[blk(t_x)], wq.at[blk(t_x)], ydev, q_xy)
    net.send(wq.at[blk(t_x)], wq.at[blk(t_x)], sib, q_s + 1)

    for src in range(4):
        net.wait(str_.at[src], got_r + src)
    join(str_, br, 384)
    r_own = net.land(2)
    r_x, r_y, r_s = net.land(4), net.land(4), net.land(8)
    e_x, e_y, e_s = net.land(4), net.land(4), net.land(8)
    net.send(br.at[:, h1], wr.at[blk(tok), h1], xdev, r_x)
    net.send(br.at[:, h2], wr.at[blk(tok), h2], ydev, r_y)
    for src in range(4):
        net.wait(wdn.at[rows_of((tok * 4 + src) * 96, 96)], got_d + src)
    net.send(wdn.at[big(tok), d1], wdn.at[big(tok), d1], xdev, e_x)
    net.send(wdn.at[big(tok), d2], wdn.at[big(tok), d2], ydev, e_y)
    net.send(br.at[:, h1], wr.at[blk(tok), h1], ydev, r_y + 1)
    net.send(br.at[:, h2], wr.at[blk(tok), h2], xdev, r_x + 1)
    net.send(wdn.at[big(tok), d1], wdn.at[big(tok), d1], ydev, e_y + 1)
    net.send(wdn.at[big(tok), d2], wdn.at[big(tok), d2], xdev, e_x + 1)
    net.local(br.at[:, h1], wr.at[blk(tok), h1], r_own)
    net.local(br.at[:, h2], wr.at[blk(tok), h2], r_own + 1)
    net.send(br.at[:, h1], wr.at[blk(tok), h1], sib, r_s)
    net.send(br.at[:, h2], wr.at[blk(tok), h2], sib, r_s + 1)
    net.send(wdn.at[big(tok), d1], wdn.at[big(tok), d1], sib, e_s)
    net.send(wdn.at[big(tok), d2], wdn.at[big(tok), d2], sib, e_s + 1)

    net.wait(wq.at[blk(t_y)], q_y)
    net.send(wq.at[blk(t_y)], wq.at[blk(t_y)], sib, q_s + 2)
    net.wait(wq.at[blk(t_xy)], q_xy)
    net.send(wq.at[blk(t_xy)], wq.at[blk(t_xy)], sib, q_s + 3)

    def passed(ref, rows, cols, slot, onward):
        net.wait(ref.at[rows, cols], slot)
        for to_dev, index in onward:
            net.send(ref.at[rows, cols], ref.at[rows, cols], to_dev, index)

    passed(wr, blk(t_x), h1, r_x, [(ydev, r_y + 2), (sib, r_s + 2)])
    passed(wr, blk(t_y), h2, r_y, [(xdev, r_x + 2), (sib, r_s + 3)])
    passed(wdn, big(t_x), d1, e_x, [(ydev, e_y + 2), (sib, e_s + 2)])
    passed(wdn, big(t_y), d2, e_y, [(xdev, e_x + 2), (sib, e_s + 3)])
    passed(wr, blk(t_y), h1, r_y + 1, [(sib, r_s + 4)])
    passed(wr, blk(t_x), h2, r_x + 1, [(sib, r_s + 5)])
    passed(wdn, big(t_y), d1, e_y + 1, [(sib, e_s + 4)])
    passed(wdn, big(t_x), d2, e_x + 1, [(sib, e_s + 5)])
    passed(wr, blk(t_xy), h1, r_y + 2, [(sib, r_s + 6)])
    passed(wr, blk(t_xy), h2, r_x + 2, [(sib, r_s + 7)])
    passed(wdn, big(t_xy), d1, e_y + 2, [(sib, e_s + 6)])
    passed(wdn, big(t_xy), d2, e_x + 2, [(sib, e_s + 7)])

    flip = 1 - 2 * c
    for i, t in enumerate((tok, t_x, t_y, t_xy)):
        net.wait(wq.at[blk(t + flip)], q_s + i)
    order = ((tok, 0), (tok, 1), (t_x, 0), (t_y, 1), (t_y, 0), (t_x, 1), (t_xy, 0), (t_xy, 1))
    for i, (t, second) in enumerate(order):
        net.wait(wr.at[blk(t + flip), h2 if second else h1], r_s + i)
        net.wait(wdn.at[big(t + flip), d2 if second else d1], e_s + i)
    net.wait(wq.at[blk(tok)], q_own)
    net.wait(wr.at[blk(tok), h1], r_own)
    net.wait(wr.at[blk(tok), h2], r_own + 1)
    sibling = quarter + flip
    for src in range(4):
        net.wait(xs.at[rows_of(src * ROWS, LEAD)], got_lead + src)
        net.wait(piece(src, sibling), fwd_s + src)
        net.wait(piece(src, sibling + 2 - 4 * x), fwd_xs + src)
    net.wait(dmh, got_dm)
    net.wait(auxh, got_aux)
    net.finish()


def nn(left, right):
    return jnp.dot(left, right, preferred_element_type=F32)


def nt(left, right):
    return lax.dot_general(left, right, (((1,), (1,)), ((), ())), preferred_element_type=F32)


def tn(left, right):
    return lax.dot_general(left, right, (((0,), (0,)), ((), ())), preferred_element_type=F32)


def segments(row, lead_len, tail_len):
    source = (
        (row >= ROWS).astype(jnp.int32)
        + (row >= 2 * ROWS).astype(jnp.int32)
        + (row >= 3 * ROWS).astype(jnp.int32)
    )
    offset = row - source * ROWS
    patch = source * PATCH + offset
    patch_seg = jnp.where(patch < lead_len, 0, jnp.where(patch < lead_len + tail_len, 1, -1))
    number = offset - PATCH
    class_seg = jnp.where(source >= 2, 1, 0)
    filler = number >= REAL
    seg = jnp.where(offset < PATCH, patch_seg, jnp.where(filler, -1, class_seg))
    return seg, filler


def normalise(values):
    centre = values - jnp.mean(values, axis=-1, keepdims=True)
    scale = lax.rsqrt(jnp.mean(centre * centre, axis=-1, keepdims=True) + 1e-05)
    return centre * scale, scale


def own_lanes(c, head, shape):
    lane = lax.broadcasted_iota(jnp.int32, shape, len(shape) - 1)
    group = lane // 64 - c
    if head is None:
        return (group >= 0) & (group < 3)
    return group == head


BLOCK = 192


def forward_kernel(xs, wq, aux, wp, zn, qr, kr, vr, out, stats, kh, vh):
    c = lax.rem(lax.axis_index("tok"), 2)
    lead_len, tail_len = aux[0:1, 0:1], aux[1:2, 0:1]
    keep = own_lanes(c, None, (768, 256))
    for part in range(3):
        cols = lanes_of(384 * part + 128 * c, 256)
        wp[:, 256 * part : 256 * part + 256] = jnp.where(keep, wq[:, cols], 0.0).astype(BF)

    def project(i, carry):
        rows = rows_of(i * ROWS, ROWS)
        normed = normalise(xs[rows, :].astype(F32))[0].astype(BF)
        zn[rows, :] = normed
        qr[rows, :] = (nn(normed, wp[:, 0:256]).astype(BF) * 0.125).astype(BF)
        kr[rows, :] = nn(normed, wp[:, 256:512]).astype(BF)
        vr[rows, :] = nn(normed, wp[:, 512:768]).astype(BF)
        return carry

    lax.fori_loop(0, 4, project, 0)
    for head in range(3):
        mine = own_lanes(c, head, (SLOT_ROWS, 256))
        kh[head] = jnp.where(mine, kr[...], 0.0).astype(BF)
        vh[head] = jnp.where(mine, vr[...], 0.0).astype(BF)
    key_row = lax.broadcasted_iota(jnp.int32, (1, SLOT_ROWS), 1)
    key_seg, key_filler = segments(key_row, lead_len, tail_len)
    key_seg = jnp.where(key_seg < 0, -5, key_seg)
    masked = jnp.where(key_filler, -3e38, -1e30)

    def attend(i, carry):
        rows = rows_of(i * BLOCK, BLOCK)
        row = lax.broadcasted_iota(jnp.int32, (BLOCK, 1), 0) + i * BLOCK
        seg = segments(row, lead_len, tail_len)[0]
        query = qr[rows, :]
        lane = lax.broadcasted_iota(jnp.int32, (BLOCK, 128), 1)
        total_out = jnp.zeros((BLOCK, 256), F32)
        kept = jnp.zeros((BLOCK, 128), F32)
        for head in range(3):
            scores = jnp.where(seg == key_seg, nt(query, kh[head]), masked)
            top = jnp.max(scores, axis=1, keepdims=True)
            expo = jnp.exp(scores - top)
            total = jnp.sum(expo, axis=1, keepdims=True)
            probs = (expo * (1.0 / total)).astype(BF)
            total_out = total_out + nn(probs, vh[head])
            kept = jnp.where(lane == head, top + jnp.log(total), kept)
        out[rows, :] = total_out.astype(BF)
        stats[rows, :] = kept
        return carry

    lax.fori_loop(0, SLOT_ROWS // BLOCK, attend, 0)


def backward_kernel(
    zn, qr, kr, vr, out, stats, d_out, wp, aux, gq, d_first, stat_t, delta, dq, dqkv, znt
):
    c = lax.rem(lax.axis_index("tok"), 2)
    lead_len, tail_len = aux[0:1, 0:1], aux[1:2, 0:1]
    stat_t[...] = stats[...].T
    head_of = own_lanes(c, None, (8, 256))
    lane = lax.broadcasted_iota(jnp.int32, (8, 256), 1)
    row8 = lax.broadcasted_iota(jnp.int32, (8, 256), 0)
    picker = jnp.where(head_of & (lane // 64 - c == row8), 1.0, 0.0)
    product = d_out[...].astype(F32) * out[...].astype(F32)
    delta[...] = lax.dot_general(
        picker,
        product,
        (((1,), (1,)), ((), ())),
        precision=lax.Precision.HIGHEST,
        preferred_element_type=F32,
    )
    dq[...] = jnp.zeros_like(dq)
    query_row = lax.broadcasted_iota(jnp.int32, (1, SLOT_ROWS), 1)
    query_seg = segments(query_row, lead_len, tail_len)[0]

    def step(j, carry):
        rows = rows_of(j * BLOCK, BLOCK)
        row = lax.broadcasted_iota(jnp.int32, (BLOCK, 1), 0) + j * BLOCK
        seg, filler = segments(row, lead_len, tail_len)
        seg = jnp.where(seg < 0, -5, seg)
        masked = jnp.where(filler, -3e38, -1e30)
        keys, values = kr[rows, :], vr[rows, :]
        queries, d_results = qr[...], d_out[...]
        allowed = seg == query_seg
        d_key = jnp.zeros((BLOCK, 256), F32)
        d_value = jnp.zeros((BLOCK, 256), F32)
        for head in range(3):
            mine = own_lanes(c, head, (BLOCK, 256))
            key = jnp.where(mine, keys, 0.0).astype(BF)
            value = jnp.where(mine, values, 0.0).astype(BF)
            scores = jnp.where(allowed, nt(key, queries), masked)
            probs = jnp.exp(scores - stat_t[head : head + 1, :])
            d_probs = nt(value, d_results)
            d_scores = jnp.where(
                allowed, probs * (d_probs - delta[head : head + 1, :]), 0.0
            ).astype(BF)
            d_value = jnp.where(mine, nn(probs.astype(BF), d_results), d_value)
            d_key = jnp.where(mine, nn(d_scores, queries), d_key)
            dq[...] += tn(d_scores, key)
        dqkv[rows, 256:512] = d_key.astype(BF)
        dqkv[rows, 512:768] = d_value.astype(BF)
        return carry

    lax.fori_loop(0, SLOT_ROWS // BLOCK, step, 0)
    dqkv[:, 0:256] = (dq[...] * 0.125).astype(BF)
    znt[...] = zn[...].T

    def first(i, carry):
        rows = rows_of(i * ROWS, ROWS)
        d_first[rows, :] = nt(dqkv[rows, :], wp[...]).astype(BF)
        return carry

    lax.fori_loop(0, 4, first, 0)

    def weight(i, carry):
        rows = rows_of(i * 256, 256)
        gq[rows, :] = nn(znt[rows, :], dqkv[...]).astype(BF)
        return carry

    lax.fori_loop(0, 3, weight, 0)


def group_of(y, x, c, z):
    quarter = 2 * x + c
    return [
        (device(y, x, 1 - c, z), quarter + 1 - 2 * c),
        (device(y, 1 - x, c, z), quarter + 2 - 4 * x),
        (device(y, 1 - x, 1 - c, z), quarter + 3 - 4 * x - 2 * c),
    ]


TILE = 256


def middle_kernel(
    xs, o_mine, wr, wdn, dmh, aux, gain,
    gr, gd, dh, d_out, masks, gain_part,
    wr_v, wd_v, xb, obuf, att, znt, zn2, gl, slope, du, h_f, dz_f, dzb, pp_f, cn, dcn, dcbuf, dob,
    inv, send_sem, recv_sem,
):
    y, x, c, z = position()
    quarter = 2 * x + c
    enter(y, x, c, z)
    net = Net(send_sem, recv_sem, None)
    group = group_of(y, x, c, z)
    got_x, got_wr, got_wd = net.land(), net.land(), net.land()
    got_o, got_cn, got_dc, got_do = net.land(4), net.land(4), net.land(4), net.land(4)
    own_rows = rows_of(quarter * ROWS, ROWS)
    for to, q in group:
        net.send(o_mine.at[rows_of(q * ROWS, ROWS)], obuf.at[quarter], to, got_o + quarter)
    net.local(o_mine.at[own_rows], obuf.at[quarter], got_o + quarter)
    net.local(xs.at[own_rows], xb, got_x)
    net.local(wr, wr_v, got_wr)
    net.local(wdn, wd_v, got_wd)
    lead_len, tail_len = aux[0:1, 0:1], aux[1:2, 0:1]
    row = lax.broadcasted_iota(jnp.int32, (PATCH, 1), 0) + quarter * ROWS
    seg = segments(row, lead_len, tail_len)[0]
    first_image = seg == 0
    valid = jnp.where(seg >= 0, 1.0, 0.0)
    up, down = 3072, wd_v
    w_out, w_patch, w_class = up, up + 768, up + 1536

    net.wait(xb, got_x)
    for q in range(4):
        net.wait(obuf.at[q], got_o + q)
    for side in range(2):
        a, b = obuf[2 * side], obuf[2 * side + 1]
        base = 384 * side
        att[:, base : base + 128] = a[:, 0:128]
        att[:, base + 128 : base + 256] = a[:, 128:256] + b[:, 0:128]
        att[:, base + 256 : base + 384] = b[:, 128:256]
    net.wait(wr_v, got_wr)
    h_f[...] = xb[...].astype(F32) + nn(att[...], wr_v[:, w_out : w_out + 768])
    normed, scale = normalise(h_f[...])
    inv[...] = jnp.broadcast_to(scale, inv.shape)
    zn2[...] = normed.astype(BF)
    znt[...] = normed.T.astype(BF)

    def up_step(i, carry):
        cols = lanes_of(i * TILE, TILE)
        u = nn(zn2[...], wr_v[:, cols])
        cdf = 0.5 * (1.0 + lax.erf(u * 0.7071067811865476))
        gl[:, cols] = (u * cdf).astype(BF)
        slope[:, cols] = cdf + u * (jnp.exp(-0.5 * u * u) * 0.3989422804014327)
        return carry

    lax.fori_loop(0, up // TILE, up_step, 0)
    net.wait(wd_v, got_wd)
    z2 = (h_f[...] + nn(gl[...], wd_v[...])).astype(BF)
    z2p, z2c = z2[0:PATCH], z2[PATCH:ROWS]

    def unit(values):
        return values * lax.rsqrt(jnp.sum(values * values, axis=-1, keepdims=True) + 1e-06)

    def unit_back(values, cot):
        r = lax.rsqrt(jnp.sum(values * values, axis=-1, keepdims=True) + 1e-06)
        return r * cot - values * (r * r * r * jnp.sum(values * cot, axis=-1, keepdims=True))

    cc = nn(z2c, wr_v[:, w_class : w_class + 768])
    own_cls = rows_of(quarter * CLS, CLS)
    cn[own_cls, :] = unit(cc).astype(BF)
    for to, q in group:
        net.send(cn.at[own_cls], cn.at[own_cls], to, got_cn + quarter)
    pp = nn(z2p, wr_v[:, w_patch : w_patch + 768])
    pp_f[...] = pp
    pn = unit(pp).astype(BF)
    for to, q in group:
        net.wait(cn.at[rows_of(q * CLS, CLS)], got_cn + q)
    low, high = cn[0 : 2 * CLS, :], cn[2 * CLS : 4 * CLS, :]
    wide = 2 * CLS
    lane = lax.broadcasted_iota(jnp.int32, (1, wide), 1)
    real = jnp.where(lane >= CLS, lane - CLS, lane) < REAL
    raw = jnp.where(first_image, nt(pn, low), nt(pn, high))

    def mean(values):
        return jnp.sum(jnp.where(real, values, 0.0), axis=1, keepdims=True) * (0.5 / REAL)

    centre = jnp.where(real, raw - mean(raw), 0.0)
    sigma = lax.rsqrt(mean(centre * centre) + 1e-05)
    xhat = centre * sigma
    mask_gain = gain[0:1, 0:wide]
    masks[:, wide:256] = jnp.zeros((PATCH, 256 - wide), BF)
    masks[:, 0:wide] = (xhat * mask_gain * valid).astype(BF)
    dm = dmh[:, 0:wide].astype(F32) * valid
    gain_part[...] = jnp.zeros_like(gain_part)
    gain_part[0:1, 0:wide] = jnp.sum(dm * xhat, axis=0, keepdims=True)
    dx = jnp.where(real, dm * mask_gain, 0.0)
    d_raw = jnp.where(real, sigma * (dx - mean(dx) - xhat * mean(dx * xhat)), 0.0)
    d_low = jnp.where(first_image, d_raw, 0.0).astype(BF)
    d_high = jnp.where(first_image, 0.0, d_raw).astype(BF)
    dcn[0:wide, :] = tn(d_low, pn).astype(BF)
    dcn[wide : 2 * wide, :] = tn(d_high, pn).astype(BF)
    for to, q in group:
        net.send(dcn.at[rows_of(q * CLS, CLS)], dcbuf.at[quarter], to, got_dc + quarter)
    net.local(dcn.at[own_cls], dcbuf.at[quarter], got_dc + quarter)
    d_pn = nn(d_low, low) + nn(d_high, high)
    d_pp = unit_back(pp_f[...], d_pn).astype(BF)
    gr[:, w_patch : w_patch + 768] = tn(z2p, d_pp).astype(BF)
    dz_f[0:PATCH, :] = nt(d_pp, wr_v[:, w_patch : w_patch + 768])
    for q in range(4):
        net.wait(dcbuf.at[q], got_dc + q)
    d_cn = dcbuf[0].astype(F32) + dcbuf[1].astype(F32) + dcbuf[2].astype(F32) + dcbuf[3].astype(F32)
    d_cc = unit_back(cc, d_cn).astype(BF)
    gr[:, w_class : w_class + 768] = tn(z2c, d_cc).astype(BF)
    dz_f[PATCH:ROWS, :] = nt(d_cc, wr_v[:, w_class : w_class + 768])
    dzb[...] = dz_f[...].astype(BF)

    def down_step(i, carry):
        cols = lanes_of(i * TILE, TILE)
        d_u = (nt(dzb[...], wd_v[cols, :]) * slope[:, cols]).astype(BF)
        du[:, cols] = d_u
        gd[cols, :] = tn(gl[:, cols], dzb[...]).astype(BF)
        gr[:, cols] = nn(znt[...], d_u).astype(BF)
        return carry

    lax.fori_loop(0, up // TILE, down_step, 0)
    d_zn = nt(du[...], wr_v[:, 0:up])
    normed = h_f[...]
    normed = (normed - jnp.mean(normed, axis=-1, keepdims=True)) * inv[:, 0:1]
    d_h = dz_f[...] + inv[:, 0:1] * (
        d_zn
        - jnp.mean(d_zn, axis=-1, keepdims=True)
        - normed * jnp.mean(d_zn * normed, axis=-1, keepdims=True)
    )
    dh[...] = d_h
    d_hb = d_h.astype(BF)
    dob[...] = nt(d_hb, wr_v[:, w_out : w_out + 768]).astype(BF)

    def piece(q):
        return dob.at[:, lanes_of(384 * lax.div(q, 2) + 128 * lax.rem(q, 2), 256)]

    for to, q in group:
        net.send(piece(q), d_out.at[own_rows], to, got_do + quarter)
    net.local(piece(quarter), d_out.at[own_rows], got_do + quarter)
    gr[:, w_out : w_out + 768] = tn(att[...], d_hb).astype(BF)
    for q in range(4):
        net.wait(d_out.at[rows_of(q * ROWS, ROWS)], got_do + q)
    net.finish()


def add_into(total, part, width):
    def body(i, carry):
        cols = lanes_of(i * width, width)
        total[:, cols] = (total[:, cols].astype(F32) + part[:, cols].astype(F32)).astype(BF)
        return carry

    lax.fori_loop(0, total.shape[1] // width, body, 0)


def split_rows(block, stage, width):
    def body(i, carry):
        cols = lanes_of(i * width, width)
        values = block[:, cols].astype(F32)
        for part in range(4):
            stage[part, :, cols] = values[24 * part : 24 * part + 24].astype(BF)
        return carry

    lax.fori_loop(0, block.shape[1] // width, body, 0)


def sum_parts(stage, total, width):
    def body(i, carry):
        cols = lanes_of(i * width, width)
        total[:, cols] = (
            stage[0, :, cols].astype(F32)
            + stage[1, :, cols].astype(F32)
            + stage[2, :, cols].astype(F32)
            + stage[3, :, cols].astype(F32)
        )
        return carry

    lax.fori_loop(0, total.shape[1] // width, body, 0)


def reduce_kernel(
    gr, gd, gq, d_first, dh, xs, masks, gain_part,
    d_rows, mask_rows, sum_q, sum_r, sum_d, gain_sum,
    xb, pr, pd, rr, rd, ry1, rx1, rx2, ry2, dy1, dx1, dx2, dy2, sp, rz, rzd,
    pq, rq, hq, ryq, rxq, fq, spq, rzq, fa, fb, fc, back, gz, gh,
    send_sem, recv_sem,
):
    y, x, c, z = position()
    quarter = 2 * x + c
    enter(y, x, c, z)
    net = Net(send_sem, recv_sem, None)
    sib, xdev, ydev = device(y, x, 1 - c, z), device(y, 1 - x, c, z), device(1 - y, x, c, z)
    peers = [(device(y, x, c, lax.rem(z + s, 4)), lax.rem(z + s, 4)) for s in (1, 3, 2)]
    half = gr.shape[1] // 2
    h1, h2 = pl.ds(0, half), pl.ds(half, half)
    d1, d2 = pl.ds(0, 384), pl.ds(384, 384)
    own_rows = rows_of(quarter * ROWS, ROWS)
    got_x, got_mask, got_back = net.land(), net.land(), net.land()
    net.local(xs.at[own_rows], xb, got_x)
    owner = device(y, lax.rem(z, 2), lax.div(z, 2), quarter)
    is_owner = (lax.rem(z, 2) == x) & (lax.div(z, 2) == c) & (quarter == z)
    net.send(masks, mask_rows, owner, got_mask, is_owner)

    def tok_of(b, core):
        return (b // 2) * 4 + (b % 2) * 2 + core

    def blk(t):
        return rows_of(t * 96, 96)

    def big(t):
        return rows_of(t * 384, 384)

    fa_in, fb_in, fc_in = net.land(2), net.land(2), net.land()
    flip = quarter + 1 - 2 * c
    cross = 2 - 4 * x
    for i, q in enumerate((flip + cross, flip)):
        net.send(d_first.at[rows_of(q * ROWS, ROWS)], fb.at[i], sib, fb_in + i)
    for i, q in enumerate((quarter + cross, quarter)):
        net.local(d_first.at[rows_of(q * ROWS, ROWS)], fa.at[i], fa_in + i)

    qa_in, qb_in = net.land(4), net.land(4)
    for b in range(4):
        net.send(gq.at[blk(tok_of(b, 1 - c))], rq.at[b], sib, qb_in + b)
        net.local(gq.at[blk(tok_of(b, c))], pq.at[b], qa_in + b)
    ra_in, rb_in, da_in, db_in = net.land(4), net.land(4), net.land(4), net.land(4)
    for b in range(4):
        net.send(gr.at[blk(tok_of(b, 1 - c))], rr.at[b], sib, rb_in + b)
        net.local(gr.at[blk(tok_of(b, c))], pr.at[b], ra_in + b)
        net.send(gd.at[big(tok_of(b, 1 - c))], rd.at[b], sib, db_in + b)
        net.local(gd.at[big(tok_of(b, c))], pd.at[b], da_in + b)

    gz_in = net.land(4)
    for peer, pz in peers:
        net.send(gain_part, gz.at[z], peer, gz_in + z)
    net.local(gain_part, gz.at[z], gz_in + z)

    for i in range(2):
        net.wait(fa.at[i], fa_in + i)
        net.wait(fb.at[i], fb_in + i)
        add_into(fa.at[i], fb.at[i], 256)
        if i == 0:
            net.send(fa.at[0], fc, xdev, fc_in)

    first_core = c == 0
    for b in range(4):
        net.wait(pq.at[b], qa_in + b)
        net.wait(rq.at[b], qb_in + b)
        for part in range(3):
            own = pq[b, :, 256 * part : 256 * part + 256].astype(F32)
            new = rq[b, :, 256 * part : 256 * part + 256].astype(F32)
            left, right = jnp.where(first_core, own, new), jnp.where(first_core, new, own)
            base = 384 * part
            hq[b, :, base : base + 128] = left[:, 0:128].astype(BF)
            hq[b, :, base + 128 : base + 256] = (left[:, 128:256] + right[:, 0:128]).astype(BF)
            hq[b, :, base + 256 : base + 384] = right[:, 128:256].astype(BF)
    qy_in, qx_in = net.land(2), net.land()
    for side in range(2):
        net.send(hq.at[2 * (1 - y) + side], ryq.at[side], ydev, qy_in + side)

    for b in range(4):
        net.wait(pr.at[b], ra_in + b)
        net.wait(rr.at[b], rb_in + b)
        add_into(pr.at[b], rr.at[b], 384)
        net.wait(pd.at[b], da_in + b)
        net.wait(rd.at[b], db_in + b)
        add_into(pd.at[b], rd.at[b], 128)
    y_in, x_in, x2_in, y2_in = net.land(2), net.land(), net.land(2), net.land()
    v_in, u_in, u2_in, v2_in = net.land(2), net.land(), net.land(2), net.land()
    for side in range(2):
        net.send(pr.at[2 * (1 - y) + side, :, h1], ry1.at[side], ydev, y_in + side)
        net.send(pr.at[2 * side + 1 - x, :, h2], rx2.at[side], xdev, x2_in + side)
    for side in range(2):
        net.send(pd.at[2 * (1 - y) + side, :, d1], dy1.at[side], ydev, v_in + side)
        net.send(pd.at[2 * side + 1 - x, :, d2], dx2.at[side], xdev, u2_in + side)

    for side in range(2):
        net.wait(ryq.at[side], qy_in + side)
        add_into(hq.at[2 * y + side], ryq.at[side], 384)
    net.send(hq.at[2 * y + 1 - x], rxq, xdev, qx_in)

    for side in range(2):
        net.wait(ry1.at[side], y_in + side)
        add_into(pr.at[2 * y + side, :, h1], ry1.at[side], 384)
        net.wait(rx2.at[side], x2_in + side)
        add_into(pr.at[2 * side + x, :, h2], rx2.at[side], 384)
    net.send(pr.at[2 * y + 1 - x, :, h1], rx1, xdev, x_in)
    net.send(pr.at[2 * (1 - y) + x, :, h2], ry2, ydev, y2_in)
    for side in range(2):
        net.wait(dy1.at[side], v_in + side)
        add_into(pd.at[2 * y + side, :, d1], dy1.at[side], 128)
        net.wait(dx2.at[side], u2_in + side)
        add_into(pd.at[2 * side + x, :, d2], dx2.at[side], 128)
    net.send(pd.at[2 * y + 1 - x, :, d1], dx1, xdev, u_in)
    net.send(pd.at[2 * (1 - y) + x, :, d2], dy2, ydev, v2_in)

    net.wait(xb, got_x)
    net.wait(fc, fc_in)
    d_zn = fa[1].astype(F32) + fc[...].astype(F32)
    normed, scale = normalise(xb[...].astype(F32))
    d_x = dh[...] + scale * (
        d_zn
        - jnp.mean(d_zn, axis=-1, keepdims=True)
        - normed * jnp.mean(d_zn * normed, axis=-1, keepdims=True)
    )
    back[...] = d_x.astype(BF)
    net.send(back, d_rows, owner, got_back, is_owner)

    net.wait(rxq, qx_in)
    fq[:, lanes_of(1152 * x, 1152)] = hq[2 * y + x]
    fq[:, lanes_of(1152 * (1 - x), 1152)] = rxq[...]
    split_rows(fq, spq, 384)
    zq_in = net.land(4)
    for peer, pz in peers:
        net.send(spq.at[pz], rzq.at[z], peer, zq_in + z)
    net.local(spq.at[z], rzq.at[z], zq_in + z)

    net.wait(rx1, x_in)
    add_into(pr.at[2 * y + x, :, h1], rx1, 384)
    net.wait(ry2, y2_in)
    add_into(pr.at[2 * y + x, :, h2], ry2, 384)
    split_rows(pr.at[2 * y + x], sp, 384)
    zr_in, zd_in = net.land(4), net.land(4)
    for peer, pz in peers:
        net.send(sp.at[pz], rz.at[z], peer, zr_in + z)
    net.local(sp.at[z], rz.at[z], zr_in + z)
    net.wait(dx1, u_in)
    add_into(pd.at[2 * y + x, :, d1], dx1, 128)
    net.wait(dy2, v2_in)
    add_into(pd.at[2 * y + x, :, d2], dy2, 128)
    for peer, pz in peers:
        net.send(pd.at[2 * y + x, rows_of(96 * pz, 96)], rzd.at[z], peer, zd_in + z)
    net.local(pd.at[2 * y + x, rows_of(96 * z, 96)], rzd.at[z], zd_in + z)

    gain_sum[...] = jnp.zeros_like(gain_sum)
    for part in range(4):
        net.wait(gz.at[part], gz_in + part)
        gain_sum[...] += gz[part]
    gh_in = net.land(3)
    for i, to in enumerate((xdev, ydev, sib)):
        gh[i] = gain_sum[...]
        net.send(gh.at[i], gh.at[3 + i], to, gh_in + i)
        net.wait(gh.at[3 + i], gh_in + i)
        gain_sum[...] += gh[3 + i]

    for part in range(4):
        net.wait(rzq.at[part], zq_in + part)
    sum_parts(rzq, sum_q, 384)
    for part in range(4):
        net.wait(rz.at[part], zr_in + part)
    sum_parts(rz, sum_r, 384)
    for part in range(4):
        net.wait(rzd.at[part], zd_in + part)
    sum_parts(rzd, sum_d, 256)
    net.wait(mask_rows, got_mask)
    net.wait(d_rows, got_back)
    net.finish()


VMEM_SPEC = pl.BlockSpec(memory_space=pltpu.VMEM)
ANY_SPEC = pl.BlockSpec(memory_space=pl.ANY)


def call(body, ident, specs, outs, scratch, sems, args, cost):
    out_shape = tuple(jax.ShapeDtypeStruct(shape, kind) for shape, kind, _ in outs)
    scratch_shapes = [pltpu.VMEM(shape, kind) for shape, kind in scratch]
    if sems:
        scratch_shapes += [pltpu.SemaphoreType.DMA((n,)) for n in sems]
    extra = {} if ident is None else dict(collective_id=ident, has_side_effects=True)
    return pl.pallas_call(
        body,
        out_shape=out_shape,
        in_specs=list(specs),
        out_specs=tuple(spec for _, _, spec in outs),
        scratch_shapes=scratch_shapes,
        compiler_params=pltpu.CompilerParams(vmem_limit_bytes=60 * 2**20, **extra),
        cost_estimate=pl.CostEstimate(flops=cost, bytes_accessed=2**24, transcendentals=0),
    )(*args)


def home_plan(
    patches,
    classes,
    slot_lengths,
    w_qkv,
    w_out,
    w_up,
    w_down,
    w_patch,
    w_class,
    norm1,
    norm2,
    mask_gain,
    d_masks,
):
    V, A = VMEM_SPEC, ANY_SPEC
    xin = jnp.concatenate([patches, jnp.pad(classes, ((0, CLS - REAL), (0, 0)))], axis=0)
    pad_cols = ((0, 0), (0, 0), (0, CLS - REAL))
    dmx = jnp.pad(d_masks.reshape(PATCH, 2, REAL), pad_cols).reshape(PATCH, 2 * CLS)
    dmx = jnp.pad(dmx, ((0, 0), (0, 256 - 2 * CLS))).astype(BF)
    gain = jnp.pad(mask_gain.reshape(1, 2, REAL), pad_cols).reshape(1, 2 * CLS)
    gain = jnp.pad(gain, ((0, 7), (0, 256 - 2 * CLS)))
    aux = jnp.broadcast_to(jnp.pad(slot_lengths.reshape(2, 1), ((0, 6), (0, 0))), (8, 128))
    g1, g2 = norm1.astype(F32)[:, None], norm2.astype(F32)[:, None]
    wqa = (w_qkv.astype(F32) * g1).astype(BF).reshape(24, 3, 2, 384)
    wqa = jnp.transpose(wqa, (0, 2, 1, 3)).reshape(24, 2304)
    wra = jnp.concatenate([(w_up.astype(F32) * g2).astype(BF), w_out, w_patch, w_class], axis=1)
    wide = wra.shape[1]
    xs, dmh, auxh, wq, wr, wdn = call(
        gather_kernel,
        1,
        [V, V, V, V, V, A],
        [
            ((SLOT_ROWS, 768), BF, A),
            ((PATCH, 256), BF, A),
            ((8, 128), jnp.int32, A),
            ((768, 1152), BF, A),
            ((768, wide), BF, A),
            ((3072, 768), BF, A),
        ],
        [
            ((4, 24, 2304), BF),
            ((4, 24, wide), BF),
            ((96, 2304), BF),
            ((96, wide), BF),
        ],
        (80, 100),
        (xin, dmx, aux, wqa, wra, w_down),
        0,
    )
    wp, zn, qr, kr, vr, out, stats = call(
        forward_kernel,
        None,
        [V] * 3,
        [((768, 768), BF, V), ((SLOT_ROWS, 768), BF, V)]
        + [((SLOT_ROWS, 256), BF, V)] * 4
        + [((SLOT_ROWS, 128), F32, V)],
        [((3, SLOT_ROWS, 256), BF)] * 2,
        (),
        (xs, wq, auxh),
        10**10,
    )
    gr, gd, dh, d_out, masks, gain_part = call(
        middle_kernel,
        2,
        [A, V, A, A, V, V, V],
        [
            ((768, wide), BF, V),
            ((3072, 768), BF, V),
            ((ROWS, 768), F32, V),
            ((SLOT_ROWS, 256), BF, V),
            ((PATCH, 256), BF, V),
            ((8, 256), F32, V),
        ],
        [
            ((768, wide), BF),
            ((3072, 768), BF),
            ((ROWS, 768), BF),
            ((4, ROWS, 256), BF),
            ((ROWS, 768), BF),
            ((768, ROWS), BF),
            ((ROWS, 768), BF),
            ((ROWS, 3072), BF),
            ((ROWS, 3072), F32),
            ((ROWS, 3072), BF),
            ((ROWS, 768), F32),
            ((ROWS, 768), F32),
            ((ROWS, 768), BF),
            ((PATCH, 768), F32),
            ((4 * CLS, 768), BF),
            ((4 * CLS, 768), BF),
            ((4, CLS, 768), BF),
            ((ROWS, 768), BF),
            ((ROWS, 128), F32),
        ],
        (24, 24),
        (xs, out, wr, wdn, dmh, auxh, gain),
        10**10,
    )
    gq, d_first = call(
        backward_kernel,
        None,
        [V] * 9,
        [((768, 768), BF, V), ((SLOT_ROWS, 768), BF, V)],
        [
            ((128, SLOT_ROWS), F32),
            ((8, SLOT_ROWS), F32),
            ((SLOT_ROWS, 256), F32),
            ((SLOT_ROWS, 768), BF),
            ((768, SLOT_ROWS), BF),
        ],
        (),
        (zn, qr, kr, vr, out, stats, d_out, wp, auxh),
        10**10,
    )
    d_rows, mask_rows, sum_q, sum_r, sum_d, gain_sum = call(
        reduce_kernel,
        3,
        [A, A, A, A, V, A, A, V],
        [
            ((ROWS, 768), BF, A),
            ((PATCH, 256), BF, A),
            ((24, 2304), F32, V),
            ((24, wide), F32, V),
            ((96, 768), F32, V),
            ((8, 256), F32, V),
        ],
        [
            ((ROWS, 768), BF),
            ((4, 96, wide), BF),
            ((4, 384, 768), BF),
            ((4, 96, wide), BF),
            ((4, 384, 768), BF),
            ((2, 96, wide // 2), BF),
            ((96, wide // 2), BF),
            ((2, 96, wide // 2), BF),
            ((96, wide // 2), BF),
            ((2, 384, 384), BF),
            ((384, 384), BF),
            ((2, 384, 384), BF),
            ((384, 384), BF),
            ((4, 24, wide), BF),
            ((4, 24, wide), BF),
            ((4, 96, 768), BF),
            ((4, 96, 768), BF),
            ((4, 96, 768), BF),
            ((4, 96, 1152), BF),
            ((2, 96, 1152), BF),
            ((96, 1152), BF),
            ((96, 2304), BF),
            ((4, 24, 2304), BF),
            ((4, 24, 2304), BF),
            ((2, ROWS, 768), BF),
            ((2, ROWS, 768), BF),
            ((ROWS, 768), BF),
            ((ROWS, 768), BF),
            ((4, 8, 256), F32),
            ((6, 8, 256), F32),
        ],
        (60, 90),
        (gr, gd, gq, d_first, dh, xs, masks, gain_part),
        0,
    )

    def unpad(values):
        return values[:, 0 : 2 * CLS].reshape(-1, 2, CLS)[:, :, 0:REAL].reshape(-1, 2 * REAL)

    d_rows = d_rows.astype(F32)
    sum_q = jnp.transpose(sum_q.reshape(24, 2, 3, 384), (0, 2, 1, 3)).reshape(24, 2304)
    sum_up = sum_r[:, 0:3072]
    return (
        unpad(mask_rows).astype(F32),
        d_rows[0:PATCH],
        d_rows[PATCH : PATCH + REAL],
        sum_q * g1,
        sum_r[:, 3072:3840],
        sum_up * g2,
        sum_d,
        sum_r[:, 3840:4608],
        sum_r[:, 4608:5376],
        jnp.sum(sum_q * w_qkv.astype(F32), axis=1),
        jnp.sum(sum_up * w_up.astype(F32), axis=1),
        unpad(gain_sum[0:1])[0],
    )


def solution(mesh):
    placed = (
        P(("tok", "head"), None),
        P(("tok", "head"), None),
        P("tok", None),
        P(("tok", "head"), None),
        P(("tok", "head"), None),
        P(("tok", "head"), None),
        P(("tok", "head"), None),
        P(("tok", "head"), None),
        P(("tok", "head"), None),
        P(("tok", "head")),
        P(("tok", "head")),
        P(),
        P(("tok", "head"), None),
    )
    fits = mesh.shape["tok"] == 8 and mesh.shape["head"] == 4
    return jax.shard_map(
        home_plan if fits else per_device,
        mesh=mesh,
        in_specs=placed,
        out_specs=(
            P(("tok", "head"), None),
            P(("tok", "head"), None),
            P(("tok", "head"), None),
            P(("tok", "head"), None),
            P(("tok", "head"), None),
            P(("tok", "head"), None),
            P(("tok", "head"), None),
            P(("tok", "head"), None),
            P(("tok", "head"), None),
            P(("tok", "head")),
            P(("tok", "head")),
            P(),
        ),
        check_vma=False,
    )
```

```python
import jax
import jax.numpy as jnp
from jax import lax
from jax.experimental import pallas as pl
from jax.experimental.pallas import tpu as pltpu
from jax.sharding import PartitionSpec as P

HEADS = 12
NCLS = 150


def layer_norm(values, gain):
    centre = values - jnp.mean(values, axis=-1, keepdims=True)
    spread = jnp.mean(centre * centre, axis=-1, keepdims=True)
    return centre * lax.rsqrt(spread + 1e-05) * gain


def unit_rows(values):
    return values * lax.rsqrt(jnp.sum(values * values, axis=-1, keepdims=True) + 1e-06)


def exact_gelu(values):
    return jax.nn.gelu(values, approximate=False)


def dot_plain(left, right):
    return jnp.dot(left, right, preferred_element_type=jnp.float32)


def dot_left_t(left, right):
    return lax.dot_general(
        left, right, (((0,), (0,)), ((), ())), preferred_element_type=jnp.float32
    )


def dot_right_t(left, right):
    return lax.dot_general(
        left, right, (((1,), (1,)), ((), ())), preferred_element_type=jnp.float32
    )


def flat_rows(matrix):
    return matrix.reshape(-1, 128)


def per_device(
    patches,
    classes,
    slot_lengths,
    w_qkv,
    w_out,
    w_up,
    w_down,
    w_patch,
    w_class,
    norm1,
    norm2,
    mask_gain,
    d_masks,
):
    tok_rows = patches.shape[0]
    cls_rows = classes.shape[0]
    all_rows = tok_rows + cls_rows
    width = patches.shape[1]
    groups = lax.axis_size("head")
    my_group = lax.axis_index("head")
    local_heads = HEADS // groups
    head_size = width // HEADS
    lead_len = slot_lengths[0, 0]
    tail_len = slot_lengths[0, 1]

    def segment_of(source, offset):
        place = source * tok_rows + offset
        patch_seg = jnp.where(place < lead_len, 0, jnp.where(place < lead_len + tail_len, 1, -1))
        class_seg = (source * cls_rows + offset - tok_rows) // NCLS
        return jnp.where(offset < tok_rows, patch_seg, class_seg)

    tok_seg = segment_of(my_group, jnp.arange(tok_rows))
    spread_rows = jnp.arange(groups * all_rows)
    head_seg = segment_of(spread_rows // all_rows, spread_rows % all_rows)
    allowed = (head_seg[:, None] == head_seg[None, :]) & (head_seg[None, :] >= 0)
    shards = (w_qkv, w_out, w_up, w_down, w_patch, w_class, norm1, norm2)
    gathered = (
        lax.all_gather(shards[0], ("tok", "head"), axis=0, tiled=True),
        lax.all_gather(shards[1], ("tok", "head"), axis=0, tiled=True),
        lax.all_gather(shards[2], ("tok", "head"), axis=0, tiled=True),
        lax.all_gather(shards[3], ("tok", "head"), axis=0, tiled=True),
        lax.all_gather(shards[4], ("tok", "head"), axis=0, tiled=True),
        lax.all_gather(shards[5], ("tok", "head"), axis=0, tiled=True),
        lax.all_gather(shards[6], ("tok", "head"), axis=0, tiled=True),
        lax.all_gather(shards[7], ("tok", "head"), axis=0, tiled=True),
    )
    full_qkv, full_out, full_up, full_down, full_patch, full_class, gain_one, gain_two = gathered
    stacked = jnp.concatenate([patches, classes], axis=0).astype(jnp.float32)
    first_in = layer_norm(stacked, gain_one.astype(jnp.float32)).astype(jnp.bfloat16)
    qkv_rows = (
        dot_plain(first_in, full_qkv)
        .astype(jnp.bfloat16)
        .reshape(all_rows, 3, groups, local_heads * head_size)
    )
    moved = lax.all_to_all(qkv_rows, "head", split_axis=2, concat_axis=0, tiled=True)
    moved = moved.reshape(groups * all_rows, 3, local_heads, head_size)
    queries = jnp.transpose(moved[:, 0], (1, 0, 2))
    key_rows = jnp.transpose(moved[:, 1], (1, 0, 2))
    value_rows = jnp.transpose(moved[:, 2], (1, 0, 2))

    def attend(parts):
        query, key_part, value_part = parts
        scores = jnp.where(allowed, dot_right_t(query, key_part) * 0.125, -1e30)
        top_score = jnp.max(scores, axis=1, keepdims=True)
        expo = jnp.exp(scores - top_score)
        total = jnp.sum(expo, axis=1, keepdims=True)
        probs = (expo / total).astype(jnp.bfloat16)
        result = dot_plain(probs, value_part).astype(jnp.bfloat16)
        return (result, top_score[:, 0] + jnp.log(total[:, 0]))

    head_out, log_total = lax.map(attend, (queries, key_rows, value_rows))
    sending = jnp.transpose(head_out, (1, 0, 2)).reshape(
        groups * all_rows, 1, local_heads * head_size
    )
    attended = lax.all_to_all(sending, "head", split_axis=0, concat_axis=1, tiled=True).reshape(
        all_rows, width
    )
    hidden = stacked + dot_plain(attended, full_out)
    second_in = layer_norm(hidden, gain_two.astype(jnp.float32)).astype(jnp.bfloat16)
    up_rows = dot_plain(second_in, full_up)
    gelu_rows = exact_gelu(up_rows).astype(jnp.bfloat16)
    after = (hidden + dot_plain(gelu_rows, full_down)).astype(jnp.bfloat16)
    patch_proj = dot_plain(after[:tok_rows], full_patch)
    class_proj = dot_plain(after[tok_rows:], full_class)
    patch_unit = unit_rows(patch_proj).astype(jnp.bfloat16)
    class_unit = unit_rows(class_proj).astype(jnp.bfloat16)
    slot_classes = lax.all_gather(class_unit, "head", axis=0, tiled=True)
    raw_both = dot_right_t(patch_unit, slot_classes)
    first_image = tok_seg[:, None] == 0
    raw = jnp.where(first_image, raw_both[:, :NCLS], raw_both[:, NCLS:])
    centre = raw - jnp.mean(raw, axis=1, keepdims=True)
    inv_sigma = lax.rsqrt(jnp.mean(centre * centre, axis=1, keepdims=True) + 1e-05)
    normed = centre * inv_sigma
    valid = (tok_seg >= 0).astype(jnp.float32)[:, None]
    masks = normed * mask_gain * valid
    regathered = (
        lax.all_gather(shards[0], ("tok", "head"), axis=0, tiled=True),
        lax.all_gather(shards[1], ("tok", "head"), axis=0, tiled=True),
        lax.all_gather(shards[2], ("tok", "head"), axis=0, tiled=True),
        lax.all_gather(shards[3], ("tok", "head"), axis=0, tiled=True),
        lax.all_gather(shards[4], ("tok", "head"), axis=0, tiled=True),
        lax.all_gather(shards[5], ("tok", "head"), axis=0, tiled=True),
        lax.all_gather(shards[6], ("tok", "head"), axis=0, tiled=True),
        lax.all_gather(shards[7], ("tok", "head"), axis=0, tiled=True),
    )
    back_qkv, back_out, back_up, back_down, back_patch, back_class, back_one, back_two = regathered
    mask_cot = d_masks * valid
    grad_mask = lax.psum(jnp.sum(mask_cot * normed, axis=0), ("tok", "head"))
    scaled = mask_cot * mask_gain
    d_raw = inv_sigma * (
        scaled
        - jnp.mean(scaled, axis=1, keepdims=True)
        - normed * jnp.mean(scaled * normed, axis=1, keepdims=True)
    )
    zero_part = jnp.zeros_like(d_raw)
    d_raw_both = jnp.concatenate(
        [jnp.where(first_image, d_raw, zero_part), jnp.where(first_image, zero_part, d_raw)], axis=1
    ).astype(jnp.bfloat16)
    d_patch_unit = dot_plain(d_raw_both, slot_classes)
    d_slot_classes = dot_left_t(d_raw_both, patch_unit)
    d_class_unit = lax.psum_scatter(
        d_slot_classes.astype(jnp.bfloat16), "head", scatter_dimension=0, tiled=True
    ).astype(jnp.float32)
    _, patch_pull = jax.vjp(unit_rows, patch_proj)
    d_patch_proj = patch_pull(d_patch_unit)[0].astype(jnp.bfloat16)
    _, class_pull = jax.vjp(unit_rows, class_proj)
    d_class_proj = class_pull(d_class_unit)[0].astype(jnp.bfloat16)
    grad_patch_w = dot_left_t(after[:tok_rows], d_patch_proj)
    grad_class_w = dot_left_t(after[tok_rows:], d_class_proj)
    d_after = jnp.concatenate(
        [dot_right_t(d_patch_proj, back_patch), dot_right_t(d_class_proj, back_class)], axis=0
    )
    d_after_low = d_after.astype(jnp.bfloat16)
    grad_down_w = dot_left_t(gelu_rows, d_after_low)
    d_gelu = dot_right_t(d_after_low, back_down)
    _, gelu_pull = jax.vjp(exact_gelu, up_rows)
    d_up_rows = gelu_pull(d_gelu)[0].astype(jnp.bfloat16)
    grad_up_w = dot_left_t(second_in, d_up_rows)
    d_second_in = dot_right_t(d_up_rows, back_up)
    _, norm_two_pull = jax.vjp(layer_norm, hidden, back_two.astype(jnp.float32))
    d_hidden_norm, grad_gain_two = norm_two_pull(d_second_in)
    d_hidden = d_after + d_hidden_norm
    d_hidden_low = d_hidden.astype(jnp.bfloat16)
    grad_out_w = dot_left_t(attended, d_hidden_low)
    d_attended = (
        dot_right_t(d_hidden_low, back_out)
        .astype(jnp.bfloat16)
        .reshape(all_rows, groups, local_heads * head_size)
    )
    d_head_out = lax.all_to_all(d_attended, "head", split_axis=1, concat_axis=0, tiled=True)
    d_head_out = jnp.transpose(
        d_head_out.reshape(groups * all_rows, local_heads, head_size), (1, 0, 2)
    )

    def attend_back(parts):
        query, key_part, value_part, log_row, d_result = parts
        scores = jnp.where(allowed, dot_right_t(query, key_part) * 0.125, -1e30)
        probs = jnp.exp(scores - log_row[:, None])
        d_probs = dot_right_t(d_result, value_part)
        inner = jnp.sum(probs * d_probs, axis=1, keepdims=True)
        d_scores = jnp.where(allowed, probs * (d_probs - inner), 0.0).astype(jnp.bfloat16)
        d_query = (dot_plain(d_scores, key_part) * 0.125).astype(jnp.bfloat16)
        d_key = (dot_left_t(d_scores, query) * 0.125).astype(jnp.bfloat16)
        d_value = dot_left_t(probs.astype(jnp.bfloat16), d_result).astype(jnp.bfloat16)
        return jnp.stack([d_query, d_key, d_value], axis=0)

    d_moved = lax.map(attend_back, (queries, key_rows, value_rows, log_total, d_head_out))
    d_moved = jnp.transpose(d_moved, (2, 1, 0, 3)).reshape(
        groups * all_rows, 3, 1, local_heads * head_size
    )
    d_qkv = lax.all_to_all(d_moved, "head", split_axis=0, concat_axis=2, tiled=True).reshape(
        all_rows, 3 * width
    )
    grad_qkv_w = dot_left_t(first_in, d_qkv)
    d_first_in = dot_right_t(d_qkv, back_qkv)
    _, norm_one_pull = jax.vjp(layer_norm, stacked, back_one.astype(jnp.float32))
    d_stacked_norm, grad_gain_one = norm_one_pull(d_first_in)
    d_stacked = d_hidden + d_stacked_norm
    every_sum = (
        lax.psum_scatter(flat_rows(grad_qkv_w), ("tok", "head"), scatter_dimension=0, tiled=True),
        lax.psum_scatter(flat_rows(grad_out_w), ("tok", "head"), scatter_dimension=0, tiled=True),
        lax.psum_scatter(flat_rows(grad_up_w), ("tok", "head"), scatter_dimension=0, tiled=True),
        lax.psum_scatter(flat_rows(grad_down_w), ("tok", "head"), scatter_dimension=0, tiled=True),
        lax.psum_scatter(flat_rows(grad_patch_w), ("tok", "head"), scatter_dimension=0, tiled=True),
        lax.psum_scatter(flat_rows(grad_class_w), ("tok", "head"), scatter_dimension=0, tiled=True),
        lax.psum_scatter(grad_gain_one, ("tok", "head"), scatter_dimension=0, tiled=True),
        lax.psum_scatter(grad_gain_two, ("tok", "head"), scatter_dimension=0, tiled=True),
    )
    sum_qkv, sum_out, sum_up, sum_down, sum_patch, sum_class, sum_one, sum_two = every_sum
    sum_qkv = sum_qkv.reshape(-1, 3 * width)
    sum_out = sum_out.reshape(-1, width)
    sum_up = sum_up.reshape(-1, grad_up_w.shape[1])
    sum_down = sum_down.reshape(-1, width)
    sum_patch = sum_patch.reshape(-1, width)
    sum_class = sum_class.reshape(-1, width)
    return (
        masks,
        d_stacked[:tok_rows],
        d_stacked[tok_rows:],
        sum_qkv,
        sum_out,
        sum_up,
        sum_down,
        sum_patch,
        sum_class,
        sum_one,
        sum_two,
        grad_mask,
    )


ROWS = 336
SLOT_ROWS = 4 * ROWS
PATCH = 256
CLS = 80
REAL = 75
PIECE = 80
LEAD = 16
MESH = pl.DeviceIdType.MESH
BF = jnp.bfloat16
F32 = jnp.float32


def position():
    tok = lax.axis_index("tok")
    return lax.div(tok, 4), lax.rem(lax.div(tok, 2), 2), lax.rem(tok, 2), lax.axis_index("head")


def device(y, x, c, z):
    return {"tok": y * 4 + x * 2 + c, "head": z}


def enter(y, x, c, z):
    barrier = pltpu.get_barrier_semaphore()
    others = [device(1 - y, x, c, z)]
    for turn in range(1, 16):
        flip_x, flip_c, step = turn // 8, (turn // 4) % 2, turn % 4
        others.append(
            device(
                y,
                1 - x if flip_x else x,
                1 - c if flip_c else c,
                lax.rem(z + step, 4),
            )
        )
    for other in others:
        pl.semaphore_signal(barrier, inc=1, device_id=other, device_id_type=MESH)
    pl.semaphore_wait(barrier, len(others))


class Net:
    def __init__(self, send_sem, recv_sem, here):
        self.send_sem, self.recv_sem, self.here = send_sem, recv_sem, here
        self.sends, self.recvs, self.open = 0, 0, []

    def land(self, count=1):
        first = self.recvs
        self.recvs += count
        return first

    def send(self, src, dst, to, slot, skip=None):
        index = self.sends
        self.sends += 1
        copy = pltpu.make_async_remote_copy(
            src_ref=src,
            dst_ref=dst,
            send_sem=self.send_sem.at[index],
            recv_sem=self.recv_sem.at[slot],
            device_id=to,
            device_id_type=MESH,
        )
        if skip is None:
            copy.start()
            self.open.append((copy, None))
        else:
            pl.when(jnp.logical_not(skip))(copy.start)
            self.open.append((copy, skip))

            @pl.when(skip)
            def _():
                pltpu.make_async_copy(src, dst, self.recv_sem.at[slot]).start()

    def local(self, src, dst, slot):
        pltpu.make_async_copy(src, dst, self.recv_sem.at[slot]).start()

    def wait(self, ref, slot):
        pltpu.make_async_copy(ref, ref, self.recv_sem.at[slot]).wait()

    def finish(self):
        for copy, skip in self.open:
            if skip is None:
                copy.wait_send()
            else:
                pl.when(jnp.logical_not(skip))(copy.wait_send)
        self.open = []


def rows_of(start, size):
    return pl.ds(pl.multiple_of(start, 16), size)


def lanes_of(start, size):
    return pl.ds(pl.multiple_of(start, 128), size)


def nn(left, right):
    return jnp.dot(left, right, preferred_element_type=F32)


def nt(left, right):
    return lax.dot_general(left, right, (((1,), (1,)), ((), ())), preferred_element_type=F32)


def tn(left, right):
    return lax.dot_general(left, right, (((0,), (0,)), ((), ())), preferred_element_type=F32)


def segments(row, lead_len, tail_len):
    source = (
        (row >= ROWS).astype(jnp.int32)
        + (row >= 2 * ROWS).astype(jnp.int32)
        + (row >= 3 * ROWS).astype(jnp.int32)
    )
    offset = row - source * ROWS
    patch = source * PATCH + offset
    patch_seg = jnp.where(patch < lead_len, 0, jnp.where(patch < lead_len + tail_len, 1, -1))
    number = offset - PATCH
    class_seg = jnp.where(source >= 2, 1, 0)
    filler = number >= REAL
    seg = jnp.where(offset < PATCH, patch_seg, jnp.where(filler, -1, class_seg))
    return seg, filler


def normalise(values):
    centre = values - jnp.mean(values, axis=-1, keepdims=True)
    scale = lax.rsqrt(jnp.mean(centre * centre, axis=-1, keepdims=True) + 1e-05)
    return centre * scale, scale


def own_lanes(c, head, shape):
    lane = lax.broadcasted_iota(jnp.int32, shape, len(shape) - 1)
    group = lane // 64 - c
    if head is None:
        return (group >= 0) & (group < 3)
    return group == head


def group_of(y, x, c, z):
    quarter = 2 * x + c
    return [
        (device(y, x, 1 - c, z), quarter + 1 - 2 * c),
        (device(y, 1 - x, c, z), quarter + 2 - 4 * x),
        (device(y, 1 - x, 1 - c, z), quarter + 3 - 4 * x - 2 * c),
    ]


TILE = 256


class Pump:
    def __init__(self):
        self.todo = []

    def add(self, step):
        self.todo.append(step)

    def run(self, count=None):
        count = len(self.todo) if count is None else min(count, len(self.todo))
        for step in self.todo[:count]:
            step()
        self.todo = self.todo[count:]


def join(stage, block, start, size, width):
    def body(i, carry):
        cols = lanes_of(start + i * width, width)
        parts = [stage[src, :, cols].astype(F32) for src in range(4)]
        block[:, cols] = jnp.concatenate(parts, axis=0).astype(BF)
        return carry

    lax.fori_loop(0, size // width, body, 0)


OUT_AT, UP_AT, PATCH_AT, CLASS_AT = 0, 768, 3840, 4608


def front_kernel(
    xin, dmx, aux_in, wqa, wra, wd_in, gain,
    gr_o, gd_o, dh, dob, masks, gain_part, zn_o, qr_o, kr_o, vr_o, out_o, stats_o, wp_o, xb_o, aux_o,
    xs, zn, qr, kr, vr, out, stats, wp, wq, wr, wd, stq, str_, bq, pool0, pool1,
    gr, gd, dmh, aux, obuf, att, znt, zn2, h_f, dz_f, dzb, pp_f, cn, dcn, dcbuf, inv,
    send_sem, recv_sem,
):
    y, x, c, z = position()
    tok = y * 4 + x * 2 + c
    quarter = 2 * x + c
    enter(y, x, c, z)
    net = Net(send_sem, recv_sem, None)
    sib, xdev, ydev = device(y, x, 1 - c, z), device(y, 1 - x, c, z), device(1 - y, x, c, z)
    flip = 1 - 2 * c
    t_x, t_y = tok + 2 - 4 * x, tok + 4 - 8 * y
    t_xy = t_x + 4 - 8 * y
    other = quarter + 2 - 4 * x
    peers = [device(y, x, c, lax.rem(z + step, 4)) for step in (1, 3, 2)]
    outs = []

    def store(src, dst):
        slot = net.land()
        net.local(src, dst, slot)
        outs.append((dst, slot))

    home = 2 * c + x
    got_lead, got_piece, got_dm, got_aux = net.land(4), net.land(4), net.land(), net.land()
    for q in (3, 2, 1, 0):
        to = device(y, q // 2, q % 2, home)
        mine = (z == home) & (quarter == q)
        off = LEAD + PIECE * q
        net.send(
            xin.at[pl.ds(off, PIECE)],
            xs.at[rows_of(z * ROWS + off, PIECE)],
            to,
            got_piece + z,
            mine,
        )
        net.send(xin.at[pl.ds(0, LEAD)], xs.at[rows_of(z * ROWS, LEAD)], to, got_lead + z, mine)
    to_home = device(y, lax.div(z, 2), lax.rem(z, 2), home)
    at_home = (z == home) & (quarter == z)
    net.send(aux_in, aux, to_home, got_aux, at_home)

    def blk(t):
        return rows_of(t * 96, 96)

    def big(t):
        return rows_of(t * 384, 384)

    q_cols = [pl.ds(768 * part, 768) for part in range(3)]
    got_q = [net.land(4) for _ in range(3)]
    for part in range(3):
        net.local(wqa.at[:, q_cols[part]], stq.at[z, :, q_cols[part]], got_q[part] + z)
        for peer in peers:
            net.send(wqa.at[:, q_cols[part]], stq.at[z, :, q_cols[part]], peer, got_q[part] + z)
    chunks = [(OUT_AT, 768), (UP_AT, 1536), (UP_AT + 1536, 1536), ("d", 0), ("d", 256), ("d", 512), (PATCH_AT, 1536)]
    got_z = [net.land(4) for _ in chunks]

    def raw_send(k):
        at, size = chunks[k]
        if at == "d":
            cols = pl.ds(size, 256)
            src, dst = wd_in.at[:, cols], wd.at[rows_of((tok * 4 + z) * 96, 96), cols]
        else:
            cols = pl.ds(at, size)
            src, dst = wra.at[:, cols], str_.at[z, :, cols]
        net.local(src, dst, got_z[k] + z)
        for peer in peers:
            net.send(src, dst, peer, got_z[k] + z)

    def piece(source, owner):
        return xs.at[rows_of(source * ROWS + LEAD + PIECE * owner, PIECE)]

    fwd_s, fwd_x, fwd_xs = net.land(4), net.land(4), net.land(4)
    for src in range(4):
        net.wait(piece(src, quarter), got_piece + src)
        net.send(piece(src, quarter), piece(src, quarter), xdev, fwd_x + src)
        net.send(piece(src, quarter), piece(src, quarter), sib, fwd_s + src)
    raw_send(0)
    raw_send(1)

    q_x, q_y, q_xy, q_s = net.land(3), net.land(3), net.land(3), net.land(12)

    def q_join(part):
        for src in range(4):
            net.wait(stq.at[src, :, q_cols[part]], got_q[part] + src)
        join(stq, bq, 768 * part, 768, 384)
        own = lanes_of(768 * part + 384 * x, 384)
        far = lanes_of(768 * part + 384 * (1 - x), 384)
        cols = pl.ds(384 * part, 384)
        net.send(bq.at[:, far], wq.at[blk(tok), cols], xdev, q_x + part)
        net.send(bq.at[:, own], wq.at[blk(tok), cols], ydev, q_y + part)
        wq[blk(tok), cols] = bq[:, own]
        net.send(bq.at[:, own], wq.at[blk(tok), cols], sib, q_s + part)

    def q_cross(part):
        cols = pl.ds(384 * part, 384)
        ref = wq.at[blk(t_x), cols]
        net.wait(ref, q_x + part)
        net.send(ref, ref, ydev, q_xy + part)
        net.send(ref, ref, sib, q_s + 3 + part)

    def q_last(part):
        cols = pl.ds(384 * part, 384)
        net.wait(wq.at[blk(t_y), cols], q_y + part)
        net.send(wq.at[blk(t_y), cols], wq.at[blk(t_y), cols], sib, q_s + 6 + part)
        net.wait(wq.at[blk(t_xy), cols], q_xy + part)
        net.send(wq.at[blk(t_xy), cols], wq.at[blk(t_xy), cols], sib, q_s + 9 + part)

    for part in range(3):
        q_join(part)
        if part:
            q_cross(part - 1)
    for src in range(4):
        net.wait(piece(src, other), fwd_x + src)
        net.send(piece(src, other), piece(src, other), sib, fwd_xs + src)
    q_cross(2)
    raw_send(2)
    net.send(dmx, dmh, to_home, got_dm, at_home)

    sx, sy, ss = [], [], []
    for _ in chunks:
        sx.append(net.land(3))
        sy.append(net.land(3))
        ss.append(net.land(4))

    def parts(k):
        at, size = chunks[k]
        if at == "d":
            return wd, big, pl.ds(size, 128), pl.ds(size + 128, 128), pl.ds(size, 256)
        return wr, blk, pl.ds(at, size // 2), pl.ds(at + size // 2, size // 2), pl.ds(at, size)

    def pass_on(ref, to, slot):
        net.send(ref, ref, to, slot)

    def stage_z(k):
        def step():
            at, size = chunks[k]
            ref, rows, a, b, both = parts(k)
            for src in range(4):
                if at == "d":
                    net.wait(wd.at[rows_of((tok * 4 + src) * 96, 96), both], got_z[k] + src)
                else:
                    net.wait(str_.at[src, :, both], got_z[k] + src)
            if at != "d":
                join(str_, wr.at[blk(tok)], at, size, 384)
            pass_on(ref.at[rows(tok), a], xdev, sx[k])
            pass_on(ref.at[rows(tok), b], ydev, sy[k])
            pass_on(ref.at[rows(tok), b], xdev, sx[k] + 1)
            pass_on(ref.at[rows(tok), a], ydev, sy[k] + 1)
            pass_on(ref.at[rows(tok), both], sib, ss[k])
            if k + 3 < len(chunks):
                raw_send(k + 3)

        return step

    def stage_one(k):
        def step():
            ref, rows, a, b, both = parts(k)
            net.wait(ref.at[rows(t_x), a], sx[k])
            pass_on(ref.at[rows(t_x), a], ydev, sy[k] + 2)
            net.wait(ref.at[rows(t_y), b], sy[k])
            pass_on(ref.at[rows(t_y), b], xdev, sx[k] + 2)

        return step

    def stage_two(k):
        def step():
            ref, rows, a, b, both = parts(k)
            net.wait(ref.at[rows(t_x), b], sx[k] + 1)
            pass_on(ref.at[rows(t_x), both], sib, ss[k] + 1)
            net.wait(ref.at[rows(t_y), a], sy[k] + 1)
            pass_on(ref.at[rows(t_y), both], sib, ss[k] + 2)

        return step

    def stage_three(k):
        def step():
            ref, rows, a, b, both = parts(k)
            net.wait(ref.at[rows(t_xy), a], sy[k] + 2)
            net.wait(ref.at[rows(t_xy), b], sx[k] + 2)
            pass_on(ref.at[rows(t_xy), both], sib, ss[k] + 3)

        return step

    def ready(k):
        ref, rows, a, b, both = parts(k)
        for i, t in enumerate((tok, t_x, t_y, t_xy)):
            net.wait(ref.at[rows(t + flip), both], ss[k] + i)

    pump = Pump()
    count = len(chunks)
    for k in range(count + 2):
        if k < count:
            pump.add(stage_z(k))
        if 0 <= k - 1 < count:
            pump.add(stage_one(k - 1))
            pump.add(stage_two(k - 1))
        if 0 <= k - 2 < count:
            pump.add(stage_three(k - 2))

    for part in range(3):
        q_last(part)
    sibling = quarter + flip
    for src in range(4):
        net.wait(xs.at[rows_of(src * ROWS, LEAD)], got_lead + src)
        net.wait(piece(src, sibling), fwd_s + src)
        net.wait(piece(src, sibling + 2 - 4 * x), fwd_xs + src)
    net.wait(aux, got_aux)
    pump.run(1)
    for part in range(3):
        cols = pl.ds(384 * part, 384)
        for i, t in enumerate((tok, t_x, t_y, t_xy)):
            net.wait(wq.at[blk(t + flip), cols], q_s + 3 * i + part)

    lead_len, tail_len = aux[0:1, 0:1], aux[1:2, 0:1]
    keep = own_lanes(c, None, (768, 256))
    for part in range(3):
        cols = lanes_of(384 * part + 128 * c, 256)
        wp[:, 256 * part : 256 * part + 256] = jnp.where(keep, wq[:, cols], 0.0).astype(BF)

    def project(i, carry):
        rows = rows_of(i * ROWS, ROWS)
        normed = normalise(xs[rows, :].astype(F32))[0].astype(BF)
        zn[rows, :] = normed
        qr[rows, :] = (nn(normed, wp[:, 0:256]).astype(BF) * 0.125).astype(BF)
        kr[rows, :] = nn(normed, wp[:, 256:512]).astype(BF)
        vr[rows, :] = nn(normed, wp[:, 512:768]).astype(BF)
        return carry

    lax.fori_loop(0, 4, project, 0)
    pump.run(2)
    for head in range(3):
        mine = own_lanes(c, head, (SLOT_ROWS, 256))
        cols = pl.ds(256 * head, 256)
        pool0[:, cols] = jnp.where(mine, kr[...], 0.0).astype(BF)
        pool1[:, cols] = jnp.where(mine, vr[...], 0.0).astype(BF)
    own_rows = rows_of(quarter * ROWS, ROWS)
    store(zn, zn_o)
    store(qr, qr_o)
    store(kr, kr_o)
    store(vr, vr_o)
    store(wp, wp_o)
    store(xs.at[own_rows], xb_o)
    store(aux, aux_o)
    key_row = lax.broadcasted_iota(jnp.int32, (1, SLOT_ROWS), 1)
    key_seg, key_filler = segments(key_row, lead_len, tail_len)
    key_seg = jnp.where(key_seg < 0, -5, key_seg)
    masked = jnp.where(key_filler, -3e38, -1e30)
    group = group_of(y, x, c, z)
    got_o, got_cn, got_dc = net.land(4), net.land(4), net.land(4)
    lane = lax.broadcasted_iota(jnp.int32, (ROWS, 128), 1)
    for to, q in group[::-1] + [(None, quarter)]:
        rows = rows_of(q * ROWS, ROWS)
        row = lax.broadcasted_iota(jnp.int32, (ROWS, 1), 0) + q * ROWS
        seg = segments(row, lead_len, tail_len)[0]
        query = qr[rows, :]
        total_out = jnp.zeros((ROWS, 256), F32)
        kept = jnp.zeros((ROWS, 128), F32)
        for head in range(3):
            cols = pl.ds(256 * head, 256)
            scores = jnp.where(seg == key_seg, nt(query, pool0[:, cols]), masked)
            top = jnp.max(scores, axis=1, keepdims=True)
            expo = jnp.exp(scores - top)
            total = jnp.sum(expo, axis=1, keepdims=True)
            probs = (expo * (1.0 / total)).astype(BF)
            total_out = total_out + nn(probs, pool1[:, cols])
            kept = jnp.where(lane == head, top + jnp.log(total), kept)
            pump.run(2)
        out[rows, :] = total_out.astype(BF)
        stats[rows, :] = kept
        if to is None:
            net.local(out.at[rows], obuf.at[quarter], got_o + quarter)
        else:
            net.send(out.at[rows], obuf.at[quarter], to, got_o + quarter)
    store(out, out_o)
    store(stats, stats_o)

    row = lax.broadcasted_iota(jnp.int32, (PATCH, 1), 0) + quarter * ROWS
    seg = segments(row, lead_len, tail_len)[0]
    first_image = seg == 0
    valid = jnp.where(seg >= 0, 1.0, 0.0)
    for q in range(4):
        net.wait(obuf.at[q], got_o + q)
    for side in range(2):
        a, b = obuf[2 * side], obuf[2 * side + 1]
        base = 384 * side
        att[:, base : base + 128] = a[:, 0:128]
        att[:, base + 128 : base + 256] = a[:, 128:256] + b[:, 0:128]
        att[:, base + 256 : base + 384] = b[:, 128:256]
    pump.run()
    ready(0)
    w_out = wr.at[:, pl.ds(OUT_AT, 768)]
    w_patch, w_class = wr.at[:, pl.ds(PATCH_AT, 768)], wr.at[:, pl.ds(CLASS_AT, 768)]
    h_f[...] = xs[own_rows, :].astype(F32) + nn(att[...], w_out[...])
    normed, scale = normalise(h_f[...])
    inv[...] = jnp.broadcast_to(scale, inv.shape)
    zn2[...] = normed.astype(BF)
    znt[...] = normed.T.astype(BF)
    ready(1)
    ready(2)
    gl, slope = pool0, pool1

    def panel(i):
        return rows_of(lax.div(i, 3) * ROWS, ROWS), lanes_of(lax.rem(i, 3) * TILE, TILE)

    def up_step(i, carry):
        u = nn(zn2[...], wr[:, lanes_of(UP_AT + i * TILE, TILE)])
        cdf = 0.5 * (1.0 + lax.erf(u * 0.7071067811865476))
        rows, cols = panel(i)
        gl[rows, cols] = (u * cdf).astype(BF)
        slope[rows, cols] = (cdf + u * (jnp.exp(-0.5 * u * u) * 0.3989422804014327)).astype(BF)
        return carry

    lax.fori_loop(0, 12, up_step, 0)
    for k in range(3, count):
        ready(k)
    mlp = nn(gl[0:ROWS, :], wd[0:768, :])
    for p in range(1, 4):
        mlp = mlp + nn(gl[ROWS * p : ROWS * p + ROWS, :], wd[768 * p : 768 * p + 768, :])
    z2 = (h_f[...] + mlp).astype(BF)
    z2p, z2c = z2[0:PATCH], z2[PATCH:ROWS]

    def unit(values):
        return values * lax.rsqrt(jnp.sum(values * values, axis=-1, keepdims=True) + 1e-06)

    def unit_back(values, cot):
        r = lax.rsqrt(jnp.sum(values * values, axis=-1, keepdims=True) + 1e-06)
        return r * cot - values * (r * r * r * jnp.sum(values * cot, axis=-1, keepdims=True))

    cc = nn(z2c, w_class[...])
    own_cls = rows_of(quarter * CLS, CLS)
    cn[own_cls, :] = unit(cc).astype(BF)
    for to, q in group:
        net.send(cn.at[own_cls], cn.at[own_cls], to, got_cn + quarter)
    pp = nn(z2p, w_patch[...])
    pp_f[...] = pp
    pn = unit(pp).astype(BF)
    net.wait(dmh, got_dm)
    for to, q in group:
        net.wait(cn.at[rows_of(q * CLS, CLS)], got_cn + q)
    low, high = cn[0 : 2 * CLS, :], cn[2 * CLS : 4 * CLS, :]
    wide = 2 * CLS
    lane = lax.broadcasted_iota(jnp.int32, (1, wide), 1)
    real = jnp.where(lane >= CLS, lane - CLS, lane) < REAL
    raw = jnp.where(first_image, nt(pn, low), nt(pn, high))

    def mean(values):
        return jnp.sum(jnp.where(real, values, 0.0), axis=1, keepdims=True) * (0.5 / REAL)

    centre = jnp.where(real, raw - mean(raw), 0.0)
    sigma = lax.rsqrt(mean(centre * centre) + 1e-05)
    xhat = centre * sigma
    mask_gain = gain[0:1, 0:wide]
    dm = dmh[:, 0:wide].astype(F32) * valid
    dx = jnp.where(real, dm * mask_gain, 0.0)
    d_raw = jnp.where(real, sigma * (dx - mean(dx) - xhat * mean(dx * xhat)), 0.0)
    d_low = jnp.where(first_image, d_raw, 0.0).astype(BF)
    d_high = jnp.where(first_image, 0.0, d_raw).astype(BF)
    dcn[0:wide, :] = tn(d_low, pn).astype(BF)
    dcn[wide : 2 * wide, :] = tn(d_high, pn).astype(BF)
    for to, q in group:
        net.send(dcn.at[rows_of(q * CLS, CLS)], dcbuf.at[quarter], to, got_dc + quarter)
    net.local(dcn.at[own_cls], dcbuf.at[quarter], got_dc + quarter)
    masks[:, wide:256] = jnp.zeros((PATCH, 256 - wide), BF)
    masks[:, 0:wide] = (xhat * mask_gain * valid).astype(BF)
    gain_part[...] = jnp.zeros_like(gain_part)
    gain_part[0:1, 0:wide] = jnp.sum(dm * xhat, axis=0, keepdims=True)
    d_pn = nn(d_low, low) + nn(d_high, high)
    d_pp = unit_back(pp_f[...], d_pn).astype(BF)
    dz_f[0:PATCH, :] = nt(d_pp, w_patch[...])
    gr[:, PATCH_AT : PATCH_AT + 768] = tn(z2p, d_pp).astype(BF)
    for q in range(4):
        net.wait(dcbuf.at[q], got_dc + q)
    d_cn = dcbuf[0].astype(F32) + dcbuf[1].astype(F32) + dcbuf[2].astype(F32) + dcbuf[3].astype(F32)
    d_cc = unit_back(cc, d_cn).astype(BF)
    dz_f[PATCH:ROWS, :] = nt(d_cc, w_class[...])
    gr[:, CLASS_AT : CLASS_AT + 768] = tn(z2c, d_cc).astype(BF)
    mask_cols = pl.ds(PATCH_AT, 1536)
    store(gr.at[:, mask_cols], gr_o.at[:, mask_cols])

    dzb[...] = dz_f[...].astype(BF)

    def down_step(i, carry):
        rows, cols = panel(i)
        flat = rows_of(i * TILE, TILE)
        d_u = (nt(dzb[...], wd[flat, :]) * slope[rows, cols].astype(F32)).astype(BF)
        slope[rows, cols] = d_u
        gd[flat, :] = tn(gl[rows, cols], dzb[...]).astype(BF)
        gr[:, lanes_of(UP_AT + i * TILE, TILE)] = nn(znt[...], d_u).astype(BF)
        return carry

    lax.fori_loop(0, 12, down_step, 0)
    store(gd, gd_o)
    up_cols = pl.ds(UP_AT, 3072)
    store(gr.at[:, up_cols], gr_o.at[:, up_cols])
    d_zn = nt(slope[0:ROWS, :], wr[:, UP_AT : UP_AT + 768])
    for p in range(1, 4):
        base = UP_AT + 768 * p
        d_zn = d_zn + nt(slope[ROWS * p : ROWS * p + ROWS, :], wr[:, base : base + 768])
    normed = h_f[...]
    normed = (normed - jnp.mean(normed, axis=-1, keepdims=True)) * inv[:, 0:1]
    d_h = dz_f[...] + inv[:, 0:1] * (
        d_zn
        - jnp.mean(d_zn, axis=-1, keepdims=True)
        - normed * jnp.mean(d_zn * normed, axis=-1, keepdims=True)
    )
    dh[...] = d_h
    d_hb = d_h.astype(BF)
    dob[...] = nt(d_hb, w_out[...]).astype(BF)
    gr[:, OUT_AT : OUT_AT + 768] = tn(att[...], d_hb).astype(BF)
    out_cols = pl.ds(OUT_AT, 768)
    store(gr.at[:, out_cols], gr_o.at[:, out_cols])
    for dst, slot in outs:
        net.wait(dst, slot)
    net.finish()


def add_into(total, part, width):
    def body(i, carry):
        cols = lanes_of(i * width, width)
        total[:, cols] = (total[:, cols].astype(F32) + part[:, cols].astype(F32)).astype(BF)
        return carry

    lax.fori_loop(0, total.shape[1] // width, body, 0)


def split_rows(block, stage, width):
    def body(i, carry):
        cols = lanes_of(i * width, width)
        values = block[:, cols].astype(F32)
        for part in range(4):
            stage[part, :, cols] = values[24 * part : 24 * part + 24].astype(BF)
        return carry

    lax.fori_loop(0, block.shape[1] // width, body, 0)


def sum_parts(stage, total, width):
    def body(i, carry):
        cols = lanes_of(i * width, width)
        total[:, cols] = (
            stage[0, :, cols].astype(F32)
            + stage[1, :, cols].astype(F32)
            + stage[2, :, cols].astype(F32)
            + stage[3, :, cols].astype(F32)
        )
        return carry

    lax.fori_loop(0, total.shape[1] // width, body, 0)


def back_kernel(
    gr, gd, zn, qr, kr, vr, out, stats, dob, wp, aux, dh, xb, masks, gain_part,
    d_rows, mask_rows, sum_q, sum_r, sum_d, gain_sum,
    pr, pd, rr, rd, ry1, rx1, rx2, ry2, dy1, dx1, dx2, dy2, sp, rz, rzd,
    gq, rq, hq, ryq, rxq, fq, spq, rzq, d_first, fb, fc, back, gz, gh, kh, vh, dqkv, dk, dv, d_out,
    send_sem, recv_sem,
):
    y, x, c, z = position()
    quarter = 2 * x + c
    enter(y, x, c, z)
    net = Net(send_sem, recv_sem, None)
    sib, xdev, ydev = device(y, x, 1 - c, z), device(y, 1 - x, c, z), device(1 - y, x, c, z)
    peers = [(device(y, x, c, lax.rem(z + s, 4)), lax.rem(z + s, 4)) for s in (1, 3, 2)]
    group = group_of(y, x, c, z)
    own_rows = rows_of(quarter * ROWS, ROWS)

    got_do = net.land(4)

    def piece(q):
        return dob.at[:, lanes_of(384 * lax.div(q, 2) + 128 * lax.rem(q, 2), 256)]

    net.local(piece(quarter), d_out.at[own_rows], got_do + quarter)
    for to, q in group:
        net.send(piece(q), d_out.at[own_rows], to, got_do + quarter)

    def tok_of(b, core):
        return (b // 2) * 4 + (b % 2) * 2 + core

    def blk(t):
        return rows_of(t * 96, 96)

    def big(t):
        return rows_of(t * 384, 384)

    chunks = [(PATCH_AT, 1536), ("d", 0), ("d", 256), ("d", 512), (UP_AT, 1536), (UP_AT + 1536, 1536), (OUT_AT, 768)]
    count = len(chunks)
    own_in = [net.land(4) for _ in chunks]
    sib_in = [net.land(4) for _ in chunks]
    y_in = [net.land(3) for _ in chunks]
    x_in = [net.land(3) for _ in chunks]
    z_in = [net.land(4) for _ in chunks]

    def parts(k):
        at, size = chunks[k]
        if at == "d":
            return pl.ds(size, 256), pl.ds(size, 128), pl.ds(size + 128, 128), pl.ds(size // 2, 128), 128
        half = size // 2
        return pl.ds(at, size), pl.ds(at, half), pl.ds(at + half, half), pl.ds(at // 2, half), 384

    for k in range(count):
        both = parts(k)[0]
        for b in range(4):
            if chunks[k][0] == "d":
                net.send(gd.at[big(tok_of(b, 1 - c)), both], rd.at[b, :, both], sib, sib_in[k] + b)
                net.local(gd.at[big(tok_of(b, c)), both], pd.at[b, :, both], own_in[k] + b)
            else:
                net.send(gr.at[blk(tok_of(b, 1 - c)), both], rr.at[b, :, both], sib, sib_in[k] + b)
                net.local(gr.at[blk(tok_of(b, c)), both], pr.at[b, :, both], own_in[k] + b)

    def bufs(k):
        if chunks[k][0] == "d":
            return pd, rd, dy1, dx1, dx2, dy2
        return pr, rr, ry1, rx1, rx2, ry2

    def stage_core(k):
        def step():
            both, a, b2, h, width = parts(k)
            mine, new, y1, x1, x2, y2 = bufs(k)
            for b in range(4):
                net.wait(mine.at[b, :, both], own_in[k] + b)
                net.wait(new.at[b, :, both], sib_in[k] + b)
                add_into(mine.at[b, :, both], new.at[b, :, both], width)
            for side in range(2):
                net.send(mine.at[2 * (1 - y) + side, :, a], y1.at[side, :, h], ydev, y_in[k] + side)
                net.send(mine.at[2 * side + 1 - x, :, b2], x2.at[side, :, h], xdev, x_in[k] + side)

        return step

    def stage_one(k):
        def step():
            both, a, b2, h, width = parts(k)
            mine, new, y1, x1, x2, y2 = bufs(k)
            for side in range(2):
                net.wait(y1.at[side, :, h], y_in[k] + side)
                add_into(mine.at[2 * y + side, :, a], y1.at[side, :, h], width)
            net.send(mine.at[2 * y + 1 - x, :, a], x1.at[:, h], xdev, x_in[k] + 2)
            for side in range(2):
                net.wait(x2.at[side, :, h], x_in[k] + side)
                add_into(mine.at[2 * side + x, :, b2], x2.at[side, :, h], width)
            net.send(mine.at[2 * (1 - y) + x, :, b2], y2.at[:, h], ydev, y_in[k] + 2)

        return step

    def stage_two(k):
        def step():
            both, a, b2, h, width = parts(k)
            mine, new, y1, x1, x2, y2 = bufs(k)
            net.wait(x1.at[:, h], x_in[k] + 2)
            add_into(mine.at[2 * y + x, :, a], x1.at[:, h], width)
            net.wait(y2.at[:, h], y_in[k] + 2)
            add_into(mine.at[2 * y + x, :, b2], y2.at[:, h], width)
            if chunks[k][0] == "d":
                for peer, pz in peers:
                    net.send(
                        pd.at[2 * y + x, rows_of(96 * pz, 96), both], rzd.at[z, :, both], peer, z_in[k] + z
                    )
                net.local(pd.at[2 * y + x, rows_of(96 * z, 96), both], rzd.at[z, :, both], z_in[k] + z)
            else:
                split_rows(pr.at[2 * y + x, :, both], sp.at[:, :, both], 384)
                for peer, pz in peers:
                    net.send(sp.at[pz, :, both], rz.at[z, :, both], peer, z_in[k] + z)
                net.local(sp.at[z, :, both], rz.at[z, :, both], z_in[k] + z)

        return step

    def stage_sum(k):
        def step():
            both = parts(k)[0]
            if chunks[k][0] == "d":
                stage, total, width = rzd, sum_d, 256
            else:
                stage, total, width = rz, sum_r, 384
            for part in range(4):
                net.wait(stage.at[part, :, both], z_in[k] + part)
            sum_parts(stage.at[:, :, both], total.at[:, both], width)

        return step

    pump = Pump()
    for k in range(count + 3):
        if k < count:
            pump.add(stage_core(k))
        if 0 <= k - 1 < count:
            pump.add(stage_one(k - 1))
        if 0 <= k - 2 < count:
            pump.add(stage_two(k - 2))
        if 0 <= k - 3 < count:
            pump.add(stage_sum(k - 3))

    got_mask, got_back = net.land(), net.land()
    owner = device(y, lax.rem(z, 2), lax.div(z, 2), quarter)
    is_owner = (lax.rem(z, 2) == x) & (lax.div(z, 2) == c) & (quarter == z)
    net.send(masks, mask_rows, owner, got_mask, is_owner)
    gz_in = net.land(4)
    for peer, pz in peers:
        net.send(gain_part, gz.at[z], peer, gz_in + z)
    net.local(gain_part, gz.at[z], gz_in + z)
    gh_in = net.land(3)

    def gain_first():
        for part in range(4):
            net.wait(gz.at[part], gz_in + part)
        gain_sum[...] = gz[0] + gz[1] + gz[2] + gz[3]
        gh[0] = gain_sum[...]
        net.send(gh.at[0], gh.at[3], xdev, gh_in)

    def gain_next(i, to):
        net.wait(gh.at[2 + i], gh_in + i - 1)
        gain_sum[...] += gh[2 + i]
        if to is not None:
            gh[i] = gain_sum[...]
            net.send(gh.at[i], gh.at[3 + i], to, gh_in + i)

    lead_len, tail_len = aux[0:1, 0:1], aux[1:2, 0:1]
    key_col = lax.broadcasted_iota(jnp.int32, (SLOT_ROWS, 1), 0)
    key_seg, key_filler = segments(key_col, lead_len, tail_len)
    key_seg = jnp.where(key_seg < 0, -5, key_seg)
    masked = jnp.where(key_filler, -3e38, -1e30)
    for head in range(3):
        mine = own_lanes(c, head, (SLOT_ROWS, 256))
        cols = pl.ds(256 * head, 256)
        kh[:, cols] = jnp.where(mine, kr[...], 0.0).astype(BF)
        vh[:, cols] = jnp.where(mine, vr[...], 0.0).astype(BF)
    lane = lax.broadcasted_iota(jnp.int32, (8, 256), 1)
    row8 = lax.broadcasted_iota(jnp.int32, (8, 256), 0)
    picker = jnp.where((row8 < 3) & (lane // 64 - c == row8), 1.0, 0.0)
    for n, q in enumerate([quarter] + [q for _, q in group]):
        rows = rows_of(q * ROWS, ROWS)
        net.wait(d_out.at[rows], got_do + q)
        query, d_result = qr[rows, :], d_out[rows, :]
        stat = stats[rows, :].T
        product = d_result.astype(F32) * out[rows, :].astype(F32)
        delta = lax.dot_general(
            picker,
            product,
            (((1,), (1,)), ((), ())),
            precision=lax.Precision.HIGHEST,
            preferred_element_type=F32,
        )
        query_row = lax.broadcasted_iota(jnp.int32, (1, ROWS), 1) + q * ROWS
        query_seg = segments(query_row, lead_len, tail_len)[0]
        d_query = jnp.zeros((ROWS, 256), F32)
        for head in range(3):
            mine = own_lanes(c, head, (ROWS, 256))
            cols = pl.ds(256 * head, 256)
            key = kh[:, cols]
            allowed = key_seg == query_seg
            scores = jnp.where(allowed, nt(key, query), masked)
            probs = jnp.exp(scores - stat[head : head + 1, :])
            d_probs = nt(vh[:, cols], d_result)
            d_scores = jnp.where(allowed, probs * (d_probs - delta[head : head + 1, :]), 0.0)
            d_scores = d_scores.astype(BF)
            d_query = d_query + tn(d_scores, key)
            d_key = nn(d_scores, jnp.where(mine, query, 0.0).astype(BF))
            d_value = nn(probs.astype(BF), jnp.where(mine, d_result, 0.0).astype(BF))
            if n == 0 and head == 0:
                dk[...] = d_key
                dv[...] = d_value
            else:
                dk[...] += d_key
                dv[...] += d_value
            pump.run(2)
            if n == 0 and head == 2:
                gain_first()
            if n > 0 and head == 2:
                gain_next(n, (ydev, sib, None)[n - 1])
        dqkv[rows, 0:256] = (d_query * 0.125).astype(BF)
    dqkv[:, 256:512] = dk[...].astype(BF)
    dqkv[:, 512:768] = dv[...].astype(BF)

    fb_in, fc_in = net.land(2), net.land()
    flip = quarter + 1 - 2 * c
    cross = 2 - 4 * x

    def first(q):
        rows = rows_of(q * ROWS, ROWS)
        d_first[rows, :] = nt(dqkv[rows, :], wp[...]).astype(BF)
        return d_first.at[rows]

    net.send(first(flip + cross), fb.at[0], sib, fb_in)
    net.send(first(flip), fb.at[1], sib, fb_in + 1)
    far = first(quarter + cross)
    net.wait(fb.at[0], fb_in)
    add_into(far, fb.at[0], 256)
    net.send(far, fc, xdev, fc_in)
    near = first(quarter)

    qb_in = [net.land(4) for _ in range(3)]
    qy_in, qx_in, qz_in = net.land(6), net.land(3), [net.land(4) for _ in range(3)]
    first_core = c == 0

    def q_make(part):
        cols = pl.ds(256 * part, 256)
        gq[:, cols] = tn(zn[...], dqkv[:, cols]).astype(BF)
        for b in range(4):
            net.send(gq.at[blk(tok_of(b, 1 - c)), cols], rq.at[b, :, cols], sib, qb_in[part] + b)

    def q_core(part):
        cols = pl.ds(256 * part, 256)
        half = pl.ds(384 * part, 384)
        base = 384 * part
        for b in range(4):
            net.wait(rq.at[b, :, cols], qb_in[part] + b)
            own = gq[blk(tok_of(b, c)), cols].astype(F32)
            new = rq[b, :, cols].astype(F32)
            left, right = jnp.where(first_core, own, new), jnp.where(first_core, new, own)
            hq[b, :, base : base + 128] = left[:, 0:128].astype(BF)
            hq[b, :, base + 128 : base + 256] = (left[:, 128:256] + right[:, 0:128]).astype(BF)
            hq[b, :, base + 256 : base + 384] = right[:, 128:256].astype(BF)
        for side in range(2):
            net.send(
                hq.at[2 * (1 - y) + side, :, half], ryq.at[side, :, half], ydev, qy_in + 2 * part + side
            )

    def q_one(part):
        half = pl.ds(384 * part, 384)
        for side in range(2):
            net.wait(ryq.at[side, :, half], qy_in + 2 * part + side)
            add_into(hq.at[2 * y + side, :, half], ryq.at[side, :, half], 384)
        net.send(hq.at[2 * y + 1 - x, :, half], rxq.at[:, half], xdev, qx_in + part)

    def q_two(part):
        half = pl.ds(384 * part, 384)
        both = pl.ds(768 * part, 768)
        net.wait(rxq.at[:, half], qx_in + part)
        fq[:, lanes_of(768 * part + 384 * x, 384)] = hq[2 * y + x, :, half]
        fq[:, lanes_of(768 * part + 384 * (1 - x), 384)] = rxq[:, half]
        split_rows(fq.at[:, both], spq.at[:, :, both], 384)
        for peer, pz in peers:
            net.send(spq.at[pz, :, both], rzq.at[z, :, both], peer, qz_in[part] + z)
        net.local(spq.at[z, :, both], rzq.at[z, :, both], qz_in[part] + z)

    def q_sum(part):
        both = pl.ds(768 * part, 768)
        for src in range(4):
            net.wait(rzq.at[src, :, both], qz_in[part] + src)
        sum_parts(rzq.at[:, :, both], sum_q.at[:, both], 384)

    q_make(0)
    q_make(1)
    q_core(0)
    q_make(2)
    q_core(1)
    q_core(2)
    net.wait(fb.at[1], fb_in + 1)
    add_into(near, fb.at[1], 256)
    q_one(0)
    net.wait(fc, fc_in)
    d_zn = near[...].astype(F32) + fc[...].astype(F32)
    normed, scale = normalise(xb[...].astype(F32))
    d_x = dh[...] + scale * (
        d_zn
        - jnp.mean(d_zn, axis=-1, keepdims=True)
        - normed * jnp.mean(d_zn * normed, axis=-1, keepdims=True)
    )
    back[...] = d_x.astype(BF)
    net.send(back, d_rows, owner, got_back, is_owner)
    q_one(1)
    q_two(0)
    q_one(2)
    q_two(1)
    q_two(2)
    pump.run()
    for part in range(3):
        q_sum(part)
    net.wait(mask_rows, got_mask)
    net.wait(d_rows, got_back)
    net.finish()


VMEM_SPEC = pl.BlockSpec(memory_space=pltpu.VMEM)
ANY_SPEC = pl.BlockSpec(memory_space=pl.ANY)


def call(body, ident, specs, outs, scratch, sems, args, cost):
    out_shape = tuple(jax.ShapeDtypeStruct(shape, kind) for shape, kind, _ in outs)
    scratch_shapes = [pltpu.VMEM(shape, kind) for shape, kind in scratch]
    if sems:
        scratch_shapes += [pltpu.SemaphoreType.DMA((n,)) for n in sems]
    extra = {} if ident is None else dict(collective_id=ident, has_side_effects=True)
    return pl.pallas_call(
        body,
        out_shape=out_shape,
        in_specs=list(specs),
        out_specs=tuple(spec for _, _, spec in outs),
        scratch_shapes=scratch_shapes,
        compiler_params=pltpu.CompilerParams(vmem_limit_bytes=63 * 2**20, **extra),
        cost_estimate=pl.CostEstimate(flops=cost, bytes_accessed=2**24, transcendentals=0),
    )(*args)


def home_plan(
    patches,
    classes,
    slot_lengths,
    w_qkv,
    w_out,
    w_up,
    w_down,
    w_patch,
    w_class,
    norm1,
    norm2,
    mask_gain,
    d_masks,
):
    V, A = VMEM_SPEC, ANY_SPEC
    xin = jnp.concatenate([patches, jnp.pad(classes, ((0, CLS - REAL), (0, 0)))], axis=0)
    pad_cols = ((0, 0), (0, 0), (0, CLS - REAL))
    dmx = jnp.pad(d_masks.reshape(PATCH, 2, REAL), pad_cols).reshape(PATCH, 2 * CLS)
    dmx = jnp.pad(dmx, ((0, 0), (0, 256 - 2 * CLS))).astype(BF)
    gain = jnp.pad(mask_gain.reshape(1, 2, REAL), pad_cols).reshape(1, 2 * CLS)
    gain = jnp.pad(gain, ((0, 7), (0, 256 - 2 * CLS)))
    aux = jnp.broadcast_to(jnp.pad(slot_lengths.reshape(2, 1), ((0, 6), (0, 0))), (8, 128))
    g1, g2 = norm1.astype(F32)[:, None], norm2.astype(F32)[:, None]
    wqa = (w_qkv.astype(F32) * g1).astype(BF)
    wra = jnp.concatenate([w_out, (w_up.astype(F32) * g2).astype(BF), w_patch, w_class], axis=1)
    wide = wra.shape[1]
    slot, part = (SLOT_ROWS, 768), (SLOT_ROWS, 256)
    row_shape = (ROWS, 768)
    (
        gr, gd, dh, dob, masks, gain_part, zn, qr, kr, vr, out, stats, wp, xb, auxh
    ) = call(
        front_kernel,
        1,
        [V] * 7,
        [
            ((768, wide), BF, A),
            ((3072, 768), BF, A),
            (row_shape, F32, V),
            (row_shape, BF, V),
            ((PATCH, 256), BF, V),
            ((8, 256), F32, V),
            (slot, BF, A),
            (part, BF, A),
            (part, BF, A),
            (part, BF, A),
            (part, BF, A),
            ((SLOT_ROWS, 128), F32, A),
            ((768, 768), BF, A),
            (row_shape, BF, A),
            ((8, 128), jnp.int32, A),
        ],
        [
            (slot, BF),
            (slot, BF),
            (part, BF),
            (part, BF),
            (part, BF),
            (part, BF),
            ((SLOT_ROWS, 128), F32),
            ((768, 768), BF),
            ((768, 1152), BF),
            ((768, wide), BF),
            ((3072, 768), BF),
            ((4, 24, 2304), BF),
            ((4, 24, wide), BF),
            ((96, 2304), BF),
            (slot, BF),
            (slot, BF),
            ((768, wide), BF),
            ((3072, 768), BF),
            ((PATCH, 256), BF),
            ((8, 128), jnp.int32),
            ((4, ROWS, 256), BF),
            (row_shape, BF),
            ((768, ROWS), BF),
            (row_shape, BF),
            (row_shape, F32),
            (row_shape, F32),
            (row_shape, BF),
            ((PATCH, 768), F32),
            ((4 * CLS, 768), BF),
            ((4 * CLS, 768), BF),
            ((4, CLS, 768), BF),
            ((ROWS, 128), F32),
        ],
        (180, 240),
        (xin, dmx, aux, wqa, wra, w_down, gain),
        10**10,
    )
    half = wide // 2
    d_rows, mask_rows, sum_q, sum_r, sum_d, gain_sum = call(
        back_kernel,
        2,
        [A, A] + [V] * 11 + [A, V],
        [
            (row_shape, BF, A),
            ((PATCH, 256), BF, A),
            ((24, 2304), F32, V),
            ((24, wide), F32, V),
            ((96, 768), F32, V),
            ((8, 256), F32, V),
        ],
        [
            ((4, 96, wide), BF),
            ((4, 384, 768), BF),
            ((4, 96, wide), BF),
            ((4, 384, 768), BF),
            ((2, 96, half), BF),
            ((96, half), BF),
            ((2, 96, half), BF),
            ((96, half), BF),
            ((2, 384, 384), BF),
            ((384, 384), BF),
            ((2, 384, 384), BF),
            ((384, 384), BF),
            ((4, 24, wide), BF),
            ((4, 24, wide), BF),
            ((4, 96, 768), BF),
            ((768, 768), BF),
            ((4, 96, 768), BF),
            ((4, 96, 1152), BF),
            ((2, 96, 1152), BF),
            ((96, 1152), BF),
            ((96, 2304), BF),
            ((4, 24, 2304), BF),
            ((4, 24, 2304), BF),
            (slot, BF),
            ((2, ROWS, 768), BF),
            (row_shape, BF),
            (row_shape, BF),
            ((4, 8, 256), F32),
            ((6, 8, 256), F32),
            (slot, BF),
            (slot, BF),
            (slot, BF),
            (part, F32),
            (part, F32),
            (part, BF),
        ],
        (160, 220),
        (gr, gd, zn, qr, kr, vr, out, stats, dob, wp, auxh, dh, xb, masks, gain_part),
        10**10,
    )

    def unpad(values):
        return values[:, 0 : 2 * CLS].reshape(-1, 2, CLS)[:, :, 0:REAL].reshape(-1, 2 * REAL)

    d_rows = d_rows.astype(F32)
    sum_up = sum_r[:, UP_AT : UP_AT + 3072]
    return (
        unpad(mask_rows).astype(F32),
        d_rows[0:PATCH],
        d_rows[PATCH : PATCH + REAL],
        sum_q * g1,
        sum_r[:, OUT_AT : OUT_AT + 768],
        sum_up * g2,
        sum_d,
        sum_r[:, PATCH_AT : PATCH_AT + 768],
        sum_r[:, CLASS_AT : CLASS_AT + 768],
        jnp.sum(sum_q * w_qkv.astype(F32), axis=1),
        jnp.sum(sum_up * w_up.astype(F32), axis=1),
        unpad(gain_sum[0:1])[0],
    )


def solution(mesh):
    placed = (
        P(("tok", "head"), None),
        P(("tok", "head"), None),
        P("tok", None),
        P(("tok", "head"), None),
        P(("tok", "head"), None),
        P(("tok", "head"), None),
        P(("tok", "head"), None),
        P(("tok", "head"), None),
        P(("tok", "head"), None),
        P(("tok", "head")),
        P(("tok", "head")),
        P(),
        P(("tok", "head"), None),
    )
    fits = mesh.shape["tok"] == 8 and mesh.shape["head"] == 4
    return jax.shard_map(
        home_plan if fits else per_device,
        mesh=mesh,
        in_specs=placed,
        out_specs=(
            P(("tok", "head"), None),
            P(("tok", "head"), None),
            P(("tok", "head"), None),
            P(("tok", "head"), None),
            P(("tok", "head"), None),
            P(("tok", "head"), None),
            P(("tok", "head"), None),
            P(("tok", "head"), None),
            P(("tok", "head"), None),
            P(("tok", "head")),
            P(("tok", "head")),
            P(),
        ),
        check_vma=False,
    )
```

```python
import jax
import jax.numpy as jnp
from jax import lax
from jax.experimental import pallas as pl
from jax.experimental.pallas import tpu as pltpu
from jax.sharding import PartitionSpec as P

HEADS = 12
NCLS = 150


def layer_norm(values, gain):
    centre = values - jnp.mean(values, axis=-1, keepdims=True)
    spread = jnp.mean(centre * centre, axis=-1, keepdims=True)
    return centre * lax.rsqrt(spread + 1e-05) * gain


def unit_rows(values):
    return values * lax.rsqrt(jnp.sum(values * values, axis=-1, keepdims=True) + 1e-06)


def exact_gelu(values):
    return jax.nn.gelu(values, approximate=False)


def dot_plain(left, right):
    return jnp.dot(left, right, preferred_element_type=jnp.float32)


def dot_left_t(left, right):
    return lax.dot_general(
        left, right, (((0,), (0,)), ((), ())), preferred_element_type=jnp.float32
    )


def dot_right_t(left, right):
    return lax.dot_general(
        left, right, (((1,), (1,)), ((), ())), preferred_element_type=jnp.float32
    )


def flat_rows(matrix):
    return matrix.reshape(-1, 128)


def per_device(
    patches,
    classes,
    slot_lengths,
    w_qkv,
    w_out,
    w_up,
    w_down,
    w_patch,
    w_class,
    norm1,
    norm2,
    mask_gain,
    d_masks,
):
    tok_rows = patches.shape[0]
    cls_rows = classes.shape[0]
    all_rows = tok_rows + cls_rows
    width = patches.shape[1]
    groups = lax.axis_size("head")
    my_group = lax.axis_index("head")
    local_heads = HEADS // groups
    head_size = width // HEADS
    lead_len = slot_lengths[0, 0]
    tail_len = slot_lengths[0, 1]

    def segment_of(source, offset):
        place = source * tok_rows + offset
        patch_seg = jnp.where(place < lead_len, 0, jnp.where(place < lead_len + tail_len, 1, -1))
        class_seg = (source * cls_rows + offset - tok_rows) // NCLS
        return jnp.where(offset < tok_rows, patch_seg, class_seg)

    tok_seg = segment_of(my_group, jnp.arange(tok_rows))
    spread_rows = jnp.arange(groups * all_rows)
    head_seg = segment_of(spread_rows // all_rows, spread_rows % all_rows)
    allowed = (head_seg[:, None] == head_seg[None, :]) & (head_seg[None, :] >= 0)
    shards = (w_qkv, w_out, w_up, w_down, w_patch, w_class, norm1, norm2)
    gathered = (
        lax.all_gather(shards[0], ("tok", "head"), axis=0, tiled=True),
        lax.all_gather(shards[1], ("tok", "head"), axis=0, tiled=True),
        lax.all_gather(shards[2], ("tok", "head"), axis=0, tiled=True),
        lax.all_gather(shards[3], ("tok", "head"), axis=0, tiled=True),
        lax.all_gather(shards[4], ("tok", "head"), axis=0, tiled=True),
        lax.all_gather(shards[5], ("tok", "head"), axis=0, tiled=True),
        lax.all_gather(shards[6], ("tok", "head"), axis=0, tiled=True),
        lax.all_gather(shards[7], ("tok", "head"), axis=0, tiled=True),
    )
    full_qkv, full_out, full_up, full_down, full_patch, full_class, gain_one, gain_two = gathered
    stacked = jnp.concatenate([patches, classes], axis=0).astype(jnp.float32)
    first_in = layer_norm(stacked, gain_one.astype(jnp.float32)).astype(jnp.bfloat16)
    qkv_rows = (
        dot_plain(first_in, full_qkv)
        .astype(jnp.bfloat16)
        .reshape(all_rows, 3, groups, local_heads * head_size)
    )
    moved = lax.all_to_all(qkv_rows, "head", split_axis=2, concat_axis=0, tiled=True)
    moved = moved.reshape(groups * all_rows, 3, local_heads, head_size)
    queries = jnp.transpose(moved[:, 0], (1, 0, 2))
    key_rows = jnp.transpose(moved[:, 1], (1, 0, 2))
    value_rows = jnp.transpose(moved[:, 2], (1, 0, 2))

    def attend(parts):
        query, key_part, value_part = parts
        scores = jnp.where(allowed, dot_right_t(query, key_part) * 0.125, -1e30)
        top_score = jnp.max(scores, axis=1, keepdims=True)
        expo = jnp.exp(scores - top_score)
        total = jnp.sum(expo, axis=1, keepdims=True)
        probs = (expo / total).astype(jnp.bfloat16)
        result = dot_plain(probs, value_part).astype(jnp.bfloat16)
        return (result, top_score[:, 0] + jnp.log(total[:, 0]))

    head_out, log_total = lax.map(attend, (queries, key_rows, value_rows))
    sending = jnp.transpose(head_out, (1, 0, 2)).reshape(
        groups * all_rows, 1, local_heads * head_size
    )
    attended = lax.all_to_all(sending, "head", split_axis=0, concat_axis=1, tiled=True).reshape(
        all_rows, width
    )
    hidden = stacked + dot_plain(attended, full_out)
    second_in = layer_norm(hidden, gain_two.astype(jnp.float32)).astype(jnp.bfloat16)
    up_rows = dot_plain(second_in, full_up)
    gelu_rows = exact_gelu(up_rows).astype(jnp.bfloat16)
    after = (hidden + dot_plain(gelu_rows, full_down)).astype(jnp.bfloat16)
    patch_proj = dot_plain(after[:tok_rows], full_patch)
    class_proj = dot_plain(after[tok_rows:], full_class)
    patch_unit = unit_rows(patch_proj).astype(jnp.bfloat16)
    class_unit = unit_rows(class_proj).astype(jnp.bfloat16)
    slot_classes = lax.all_gather(class_unit, "head", axis=0, tiled=True)
    raw_both = dot_right_t(patch_unit, slot_classes)
    first_image = tok_seg[:, None] == 0
    raw = jnp.where(first_image, raw_both[:, :NCLS], raw_both[:, NCLS:])
    centre = raw - jnp.mean(raw, axis=1, keepdims=True)
    inv_sigma = lax.rsqrt(jnp.mean(centre * centre, axis=1, keepdims=True) + 1e-05)
    normed = centre * inv_sigma
    valid = (tok_seg >= 0).astype(jnp.float32)[:, None]
    masks = normed * mask_gain * valid
    regathered = (
        lax.all_gather(shards[0], ("tok", "head"), axis=0, tiled=True),
        lax.all_gather(shards[1], ("tok", "head"), axis=0, tiled=True),
        lax.all_gather(shards[2], ("tok", "head"), axis=0, tiled=True),
        lax.all_gather(shards[3], ("tok", "head"), axis=0, tiled=True),
        lax.all_gather(shards[4], ("tok", "head"), axis=0, tiled=True),
        lax.all_gather(shards[5], ("tok", "head"), axis=0, tiled=True),
        lax.all_gather(shards[6], ("tok", "head"), axis=0, tiled=True),
        lax.all_gather(shards[7], ("tok", "head"), axis=0, tiled=True),
    )
    back_qkv, back_out, back_up, back_down, back_patch, back_class, back_one, back_two = regathered
    mask_cot = d_masks * valid
    grad_mask = lax.psum(jnp.sum(mask_cot * normed, axis=0), ("tok", "head"))
    scaled = mask_cot * mask_gain
    d_raw = inv_sigma * (
        scaled
        - jnp.mean(scaled, axis=1, keepdims=True)
        - normed * jnp.mean(scaled * normed, axis=1, keepdims=True)
    )
    zero_part = jnp.zeros_like(d_raw)
    d_raw_both = jnp.concatenate(
        [jnp.where(first_image, d_raw, zero_part), jnp.where(first_image, zero_part, d_raw)], axis=1
    ).astype(jnp.bfloat16)
    d_patch_unit = dot_plain(d_raw_both, slot_classes)
    d_slot_classes = dot_left_t(d_raw_both, patch_unit)
    d_class_unit = lax.psum_scatter(
        d_slot_classes.astype(jnp.bfloat16), "head", scatter_dimension=0, tiled=True
    ).astype(jnp.float32)
    _, patch_pull = jax.vjp(unit_rows, patch_proj)
    d_patch_proj = patch_pull(d_patch_unit)[0].astype(jnp.bfloat16)
    _, class_pull = jax.vjp(unit_rows, class_proj)
    d_class_proj = class_pull(d_class_unit)[0].astype(jnp.bfloat16)
    grad_patch_w = dot_left_t(after[:tok_rows], d_patch_proj)
    grad_class_w = dot_left_t(after[tok_rows:], d_class_proj)
    d_after = jnp.concatenate(
        [dot_right_t(d_patch_proj, back_patch), dot_right_t(d_class_proj, back_class)], axis=0
    )
    d_after_low = d_after.astype(jnp.bfloat16)
    grad_down_w = dot_left_t(gelu_rows, d_after_low)
    d_gelu = dot_right_t(d_after_low, back_down)
    _, gelu_pull = jax.vjp(exact_gelu, up_rows)
    d_up_rows = gelu_pull(d_gelu)[0].astype(jnp.bfloat16)
    grad_up_w = dot_left_t(second_in, d_up_rows)
    d_second_in = dot_right_t(d_up_rows, back_up)
    _, norm_two_pull = jax.vjp(layer_norm, hidden, back_two.astype(jnp.float32))
    d_hidden_norm, grad_gain_two = norm_two_pull(d_second_in)
    d_hidden = d_after + d_hidden_norm
    d_hidden_low = d_hidden.astype(jnp.bfloat16)
    grad_out_w = dot_left_t(attended, d_hidden_low)
    d_attended = (
        dot_right_t(d_hidden_low, back_out)
        .astype(jnp.bfloat16)
        .reshape(all_rows, groups, local_heads * head_size)
    )
    d_head_out = lax.all_to_all(d_attended, "head", split_axis=1, concat_axis=0, tiled=True)
    d_head_out = jnp.transpose(
        d_head_out.reshape(groups * all_rows, local_heads, head_size), (1, 0, 2)
    )

    def attend_back(parts):
        query, key_part, value_part, log_row, d_result = parts
        scores = jnp.where(allowed, dot_right_t(query, key_part) * 0.125, -1e30)
        probs = jnp.exp(scores - log_row[:, None])
        d_probs = dot_right_t(d_result, value_part)
        inner = jnp.sum(probs * d_probs, axis=1, keepdims=True)
        d_scores = jnp.where(allowed, probs * (d_probs - inner), 0.0).astype(jnp.bfloat16)
        d_query = (dot_plain(d_scores, key_part) * 0.125).astype(jnp.bfloat16)
        d_key = (dot_left_t(d_scores, query) * 0.125).astype(jnp.bfloat16)
        d_value = dot_left_t(probs.astype(jnp.bfloat16), d_result).astype(jnp.bfloat16)
        return jnp.stack([d_query, d_key, d_value], axis=0)

    d_moved = lax.map(attend_back, (queries, key_rows, value_rows, log_total, d_head_out))
    d_moved = jnp.transpose(d_moved, (2, 1, 0, 3)).reshape(
        groups * all_rows, 3, 1, local_heads * head_size
    )
    d_qkv = lax.all_to_all(d_moved, "head", split_axis=0, concat_axis=2, tiled=True).reshape(
        all_rows, 3 * width
    )
    grad_qkv_w = dot_left_t(first_in, d_qkv)
    d_first_in = dot_right_t(d_qkv, back_qkv)
    _, norm_one_pull = jax.vjp(layer_norm, stacked, back_one.astype(jnp.float32))
    d_stacked_norm, grad_gain_one = norm_one_pull(d_first_in)
    d_stacked = d_hidden + d_stacked_norm
    every_sum = (
        lax.psum_scatter(flat_rows(grad_qkv_w), ("tok", "head"), scatter_dimension=0, tiled=True),
        lax.psum_scatter(flat_rows(grad_out_w), ("tok", "head"), scatter_dimension=0, tiled=True),
        lax.psum_scatter(flat_rows(grad_up_w), ("tok", "head"), scatter_dimension=0, tiled=True),
        lax.psum_scatter(flat_rows(grad_down_w), ("tok", "head"), scatter_dimension=0, tiled=True),
        lax.psum_scatter(flat_rows(grad_patch_w), ("tok", "head"), scatter_dimension=0, tiled=True),
        lax.psum_scatter(flat_rows(grad_class_w), ("tok", "head"), scatter_dimension=0, tiled=True),
        lax.psum_scatter(grad_gain_one, ("tok", "head"), scatter_dimension=0, tiled=True),
        lax.psum_scatter(grad_gain_two, ("tok", "head"), scatter_dimension=0, tiled=True),
    )
    sum_qkv, sum_out, sum_up, sum_down, sum_patch, sum_class, sum_one, sum_two = every_sum
    sum_qkv = sum_qkv.reshape(-1, 3 * width)
    sum_out = sum_out.reshape(-1, width)
    sum_up = sum_up.reshape(-1, grad_up_w.shape[1])
    sum_down = sum_down.reshape(-1, width)
    sum_patch = sum_patch.reshape(-1, width)
    sum_class = sum_class.reshape(-1, width)
    return (
        masks,
        d_stacked[:tok_rows],
        d_stacked[tok_rows:],
        sum_qkv,
        sum_out,
        sum_up,
        sum_down,
        sum_patch,
        sum_class,
        sum_one,
        sum_two,
        grad_mask,
    )


ROWS = 336
SLOT_ROWS = 4 * ROWS
PATCH = 256
CLS = 80
REAL = 75
PIECE = 80
LEAD = 16
MESH = pl.DeviceIdType.MESH
BF = jnp.bfloat16
F32 = jnp.float32


def position():
    tok = lax.axis_index("tok")
    return lax.div(tok, 4), lax.rem(lax.div(tok, 2), 2), lax.rem(tok, 2), lax.axis_index("head")


def device(y, x, c, z):
    return {"tok": y * 4 + x * 2 + c, "head": z}


def enter(y, x, c, z):
    barrier = pltpu.get_barrier_semaphore()
    others = [device(1 - y, x, c, z)]
    for turn in range(1, 16):
        flip_x, flip_c, step = turn // 8, (turn // 4) % 2, turn % 4
        others.append(
            device(
                y,
                1 - x if flip_x else x,
                1 - c if flip_c else c,
                lax.rem(z + step, 4),
            )
        )
    for other in others:
        pl.semaphore_signal(barrier, inc=1, device_id=other, device_id_type=MESH)
    pl.semaphore_wait(barrier, len(others))


class Net:
    def __init__(self, send_sem, recv_sem, here):
        self.send_sem, self.recv_sem, self.here = send_sem, recv_sem, here
        self.sends, self.recvs, self.open = 0, 0, []

    def land(self, count=1):
        first = self.recvs
        self.recvs += count
        return first

    def send(self, src, dst, to, slot, skip=None):
        index = self.sends
        self.sends += 1
        copy = pltpu.make_async_remote_copy(
            src_ref=src,
            dst_ref=dst,
            send_sem=self.send_sem.at[index],
            recv_sem=self.recv_sem.at[slot],
            device_id=to,
            device_id_type=MESH,
        )
        if skip is None:
            copy.start()
            self.open.append((copy, None))
        else:
            pl.when(jnp.logical_not(skip))(copy.start)
            self.open.append((copy, skip))

            @pl.when(skip)
            def _():
                pltpu.make_async_copy(src, dst, self.recv_sem.at[slot]).start()

    def local(self, src, dst, slot):
        pltpu.make_async_copy(src, dst, self.recv_sem.at[slot]).start()

    def wait(self, ref, slot):
        pltpu.make_async_copy(ref, ref, self.recv_sem.at[slot]).wait()

    def take(self, mark):
        taken, self.open = self.open[mark:], self.open[:mark]
        return taken

    def finish_some(self, taken):
        for copy, _ in taken:
            copy.wait_send()

    def finish(self):
        for copy, skip in self.open:
            if skip is None:
                copy.wait_send()
            else:
                pl.when(jnp.logical_not(skip))(copy.wait_send)
        self.open = []


def rows_of(start, size):
    return pl.ds(pl.multiple_of(start, 16), size)


def lanes_of(start, size):
    return pl.ds(pl.multiple_of(start, 128), size)


def nn(left, right):
    return jnp.dot(left, right, preferred_element_type=F32)


def nt(left, right):
    return lax.dot_general(left, right, (((1,), (1,)), ((), ())), preferred_element_type=F32)


def tn(left, right):
    return lax.dot_general(left, right, (((0,), (0,)), ((), ())), preferred_element_type=F32)


def segments(row, lead_len, tail_len):
    source = (
        (row >= ROWS).astype(jnp.int32)
        + (row >= 2 * ROWS).astype(jnp.int32)
        + (row >= 3 * ROWS).astype(jnp.int32)
    )
    offset = row - source * ROWS
    patch = source * PATCH + offset
    patch_seg = jnp.where(patch < lead_len, 0, jnp.where(patch < lead_len + tail_len, 1, -1))
    number = offset - PATCH
    class_seg = jnp.where(source >= 2, 1, 0)
    filler = number >= REAL
    seg = jnp.where(offset < PATCH, patch_seg, jnp.where(filler, -1, class_seg))
    return seg, filler


def normalise(values):
    centre = values - jnp.mean(values, axis=-1, keepdims=True)
    scale = lax.rsqrt(jnp.mean(centre * centre, axis=-1, keepdims=True) + 1e-05)
    return centre * scale, scale


def own_lanes(c, head, shape):
    lane = lax.broadcasted_iota(jnp.int32, shape, len(shape) - 1)
    group = lane // 64 - c
    if head is None:
        return (group >= 0) & (group < 3)
    return group == head


def group_of(y, x, c, z):
    near = [(x, 1 - c), (1 - x, c), (1 - x, 1 - c)]
    return [(device(y, a, b, z), 2 * a + b, 2 * b + a) for a, b in near]


def spread_matrix(kind, shape, lane_axis):
    packed = lax.broadcasted_iota(jnp.int32, shape, 1 - lane_axis)
    padded = lax.broadcasted_iota(jnp.int32, shape, lane_axis)
    return jnp.where(padded == packed + jnp.where(packed >= REAL, CLS - REAL, 0), 1.0, 0.0).astype(
        kind
    )


def exact(left, right, dims):
    return lax.dot_general(
        left,
        right,
        (dims, ((), ())),
        precision=lax.Precision.HIGHEST,
        preferred_element_type=F32,
    )


def column(row):
    size = row.shape[1]
    first = lax.broadcasted_iota(jnp.int32, (size, size), 0)
    second = lax.broadcasted_iota(jnp.int32, (size, size), 1)
    spread = jnp.where(first == second, jnp.broadcast_to(row[...].astype(F32), (size, size)), 0.0)
    return jnp.sum(spread, axis=1, keepdims=True)


TILE = 256
PANEL = 384


class Pump:
    def __init__(self):
        self.todo = []

    def add(self, step):
        self.todo.append(step)

    def run(self, count=None):
        count = len(self.todo) if count is None else min(count, len(self.todo))
        for step in self.todo[:count]:
            step()
        self.todo = self.todo[count:]


def join(stage, block, start, size, width):
    def body(i, carry):
        cols = lanes_of(start + i * width, width)
        parts = [stage[src, :, cols].astype(F32) for src in range(4)]
        block[:, cols] = jnp.concatenate(parts, axis=0).astype(BF)
        return carry

    lax.fori_loop(0, size // width, body, 0)


OUT_AT, UP_AT, PATCH_AT, CLASS_AT = 0, 768, 3840, 4608


def front_kernel(
    patches, classes, lens, w_qkv, w_out_in, w_up, wd_in, w_patch_in, w_class_in, g1, g2, gain_in,
    d_masks,
    dpc, z2, znt, h_f, inv, att, masks, gain_part,
    gl_o, slope_o, wr_o, wd_o, xs_o, qr_o, kr_o, vr_o, out_o, stats_o, wp_o, aux_o,
    xs, zn, qr, kr, vr, out, stats, wp, wq, wr, wd, stq, str_, bq, pool0, pool1,
    dmh, aux, cls_in, dmx, aux_in, wqa, wra, obuf, zn2, pp_f, cn, dcn, dcbuf,
    send_sem, recv_sem,
):
    y, x, c, z = position()
    tok = y * 4 + x * 2 + c
    quarter, block_id = 2 * x + c, 2 * c + x
    wra[:, UP_AT : UP_AT + 3072] = (w_up[...].astype(F32) * column(g2)).astype(BF)
    wqa[...] = (w_qkv[...].astype(F32) * column(g1)).astype(BF)
    cls_in[...] = jnp.zeros_like(cls_in)
    cls_in[0:REAL, :] = classes[...]
    pair = lens[...]
    aux_row = lax.broadcasted_iota(jnp.int32, (8, 128), 0)
    aux_in[...] = jnp.where(aux_row == 0, pair[0:1, 0:1], pair[0:1, 1:2])
    enter(y, x, c, z)
    net = Net(send_sem, recv_sem, None)
    sib, xdev, ydev = device(y, x, 1 - c, z), device(y, 1 - x, c, z), device(1 - y, x, c, z)
    flip = 1 - 2 * c
    t_x, t_y = tok + 2 - 4 * x, tok + 4 - 8 * y
    t_xy = t_x + 4 - 8 * y
    other = quarter + 2 - 4 * x
    peers = [device(y, x, c, lax.rem(z + step, 4)) for step in (1, 3, 2)]
    outs = []

    def store(src, dst):
        slot = net.land()
        net.local(src, dst, slot)
        outs.append((dst, slot))

    def blk(t):
        return rows_of(t * 96, 96)

    def big(t):
        return rows_of(t * 384, 384)

    q_cols = [pl.ds(768 * part, 768) for part in range(3)]
    got_q = [net.land(4) for _ in range(3)]
    chunks = [
        (UP_AT, 768, 0),
        (UP_AT + 768, 768, 0),
        (UP_AT + 1536, 1536, 0),
        (OUT_AT, 768, 1),
        ("d", 0, 1),
        ("d", 256, 1),
        ("d", 512, 1),
        (PATCH_AT, 1536, 1),
    ]
    got_z = [net.land(4) for _ in chunks]

    def raw_send(k):
        at, size, _ = chunks[k]
        if at == "d":
            cols = pl.ds(size, 256)
            src, dst = wd_in.at[:, cols], wd.at[rows_of((tok * 4 + z) * 96, 96), cols]
            pieces = [(src, dst)]
        elif at == OUT_AT:
            pieces = [(w_out_in, str_.at[z, :, pl.ds(at, 768)])]
        elif at == PATCH_AT:
            pieces = [
                (w_patch_in, str_.at[z, :, pl.ds(PATCH_AT, 768)]),
                (w_class_in, str_.at[z, :, pl.ds(CLASS_AT, 768)]),
            ]
        else:
            cols = pl.ds(at, size)
            pieces = [(wra.at[:, cols], str_.at[z, :, cols])]
        got = [got_z[k] + z] if len(pieces) == 1 else [got_z[k] + z, got_p + z]
        for (src, dst), slot in zip(pieces, got):
            net.local(src, dst, slot)
            for peer in peers:
                net.send(src, dst, peer, slot)

    got_p = net.land(4)
    raw_send(0)
    raw_send(1)
    raw_send(2)
    home = 2 * c + x
    got_lead, got_piece, got_cls = net.land(4), net.land(4), net.land(4)
    got_dm, got_aux = net.land(), net.land()
    for q in (3, 2, 1, 0):
        to = device(y, q // 2, q % 2, home)
        mine = (z == home) & (quarter == q)
        off = LEAD + PIECE * q
        if q == 3:
            src = cls_in
        else:
            src = patches.at[pl.ds(off, PIECE)]
        net.send(src, xs.at[rows_of(z * ROWS + off, PIECE)], to, got_piece + z, mine)
        net.send(
            patches.at[pl.ds(0, LEAD)], xs.at[rows_of(z * ROWS, LEAD)], to, got_lead + z, mine
        )
    to_home = device(y, lax.rem(z, 2), lax.div(z, 2), home)
    at_home = z == home
    net.send(aux_in, aux, to_home, got_aux, at_home)
    for part in range(3):
        net.local(wqa.at[:, q_cols[part]], stq.at[z, :, q_cols[part]], got_q[part] + z)
        for peer in peers:
            net.send(wqa.at[:, q_cols[part]], stq.at[z, :, q_cols[part]], peer, got_q[part] + z)
    for k in range(3, len(chunks)):
        raw_send(k)
    dmx[...] = tn(d_masks[...].astype(BF), spread_matrix(BF, (2 * REAL, 256), 1)).astype(BF)
    net.send(dmx, dmh, to_home, got_dm, at_home)

    sx, sy, ss = [], [], []
    for _ in chunks:
        sx.append(net.land(3))
        sy.append(net.land(3))
        ss.append(net.land(4))

    def parts(k):
        at, size = chunks[k][0:2]
        if at == "d":
            return wd, big, pl.ds(size, 128), pl.ds(size + 128, 128), pl.ds(size, 256)
        return wr, blk, pl.ds(at, size // 2), pl.ds(at + size // 2, size // 2), pl.ds(at, size)

    def pass_on(ref, to, slot):
        net.send(ref, ref, to, slot)

    def stage_z(k):
        def step():
            at, size, split = chunks[k]
            ref, rows, a, b, both = parts(k)
            for src in range(4):
                if at == "d":
                    net.wait(wd.at[rows_of((tok * 4 + src) * 96, 96), both], got_z[k] + src)
                elif at == PATCH_AT:
                    net.wait(str_.at[src, :, pl.ds(PATCH_AT, 768)], got_z[k] + src)
                    net.wait(str_.at[src, :, pl.ds(CLASS_AT, 768)], got_p + src)
                else:
                    net.wait(str_.at[src, :, both], got_z[k] + src)
            if at != "d":
                join(str_, wr.at[blk(tok)], at, size, 384)
            own = ref.at[rows(tok)]
            if split:
                pass_on(own.at[:, a], xdev, sx[k])
                pass_on(own.at[:, b], ydev, sy[k])
                pass_on(own.at[:, b], xdev, sx[k] + 1)
                pass_on(own.at[:, a], ydev, sy[k] + 1)
            else:
                pass_on(own.at[:, both], xdev, sx[k])
                pass_on(own.at[:, both], ydev, sy[k])
            pass_on(own.at[:, both], sib, ss[k])

        return step

    def stage_one(k):
        def step():
            ref, rows, a, b, both = parts(k)
            got_x, got_y = ref.at[rows(t_x)], ref.at[rows(t_y)]
            if chunks[k][2]:
                net.wait(got_x.at[:, a], sx[k])
                pass_on(got_x.at[:, a], ydev, sy[k] + 2)
                net.wait(got_y.at[:, b], sy[k])
                pass_on(got_y.at[:, b], xdev, sx[k] + 2)
            else:
                net.wait(got_x.at[:, both], sx[k])
                pass_on(got_x.at[:, both], ydev, sy[k] + 1)
                pass_on(got_x.at[:, both], sib, ss[k] + 1)

        return step

    def stage_two(k):
        def step():
            ref, rows, a, b, both = parts(k)
            got_x, got_y = ref.at[rows(t_x)], ref.at[rows(t_y)]
            if chunks[k][2]:
                net.wait(got_x.at[:, b], sx[k] + 1)
                pass_on(got_x.at[:, both], sib, ss[k] + 1)
                net.wait(got_y.at[:, a], sy[k] + 1)
            else:
                net.wait(got_y.at[:, both], sy[k])
            pass_on(got_y.at[:, both], sib, ss[k] + 2)

        return step

    def stage_three(k):
        def step():
            ref, rows, a, b, both = parts(k)
            got = ref.at[rows(t_xy)]
            if chunks[k][2]:
                net.wait(got.at[:, a], sy[k] + 2)
                net.wait(got.at[:, b], sx[k] + 2)
            else:
                net.wait(got.at[:, both], sy[k] + 1)
            pass_on(got.at[:, both], sib, ss[k] + 3)

        return step

    def ready(k):
        ref, rows, a, b, both = parts(k)
        for i, t in enumerate((tok, t_x, t_y, t_xy)):
            net.wait(ref.at[rows(t + flip), both], ss[k] + i)

    def piece(source, owner):
        return xs.at[rows_of(source * ROWS + LEAD + PIECE * owner, PIECE)]

    fwd_s, fwd_x, fwd_xs = net.land(4), net.land(4), net.land(4)
    near = [lax.rem(z + step, 4) for step in (0, 1, 3, 2)]

    def row_step(i):
        src = near[i]
        net.wait(piece(src, quarter), got_piece + src)
        net.send(piece(src, quarter), piece(src, quarter), xdev, fwd_x + src)
        net.send(piece(src, quarter), piece(src, quarter), sib, fwd_s + src)

    def row_cross(i):
        src = near[i]
        net.wait(piece(src, other), fwd_x + src)
        net.send(piece(src, other), piece(src, other), sib, fwd_xs + src)

    stage_z(0)()
    row_step(0)
    stage_z(1)()
    stage_one(0)()
    stage_z(2)()
    stage_two(0)()
    stage_one(1)()
    row_step(1)
    stage_three(0)()
    row_step(2)
    stage_two(1)()
    stage_one(2)()
    row_step(3)
    stage_three(1)()

    q_x, q_y, q_xy, q_s = net.land(3), net.land(3), net.land(3), net.land(12)

    def q_join(part):
        for src in range(4):
            net.wait(stq.at[src, :, q_cols[part]], got_q[part] + src)
        join(stq, bq, 768 * part, 768, 384)
        own = lanes_of(768 * part + 384 * x, 384)
        far = lanes_of(768 * part + 384 * (1 - x), 384)
        cols = pl.ds(384 * part, 384)
        net.send(bq.at[:, far], wq.at[blk(tok), cols], xdev, q_x + part)
        net.send(bq.at[:, own], wq.at[blk(tok), cols], ydev, q_y + part)
        wq[blk(tok), cols] = bq[:, own]
        net.send(bq.at[:, own], wq.at[blk(tok), cols], sib, q_s + part)

    def q_cross(part):
        cols = pl.ds(384 * part, 384)
        ref = wq.at[blk(t_x), cols]
        net.wait(ref, q_x + part)
        net.send(ref, ref, ydev, q_xy + part)
        net.send(ref, ref, sib, q_s + 3 + part)

    def q_last(part):
        cols = pl.ds(384 * part, 384)
        net.wait(wq.at[blk(t_y), cols], q_y + part)
        net.send(wq.at[blk(t_y), cols], wq.at[blk(t_y), cols], sib, q_s + 6 + part)
        net.wait(wq.at[blk(t_xy), cols], q_xy + part)
        net.send(wq.at[blk(t_xy), cols], wq.at[blk(t_xy), cols], sib, q_s + 9 + part)

    q_join(0)
    row_cross(0)
    row_cross(1)
    q_join(1)
    q_cross(0)
    row_cross(2)
    q_join(2)
    q_cross(1)
    row_cross(3)
    stage_two(2)()
    q_cross(2)
    sibling = quarter + flip
    for src in range(4):
        net.wait(xs.at[rows_of(src * ROWS, LEAD)], got_lead + src)
        net.wait(piece(src, sibling), fwd_s + src)
    stage_three(2)()
    stage_z(3)()
    for part in range(3):
        q_last(part)
    for src in range(4):
        net.wait(piece(src, sibling + 2 - 4 * x), fwd_xs + src)
    net.wait(aux, got_aux)

    def norm_step(i, carry):
        rows = rows_of(i * ROWS, ROWS)
        zn[rows, :] = normalise(xs[rows, :].astype(F32))[0].astype(BF)
        return carry

    lax.fori_loop(0, 4, norm_step, 0)
    count = len(chunks)
    pump = Pump()
    z_, o_, t_, h_ = stage_z, stage_one, stage_two, stage_three
    order = [z_(4), o_(3), z_(5), t_(3), o_(4), z_(6), h_(3), t_(4), o_(5), z_(7), h_(4), t_(5)]
    order += [o_(6), h_(5), t_(6), o_(7), t_(7), h_(6), h_(7)]
    for step in order:
        pump.add(step)
    pump.run(2)
    for part in range(3):
        cols = pl.ds(384 * part, 384)
        for i, t in enumerate((tok, t_x, t_y, t_xy)):
            net.wait(wq.at[blk(t + flip), cols], q_s + 3 * i + part)

    lead_len, tail_len = aux[0:1, 0:1], aux[1:2, 0:1]
    keep = own_lanes(c, None, (768, 256))
    for part in range(3):
        cols = lanes_of(384 * part + 128 * c, 256)
        wp[:, 256 * part : 256 * part + 256] = jnp.where(keep, wq[:, cols], 0.0).astype(BF)

    def project(i, carry):
        rows = rows_of(i * ROWS, ROWS)
        normed = zn[rows, :]
        qr[rows, :] = (nn(normed, wp[:, 0:256]).astype(BF) * 0.125).astype(BF)
        kr[rows, :] = nn(normed, wp[:, 256:512]).astype(BF)
        vr[rows, :] = nn(normed, wp[:, 512:768]).astype(BF)
        return carry

    lax.fori_loop(0, 4, project, 0)
    pump.run(1)
    for head in range(3):
        mine = own_lanes(c, head, (SLOT_ROWS, 256))
        cols = pl.ds(256 * head, 256)
        pool0[:, cols] = jnp.where(mine, kr[...], 0.0).astype(BF)
        pool1[:, cols] = jnp.where(mine, vr[...], 0.0).astype(BF)
    own_rows = rows_of(block_id * ROWS, ROWS)
    store(xs, xs_o)
    store(qr, qr_o)
    store(kr, kr_o)
    store(vr, vr_o)
    store(wp, wp_o)
    store(aux, aux_o)
    key_row = lax.broadcasted_iota(jnp.int32, (1, SLOT_ROWS), 1)
    key_seg, key_filler = segments(key_row, lead_len, tail_len)
    key_seg = jnp.where(key_seg < 0, -5, key_seg)
    masked = jnp.where(key_filler, -3e38, -1e30)
    group = group_of(y, x, c, z)
    got_o, got_cn, got_dc = net.land(4), net.land(4), net.land(4)
    lane = lax.broadcasted_iota(jnp.int32, (ROWS, 128), 1)
    for to, _, q in group[::-1] + [(None, quarter, block_id)]:
        rows = rows_of(q * ROWS, ROWS)
        row = lax.broadcasted_iota(jnp.int32, (ROWS, 1), 0) + q * ROWS
        seg = segments(row, lead_len, tail_len)[0]
        query = qr[rows, :]
        total_out = jnp.zeros((ROWS, 256), F32)
        kept = jnp.zeros((ROWS, 128), F32)
        for head in range(3):
            cols = pl.ds(256 * head, 256)
            scores = jnp.where(seg == key_seg, nt(query, pool0[:, cols]), masked)
            top = jnp.max(scores, axis=1, keepdims=True)
            expo = jnp.exp(scores - top)
            total = jnp.sum(expo, axis=1, keepdims=True)
            probs = (expo * (1.0 / total)).astype(BF)
            total_out = total_out + nn(probs, pool1[:, cols])
            kept = jnp.where(lane == head, top + jnp.log(total), kept)
            pump.run(1)
        out[rows, :] = total_out.astype(BF)
        stats[rows, :] = kept
        if to is None:
            net.local(out.at[rows], obuf.at[quarter], got_o + quarter)
        else:
            net.send(out.at[rows], obuf.at[quarter], to, got_o + quarter)
    store(out, out_o)
    store(stats, stats_o)

    row = lax.broadcasted_iota(jnp.int32, (PATCH, 1), 0) + block_id * ROWS
    seg = segments(row, lead_len, tail_len)[0]
    first_image = seg == 0
    valid = jnp.where(seg >= 0, 1.0, 0.0)
    for q in range(4):
        net.wait(obuf.at[q], got_o + q)
    for side in range(2):
        a, b = obuf[2 * side], obuf[2 * side + 1]
        base = 384 * side
        att[:, base : base + 128] = a[:, 0:128]
        att[:, base + 128 : base + 256] = a[:, 128:256] + b[:, 0:128]
        att[:, base + 256 : base + 384] = b[:, 128:256]
    ready(3)
    store(wr.at[:, pl.ds(OUT_AT, 768)], wr_o.at[:, pl.ds(OUT_AT, 768)])
    w_out = wr.at[:, pl.ds(OUT_AT, 768)]
    w_patch, w_class = wr.at[:, pl.ds(PATCH_AT, 768)], wr.at[:, pl.ds(CLASS_AT, 768)]
    h_f[...] = xs[own_rows, :].astype(F32) + nn(att[...], w_out[...])
    normed, scale = normalise(h_f[...])
    inv[...] = jnp.broadcast_to(scale, inv.shape)
    zn2[...] = normed.astype(BF)
    znt[...] = normed.T.astype(BF)
    for k in range(3):
        ready(k)
    store(wr.at[:, pl.ds(UP_AT, 3072)], wr_o.at[:, pl.ds(UP_AT, 3072)])
    gl, slope = pool0, pool1

    def panel(i):
        return rows_of(lax.div(i, 3) * ROWS, ROWS), lanes_of(lax.rem(i, 3) * TILE, TILE)

    def up_step(i, carry):
        u = nn(zn2[...], wr[:, lanes_of(UP_AT + i * TILE, TILE)])
        cdf = 0.5 * (1.0 + lax.erf(u * 0.7071067811865476))
        rows, cols = panel(i)
        gl[rows, cols] = (u * cdf).astype(BF)
        slope[rows, cols] = (cdf + u * (jnp.exp(-0.5 * u * u) * 0.3989422804014327)).astype(BF)
        return carry

    for turn in range(4):
        lax.fori_loop(3 * turn, 3 * turn + 3, up_step, 0)
        pump.run(1)
    pump.run()
    store(gl, gl_o)
    store(slope, slope_o)
    for k in range(4, 7):
        ready(k)
    store(wd, wd_o)
    mlp = nn(gl[0:ROWS, :], wd[0:768, :])
    for p in range(1, 4):
        mlp = mlp + nn(gl[ROWS * p : ROWS * p + ROWS, :], wd[768 * p : 768 * p + 768, :])
    z2[...] = (h_f[...] + mlp).astype(BF)
    z2p, z2c = z2[0:PATCH, :], z2[PATCH:ROWS, :]

    def unit(values):
        return values * lax.rsqrt(jnp.sum(values * values, axis=-1, keepdims=True) + 1e-06)

    def unit_back(values, cot):
        r = lax.rsqrt(jnp.sum(values * values, axis=-1, keepdims=True) + 1e-06)
        return r * cot - values * (r * r * r * jnp.sum(values * cot, axis=-1, keepdims=True))

    ready(7)
    store(wr.at[:, pl.ds(PATCH_AT, 1536)], wr_o.at[:, pl.ds(PATCH_AT, 1536)])
    cc = nn(z2c, w_class[...])
    own_cls = rows_of(block_id * CLS, CLS)
    cn[own_cls, :] = unit(cc).astype(BF)
    for to, _, q in group:
        net.send(cn.at[own_cls], cn.at[own_cls], to, got_cn + block_id)
    pp = nn(z2p, w_patch[...])
    pp_f[...] = pp
    pn = unit(pp).astype(BF)
    net.wait(dmh, got_dm)
    for _, _, q in group:
        net.wait(cn.at[rows_of(q * CLS, CLS)], got_cn + q)
    low, high = cn[0 : 2 * CLS, :], cn[2 * CLS : 4 * CLS, :]
    wide = 2 * CLS
    lane = lax.broadcasted_iota(jnp.int32, (1, wide), 1)
    real = jnp.where(lane >= CLS, lane - CLS, lane) < REAL
    gain = exact(gain_in[...], spread_matrix(F32, (2 * REAL, 2 * CLS), 1), ((1,), (0,)))
    raw = jnp.where(first_image, nt(pn, low), nt(pn, high))

    def mean(values):
        return jnp.sum(jnp.where(real, values, 0.0), axis=1, keepdims=True) * (0.5 / REAL)

    centre = jnp.where(real, raw - mean(raw), 0.0)
    sigma = lax.rsqrt(mean(centre * centre) + 1e-05)
    xhat = centre * sigma
    mask_gain = gain[0:1, :]
    dm = dmh[:, 0:wide].astype(F32) * valid
    dx = jnp.where(real, dm * mask_gain, 0.0)
    d_raw = jnp.where(real, sigma * (dx - mean(dx) - xhat * mean(dx * xhat)), 0.0)
    d_low = jnp.where(first_image, d_raw, 0.0).astype(BF)
    d_high = jnp.where(first_image, 0.0, d_raw).astype(BF)
    dcn[0:wide, :] = tn(d_low, pn).astype(BF)
    dcn[wide : 2 * wide, :] = tn(d_high, pn).astype(BF)
    for to, _, q in group:
        net.send(dcn.at[rows_of(q * CLS, CLS)], dcbuf.at[quarter], to, got_dc + quarter)
    net.local(dcn.at[own_cls], dcbuf.at[quarter], got_dc + quarter)
    masks[:, wide:256] = jnp.zeros((PATCH, 256 - wide), BF)
    masks[:, 0:wide] = (xhat * mask_gain * valid).astype(BF)
    gain_part[...] = jnp.zeros_like(gain_part)
    gain_part[0:1, 0:wide] = jnp.sum(dm * xhat, axis=0, keepdims=True)
    d_pn = nn(d_low, low) + nn(d_high, high)
    dpc[0:PATCH, :] = unit_back(pp_f[...], d_pn).astype(BF)
    for q in range(4):
        net.wait(dcbuf.at[q], got_dc + q)
    d_cn = dcbuf[0].astype(F32) + dcbuf[1].astype(F32) + dcbuf[2].astype(F32) + dcbuf[3].astype(F32)
    dpc[PATCH:ROWS, :] = unit_back(cc, d_cn).astype(BF)
    for dst, slot in outs:
        net.wait(dst, slot)
    net.finish()


def add_into(total, part, width):
    def body(i, carry):
        cols = lanes_of(i * width, width)
        total[:, cols] = (total[:, cols].astype(F32) + part[:, cols].astype(F32)).astype(BF)
        return carry

    lax.fori_loop(0, total.shape[1] // width, body, 0)


def split_rows(block, stage, width):
    def body(i, carry):
        cols = lanes_of(i * width, width)
        values = block[:, cols].astype(F32)
        for part in range(4):
            stage[part, :, cols] = values[24 * part : 24 * part + 24].astype(BF)
        return carry

    lax.fori_loop(0, block.shape[1] // width, body, 0)


def sum_parts(stage, total, width):
    def body(i, carry):
        cols = lanes_of(i * width, width)
        total[:, cols] = (
            stage[0, :, cols].astype(F32)
            + stage[1, :, cols].astype(F32)
            + stage[2, :, cols].astype(F32)
            + stage[3, :, cols].astype(F32)
        )
        return carry

    lax.fori_loop(0, total.shape[1] // width, body, 0)


def back_kernel(
    dpc, z2, znt, h_f, inv, att, masks, gain_part, gl_in, slope_in, wr, wd, xs_in,
    qr, kr, vr, out, stats, wp, aux,
    d_rows, mask_rows, sum_q, sum_r, sum_d, gain_sum,
    pool0, pool1, wpo, wds, wus, gr, gd, rr, rd, ra_r, rb_r, ra_d, rb_d, sp, rz, rzd,
    rq, ryq, rxq, spq, rzq, fb, fc, back, gz, gh, dk, dv, d_out, dz_f, dzb, dzn,
    send_sem, recv_sem,
):
    y, x, c, z = position()
    quarter, block_id = 2 * x + c, 2 * c + x
    net = Net(send_sem, recv_sem, None)
    got_gl, got_sl, got_wpo, got_xb = net.land(), net.land(), net.land(), net.land()
    got_wd, got_wu = net.land(8), net.land(8)
    own_rows = rows_of(block_id * ROWS, ROWS)
    own_wpo = wpo.at[:, pl.ds(768, 1536)]
    got_wo = net.land()
    net.local(wr.at[:, pl.ds(PATCH_AT, 1536)], own_wpo, got_wpo)
    net.local(gl_in, pool0, got_gl)
    net.local(slope_in, pool1, got_sl)

    def load(i):
        net.local(wd.at[pl.ds(PANEL * i, PANEL)], wds.at[i % 2], got_wd + i)
        net.local(wr.at[:, pl.ds(UP_AT + PANEL * i, PANEL)], wus.at[i % 2], got_wu + i)

    load(0)
    load(1)
    net.local(wr.at[:, pl.ds(OUT_AT, 768)], wpo.at[:, pl.ds(0, 768)], got_wo)
    net.local(xs_in.at[own_rows], back, got_xb)
    enter(y, x, c, z)
    sib, xdev, ydev = device(y, x, 1 - c, z), device(y, 1 - x, c, z), device(1 - y, x, c, z)
    peers = [(device(y, x, c, lax.rem(z + s, 4)), lax.rem(z + s, 4)) for s in (1, 3, 2)]
    group = group_of(y, x, c, z)

    def tok_of(b, core):
        return (b // 2) * 4 + (b % 2) * 2 + core

    def tok_of2(q, core):
        return lax.div(q, 2) * 4 + lax.rem(q, 2) * 2 + core

    def blk(t):
        return rows_of(t * 96, 96)

    def big(t):
        return rows_of(t * 384, 384)

    chunks = [
        (PATCH_AT, 1536, 1),
        (UP_AT, 1536, 1),
        (UP_AT + 1536, 1536, 1),
        ("d", 0, 1),
        ("d", 256, 0),
        ("d", 512, 1),
        (OUT_AT, 768, 0),
    ]
    count = len(chunks)
    sib_in = [net.land(4) for _ in chunks]
    a_in = [net.land(2) for _ in chunks]
    b_in = [net.land() for _ in chunks]
    z_in = [net.land(4) for _ in chunks]

    def parts(k):
        at, size, y_first = chunks[k]
        if at == "d":
            cols = pl.ds(size, 256)
            grad, rows, width = gd, big, 256
            views = [ref.at[:, :, cols] for ref in (rd, ra_d)] + [rb_d.at[:, cols]]
        else:
            cols = pl.ds(at, size)
            grad, rows, width = gr, blk, 384
            views = [ref.at[:, :, cols] for ref in (rr, ra_r)] + [rb_r.at[:, cols]]

        def mine(a, b):
            return grad.at[rows(a * 4 + b * 2 + c), cols]

        return cols, mine, views, width, y_first

    def core_send(k):
        at = chunks[k][0]
        cols, mine, (new, _, _), _, _ = parts(k)
        for b in range(4):
            t = tok_of(b, 1 - c)
            src = gd.at[big(t), cols] if at == "d" else gr.at[blk(t), cols]
            net.send(src, new.at[b], sib, sib_in[k] + b)

    def stage_core(k):
        def step():
            cols, mine, (new, ra, rb), width, y_first = parts(k)
            for b in range(4):
                net.wait(new.at[b], sib_in[k] + b)
                add_into(mine(b // 2, b % 2), new.at[b], width)
            for i in range(2):
                far, to = (mine(1 - y, i), ydev) if y_first else (mine(i, 1 - x), xdev)
                net.send(far, ra.at[i], to, a_in[k] + i)

        return step

    def stage_one(k):
        def step():
            cols, mine, (new, ra, rb), width, y_first = parts(k)
            for i in range(2):
                net.wait(ra.at[i], a_in[k] + i)
                add_into(mine(y, i) if y_first else mine(i, x), ra.at[i], width)
            last, to = (mine(y, 1 - x), xdev) if y_first else (mine(1 - y, x), ydev)
            net.send(last, rb, to, b_in[k])

        return step

    def stage_two(k):
        def step():
            cols, mine, (new, ra, rb), width, y_first = parts(k)
            net.wait(rb, b_in[k])
            add_into(mine(y, x), rb, width)
            if chunks[k][0] == "d":
                base = (y * 4 + x * 2 + c) * 384
                for peer, pz in peers:
                    net.send(
                        gd.at[rows_of(base + 96 * pz, 96), cols], rzd.at[z, :, cols], peer, z_in[k] + z
                    )
                net.local(gd.at[rows_of(base + 96 * z, 96), cols], rzd.at[z, :, cols], z_in[k] + z)
            else:
                split_rows(mine(y, x), sp.at[:, :, cols], width)
                for peer, pz in peers:
                    net.send(sp.at[pz, :, cols], rz.at[z, :, cols], peer, z_in[k] + z)
                net.local(sp.at[z, :, cols], rz.at[z, :, cols], z_in[k] + z)

        return step

    def stage_sum(k):
        def step():
            cols, _, _, width, _ = parts(k)
            if chunks[k][0] == "d":
                stage, total = rzd, sum_d
            else:
                stage, total = rz, sum_r
            for part in range(4):
                net.wait(stage.at[part, :, cols], z_in[k] + part)
            sum_parts(stage.at[:, :, cols], total.at[:, cols], width)

        return step

    pump = Pump()
    c_, o_, t_, s_ = stage_core, stage_one, stage_two, stage_sum
    order = [c_(0), c_(1), c_(2), c_(3), o_(0), c_(4), o_(1), c_(5), t_(0), o_(2), c_(6), t_(1), o_(3), t_(2)]
    order += [s_(0), o_(4), t_(3), s_(1), o_(5), t_(4), s_(2), o_(6), t_(5), s_(3), t_(6), s_(4), s_(5), s_(6)]
    for step in order:
        pump.add(step)

    got_mask, got_back = net.land(), net.land(2)
    owner = device(y, lax.rem(z, 2), lax.div(z, 2), block_id)
    is_owner = block_id == z
    net.send(masks, mask_rows, owner, got_mask, is_owner)
    gz_in = net.land(4)
    for peer, pz in peers:
        net.send(gain_part, gz.at[z], peer, gz_in + z)
    net.local(gain_part, gz.at[z], gz_in + z)
    gh_in = net.land(3)

    def gain_first():
        for part in range(4):
            net.wait(gz.at[part], gz_in + part)
        gain_sum[...] = gz[0] + gz[1] + gz[2] + gz[3]
        gh[0] = gain_sum[...]
        net.send(gh.at[0], gh.at[3], xdev, gh_in)

    def gain_next(i, to):
        net.wait(gh.at[2 + i], gh_in + i - 1)
        gain_sum[...] += gh[2 + i]
        if to is not None:
            gh[i] = gain_sum[...]
            net.send(gh.at[i], gh.at[3 + i], to, gh_in + i)

    net.wait(own_wpo, got_wpo)
    z2p, z2c = z2[0:PATCH, :], z2[PATCH:ROWS, :]
    d_pp, d_cc = dpc[0:PATCH, :], dpc[PATCH:ROWS, :]
    gr[:, PATCH_AT : PATCH_AT + 768] = tn(z2p, d_pp).astype(BF)
    gr[:, CLASS_AT : CLASS_AT + 768] = tn(z2c, d_cc).astype(BF)
    core_send(0)
    dz_f[0:PATCH, :] = nt(d_pp, wpo[:, 768:1536])
    dz_f[PATCH:ROWS, :] = nt(d_cc, wpo[:, 1536:2304])
    dzb[...] = dz_f[...].astype(BF)
    net.wait(pool0, got_gl)
    net.wait(pool1, got_sl)
    for i in range(8):
        net.wait(wds.at[i % 2], got_wd + i)
        net.wait(wus.at[i % 2], got_wu + i)
        rows = pl.ds(ROWS * (i // 2), ROWS)
        cols = pl.ds(PANEL * (i % 2), PANEL)
        d_u = (nt(dzb[...], wds[i % 2]) * pool1[rows, cols].astype(F32)).astype(BF)
        gd[PANEL * i : PANEL * i + PANEL, :] = tn(pool0[rows, cols], dzb[...]).astype(BF)
        gr[:, UP_AT + PANEL * i : UP_AT + PANEL * i + PANEL] = nn(znt[...], d_u).astype(BF)
        part = nt(d_u, wus[i % 2])
        if i == 0:
            dzn[...] = part
        else:
            dzn[...] += part
        if i + 2 < 8:
            load(i + 2)
        if i == 3:
            core_send(1)
            pump.run(1)
        if i == 7:
            core_send(2)
            pump.run(1)
    mark = len(net.open)
    for k in (3, 4, 5):
        core_send(k)
    dsent = net.take(mark)
    d_zn = dzn[...]
    normed = h_f[...]
    normed = (normed - jnp.mean(normed, axis=-1, keepdims=True)) * inv[:, 0:1]
    d_h = dz_f[...] + inv[:, 0:1] * (
        d_zn
        - jnp.mean(d_zn, axis=-1, keepdims=True)
        - normed * jnp.mean(d_zn * normed, axis=-1, keepdims=True)
    )
    dz_f[...] = d_h
    d_hb = d_h.astype(BF)
    net.wait(wpo.at[:, pl.ds(0, 768)], got_wo)
    dob, dh = dzb, dz_f
    dob[...] = nt(d_hb, wpo[:, 0:768]).astype(BF)

    got_do = net.land(4)

    def piece(q):
        return dob.at[:, lanes_of(384 * lax.div(q, 2) + 128 * lax.rem(q, 2), 256)]

    net.local(piece(quarter), d_out.at[own_rows], got_do + block_id)
    for to, q, _ in group:
        net.send(piece(q), d_out.at[own_rows], to, got_do + block_id)
    gr[:, OUT_AT : OUT_AT + 768] = tn(att[...], d_hb).astype(BF)
    core_send(6)
    kh, vh = pool0, pool1

    lead_len, tail_len = aux[0:1, 0:1], aux[1:2, 0:1]
    key_col = lax.broadcasted_iota(jnp.int32, (SLOT_ROWS, 1), 0)
    key_seg, key_filler = segments(key_col, lead_len, tail_len)
    key_seg = jnp.where(key_seg < 0, -5, key_seg)
    masked = jnp.where(key_filler, -3e38, -1e30)
    def dqkv(q):
        return gd.at[rows_of(384 * tok_of2(q, 1 - c), ROWS)]

    for head in range(3):
        mine = own_lanes(c, head, (SLOT_ROWS, 256))
        cols = pl.ds(256 * head, 256)
        kh[:, cols] = jnp.where(mine, kr[...], 0.0).astype(BF)
        vh[:, cols] = jnp.where(mine, vr[...], 0.0).astype(BF)
    lane = lax.broadcasted_iota(jnp.int32, (8, 256), 1)
    row8 = lax.broadcasted_iota(jnp.int32, (8, 256), 0)
    picker = jnp.where((row8 < 3) & (lane // 64 - c == row8), 1.0, 0.0)
    for n, q in enumerate([block_id] + [q for _, _, q in group]):
        rows = rows_of(q * ROWS, ROWS)
        net.wait(d_out.at[rows], got_do + q)
        query, d_result = qr[rows, :], d_out[rows, :]
        stat = stats[rows, :].T
        product = d_result.astype(F32) * out[rows, :].astype(F32)
        delta = lax.dot_general(
            picker,
            product,
            (((1,), (1,)), ((), ())),
            precision=lax.Precision.HIGHEST,
            preferred_element_type=F32,
        )
        query_row = lax.broadcasted_iota(jnp.int32, (1, ROWS), 1) + q * ROWS
        query_seg = segments(query_row, lead_len, tail_len)[0]
        d_query = jnp.zeros((ROWS, 256), F32)
        for head in range(3):
            mine = own_lanes(c, head, (ROWS, 256))
            cols = pl.ds(256 * head, 256)
            own_query = jnp.where(mine, query, 0.0).astype(BF)
            own_result = jnp.where(mine, d_result, 0.0).astype(BF)
            for side in range(2):
                low, high = side * SLOT_ROWS // 2, (side + 1) * SLOT_ROWS // 2
                keys = pl.ds(low, SLOT_ROWS // 2)
                key = kh[keys, cols]
                allowed = key_seg[low:high] == query_seg
                scores = jnp.where(allowed, nt(key, query), masked[low:high])
                probs = jnp.exp(scores - stat[head : head + 1, :])
                d_probs = nt(vh[keys, cols], d_result)
                d_scores = jnp.where(allowed, probs * (d_probs - delta[head : head + 1, :]), 0.0)
                d_scores = d_scores.astype(BF)
                d_query = d_query + tn(d_scores, key)
                d_key = nn(d_scores, own_query)
                d_value = nn(probs.astype(BF), own_result)
                if n == 0 and head == 0:
                    dk[keys, :] = d_key
                    dv[keys, :] = d_value
                else:
                    dk[keys, :] += d_key
                    dv[keys, :] += d_value
            pump.run(2)
            if n == 0 and head == 2:
                gain_first()
            if n > 0 and head == 2:
                gain_next(n, (ydev, sib, None)[n - 1])
        if n == 0:
            net.finish_some(dsent)
        dqkv(q)[:, 0:256] = (d_query * 0.125).astype(BF)
    for q in range(4):
        rows = pl.ds(ROWS * q, ROWS)
        dqkv(q)[:, 256:512] = dk[rows, :].astype(BF)
        dqkv(q)[:, 512:768] = dv[rows, :].astype(BF)
    got_xs = net.land()
    net.local(xs_in, pool1, got_xs)

    fb_in, fc_in = net.land(2), net.land(2)
    halves = (pl.ds(0, 176), pl.ds(176, 160))
    (_, _, sib_q), (_, _, cross_q), (_, _, diag_q) = group

    def first(q):
        rows = rows_of(q * ROWS, ROWS)
        pool0[rows, :] = nt(dqkv(q)[...], wp[...]).astype(BF)
        return pool0.at[rows]

    net.send(first(diag_q), fb.at[0], sib, fb_in)
    net.send(first(sib_q), fb.at[1], sib, fb_in + 1)
    far = first(cross_q)
    net.wait(fb.at[0], fb_in)
    for i, part in enumerate(halves):
        add_into(far.at[part], fb.at[0, part], 256)
        net.send(far.at[part], fc.at[part], xdev, fc_in + i)
    near = first(block_id)

    qb_in = [net.land(4) for _ in range(3)]
    qy_in, qx_in, qz_in = net.land(6), net.land(3), [net.land(4) for _ in range(3)]
    first_core = c == 0

    gq = wpo.at[:, pl.ds(0, 768)]

    def hq(b):
        return wpo.at[rows_of(96 * b, 96), pl.ds(768, 1152)]

    def fq(part):
        return wds.at[0, pl.ds(96 * part, 96)]

    def q_make(part):
        cols = pl.ds(256 * part, 256)
        total = tn(pool1[0:ROWS, :], dqkv(0)[:, cols])
        for q in range(1, 4):
            total = total + tn(pool1[ROWS * q : ROWS * q + ROWS, :], dqkv(q)[:, cols])
        gq[:, cols] = total.astype(BF)
        for b in range(4):
            net.send(gq.at[blk(tok_of(b, 1 - c)), cols], rq.at[b, :, cols], sib, qb_in[part] + b)

    def q_core(part):
        cols = pl.ds(256 * part, 256)
        half = pl.ds(384 * part, 384)
        base = 384 * part
        for b in range(4):
            net.wait(rq.at[b, :, cols], qb_in[part] + b)
            own = gq[blk(tok_of(b, c)), cols].astype(F32)
            new = rq[b, :, cols].astype(F32)
            left, right = jnp.where(first_core, own, new), jnp.where(first_core, new, own)
            hq(b)[:, base : base + 128] = left[:, 0:128].astype(BF)
            hq(b)[:, base + 128 : base + 256] = (left[:, 128:256] + right[:, 0:128]).astype(BF)
            hq(b)[:, base + 256 : base + 384] = right[:, 128:256].astype(BF)
        for side in range(2):
            net.send(
                hq(2 * (1 - y) + side).at[:, half], ryq.at[side, :, half], ydev, qy_in + 2 * part + side
            )

    def q_one(part):
        half = pl.ds(384 * part, 384)
        for side in range(2):
            net.wait(ryq.at[side, :, half], qy_in + 2 * part + side)
            add_into(hq(2 * y + side).at[:, half], ryq.at[side, :, half], 384)
        net.send(hq(2 * y + 1 - x).at[:, half], rxq.at[:, half], xdev, qx_in + part)

    def q_two(part):
        half = pl.ds(384 * part, 384)
        both = pl.ds(768 * part, 768)
        net.wait(rxq.at[:, half], qx_in + part)
        fq(part)[:, lanes_of(384 * x, 384)] = hq(2 * y + x)[:, half]
        fq(part)[:, lanes_of(384 * (1 - x), 384)] = rxq[:, half]
        split_rows(fq(part), spq.at[:, :, both], 384)
        for peer, pz in peers:
            net.send(spq.at[pz, :, both], rzq.at[z, :, both], peer, qz_in[part] + z)
        net.local(spq.at[z, :, both], rzq.at[z, :, both], qz_in[part] + z)

    def q_sum(part):
        both = pl.ds(768 * part, 768)
        for src in range(4):
            net.wait(rzq.at[src, :, both], qz_in[part] + src)
        sum_parts(rzq.at[:, :, both], sum_q.at[:, both], 384)

    def finish_rows(i):
        part = halves[i]
        net.wait(fc.at[part], fc_in + i)
        d_zn = near[part, :].astype(F32) + fc[part, :].astype(F32)
        normed, scale = normalise(back[part, :].astype(F32))
        d_x = dh[part, :] + scale * (
            d_zn
            - jnp.mean(d_zn, axis=-1, keepdims=True)
            - normed * jnp.mean(d_zn * normed, axis=-1, keepdims=True)
        )
        back[part, :] = d_x.astype(BF)
        net.send(back.at[part], d_rows.at[part], owner, got_back + i, is_owner)

    net.wait(pool1, got_xs)

    def norm_step(i, carry):
        rows = rows_of(i * ROWS, ROWS)
        pool1[rows, :] = normalise(pool1[rows, :].astype(F32))[0].astype(BF)
        return carry

    lax.fori_loop(0, 4, norm_step, 0)
    q_make(0)
    q_make(1)
    q_core(0)
    q_make(2)
    q_core(1)
    q_core(2)
    net.wait(back, got_xb)
    net.wait(fb.at[1], fb_in + 1)
    add_into(near, fb.at[1], 256)
    pump.run(1)
    finish_rows(0)
    q_one(0)
    finish_rows(1)
    q_one(1)
    q_one(2)
    pump.run(2)
    q_two(0)
    q_two(1)
    q_two(2)
    pump.run()
    for part in range(3):
        q_sum(part)
    net.wait(mask_rows, got_mask)
    for i, part in enumerate(halves):
        net.wait(d_rows.at[part], got_back + i)
    net.finish()


def last_kernel(
    d_rows, mask_rows, sum_q, sum_r, sum_d, gain_sum, w_qkv, w_up, g1, g2,
    masks, d_patches, d_classes, d_qkv, d_out, d_up, d_down, d_patch, d_class, d_one, d_two, d_gain,
):
    masks[...] = nt(spread_matrix(BF, (2 * REAL, 256), 1), mask_rows[...])
    d_patches[...] = d_rows[0:PATCH, :].astype(F32)
    d_classes[...] = d_rows[PATCH : PATCH + REAL, :].astype(F32)
    total = sum_q[...]
    d_qkv[...] = total * column(g1)
    ones = jnp.ones((8, total.shape[1]), F32)
    d_one[...] = exact(ones, total * w_qkv[...].astype(F32), ((1,), (1,)))[0:1, :]
    total = sum_r[:, UP_AT : UP_AT + 3072]
    d_up[...] = total * column(g2)
    ones = jnp.ones((8, total.shape[1]), F32)
    d_two[...] = exact(ones, total * w_up[...].astype(F32), ((1,), (1,)))[0:1, :]
    d_out[...] = sum_r[:, OUT_AT : OUT_AT + 768]
    d_down[...] = sum_d[...]
    d_patch[...] = sum_r[:, PATCH_AT : PATCH_AT + 768]
    d_class[...] = sum_r[:, CLASS_AT : CLASS_AT + 768]
    d_gain[...] = exact(gain_sum[...], spread_matrix(F32, (256, 2 * REAL), 0), ((1,), (0,)))[0:1, :]


VMEM_SPEC = pl.BlockSpec(memory_space=pltpu.VMEM)
ANY_SPEC = pl.BlockSpec(memory_space=pl.ANY)


def call(body, ident, specs, outs, scratch, sems, args, cost):
    out_shape = tuple(jax.ShapeDtypeStruct(shape, kind) for shape, kind, _ in outs)
    scratch_shapes = [pltpu.VMEM(shape, kind) for shape, kind in scratch]
    if sems:
        scratch_shapes += [pltpu.SemaphoreType.DMA((n,)) for n in sems]
    extra = {} if ident is None else dict(collective_id=ident, has_side_effects=True)
    return pl.pallas_call(
        body,
        out_shape=out_shape,
        in_specs=list(specs),
        out_specs=tuple(spec for _, _, spec in outs),
        scratch_shapes=scratch_shapes,
        compiler_params=pltpu.CompilerParams(vmem_limit_bytes=63 * 2**20, **extra),
        cost_estimate=pl.CostEstimate(flops=cost, bytes_accessed=2**24, transcendentals=0),
    )(*args)


def home_plan(
    patches,
    classes,
    slot_lengths,
    w_qkv,
    w_out,
    w_up,
    w_down,
    w_patch,
    w_class,
    norm1,
    norm2,
    mask_gain,
    d_masks,
):
    V, A = VMEM_SPEC, ANY_SPEC
    wide = 3 * w_out.shape[1] + w_up.shape[1]
    rows = w_qkv.shape[0]
    g1, g2 = norm1.reshape(1, rows), norm2.reshape(1, rows)
    slot, part = (SLOT_ROWS, 768), (SLOT_ROWS, 256)
    row_shape = (ROWS, 768)
    kept = call(
        front_kernel,
        1,
        [V] * 13,
        [
            (row_shape, BF, V),
            (row_shape, BF, V),
            ((768, ROWS), BF, V),
            (row_shape, F32, V),
            ((ROWS, 128), F32, V),
            (row_shape, BF, V),
            ((PATCH, 256), BF, V),
            ((8, 256), F32, V),
            (slot, BF, A),
            (slot, BF, A),
            ((768, wide), BF, A),
            ((3072, 768), BF, A),
            (slot, BF, A),
            (part, BF, A),
            (part, BF, A),
            (part, BF, A),
            (part, BF, A),
            ((SLOT_ROWS, 128), F32, A),
            ((768, 768), BF, A),
            ((8, 128), jnp.int32, A),
        ],
        [
            (slot, BF),
            (slot, BF),
            (part, BF),
            (part, BF),
            (part, BF),
            (part, BF),
            ((SLOT_ROWS, 128), F32),
            ((768, 768), BF),
            ((768, 1152), BF),
            ((768, wide), BF),
            ((3072, 768), BF),
            ((4, 24, 2304), BF),
            ((4, 24, wide), BF),
            ((96, 2304), BF),
            (slot, BF),
            (slot, BF),
            ((PATCH, 256), BF),
            ((8, 128), jnp.int32),
            ((CLS, 768), BF),
            ((PATCH, 256), BF),
            ((8, 128), jnp.int32),
            ((24, 2304), BF),
            ((24, wide), BF),
            ((4, ROWS, 256), BF),
            (row_shape, BF),
            ((PATCH, 768), F32),
            ((4 * CLS, 768), BF),
            ((4 * CLS, 768), BF),
            ((4, CLS, 768), BF),
        ],
        (200, 260),
        (
            patches,
            classes,
            slot_lengths,
            w_qkv,
            w_out,
            w_up,
            w_down,
            w_patch,
            w_class,
            g1,
            g2,
            mask_gain.reshape(1, -1),
            d_masks.T,
        ),
        10**10,
    )
    d_rows, mask_rows, sum_q, sum_r, sum_d, gain_sum = call(
        back_kernel,
        2,
        [V] * 6 + [A, V] + [A] * 5 + [V] * 7,
        [
            (row_shape, BF, A),
            ((PATCH, 256), BF, A),
            ((24, 2304), F32, V),
            ((24, wide), F32, V),
            ((96, 768), F32, V),
            ((8, 256), F32, V),
        ],
        [
            (slot, BF),
            (slot, BF),
            ((768, 2304), BF),
            ((2, PANEL, 768), BF),
            ((2, 768, PANEL), BF),
            ((768, wide), BF),
            ((3072, 768), BF),
            ((4, 96, wide), BF),
            ((4, 384, 768), BF),
            ((2, 96, wide), BF),
            ((96, wide), BF),
            ((2, 384, 768), BF),
            ((384, 768), BF),
            ((4, 24, wide), BF),
            ((4, 24, wide), BF),
            ((4, 96, 768), BF),
            ((4, 96, 768), BF),
            ((2, 96, 1152), BF),
            ((96, 1152), BF),
            ((4, 24, 2304), BF),
            ((4, 24, 2304), BF),
            ((2, ROWS, 768), BF),
            (row_shape, BF),
            (row_shape, BF),
            ((4, 8, 256), F32),
            ((6, 8, 256), F32),
            (part, F32),
            (part, F32),
            (part, BF),
            (row_shape, F32),
            (row_shape, BF),
            (row_shape, F32),
        ],
        (160, 240),
        kept,
        10**10,
    )
    square = ((rows, 768), F32, V)
    masks, d_patches, d_classes, d_qkv, d_w_out, d_up, d_down, d_patch, d_class, d_one, d_two, d_gain = call(
        last_kernel,
        None,
        [V] * 10,
        [
            (d_masks.shape[::-1], F32, V),
            (patches.shape, F32, V),
            (classes.shape, F32, V),
            (w_qkv.shape, F32, V),
            square,
            (w_up.shape, F32, V),
            (w_down.shape, F32, V),
            square,
            square,
            ((1, rows), F32, V),
            ((1, rows), F32, V),
            ((1, 2 * REAL), F32, V),
        ],
        [],
        (),
        (d_rows, mask_rows, sum_q, sum_r, sum_d, gain_sum, w_qkv, w_up, g1, g2),
        10**7,
    )
    return (
        masks.T,
        d_patches,
        d_classes,
        d_qkv,
        d_w_out,
        d_up,
        d_down,
        d_patch,
        d_class,
        d_one.reshape(-1),
        d_two.reshape(-1),
        d_gain.reshape(-1),
    )


def solution(mesh):
    placed = (
        P(("tok", "head"), None),
        P(("tok", "head"), None),
        P("tok", None),
        P(("tok", "head"), None),
        P(("tok", "head"), None),
        P(("tok", "head"), None),
        P(("tok", "head"), None),
        P(("tok", "head"), None),
        P(("tok", "head"), None),
        P(("tok", "head")),
        P(("tok", "head")),
        P(),
        P(("tok", "head"), None),
    )
    fits = mesh.shape["tok"] == 8 and mesh.shape["head"] == 4
    return jax.shard_map(
        home_plan if fits else per_device,
        mesh=mesh,
        in_specs=placed,
        out_specs=(
            P(("tok", "head"), None),
            P(("tok", "head"), None),
            P(("tok", "head"), None),
            P(("tok", "head"), None),
            P(("tok", "head"), None),
            P(("tok", "head"), None),
            P(("tok", "head"), None),
            P(("tok", "head"), None),
            P(("tok", "head"), None),
            P(("tok", "head")),
            P(("tok", "head")),
            P(),
        ),
        check_vma=False,
    )
```

```python
import jax
import jax.numpy as jnp
from jax import lax
from jax.experimental import pallas as pl
from jax.experimental.pallas import tpu as pltpu
from jax.sharding import PartitionSpec as P

HEADS = 12
NCLS = 150


def layer_norm(values, gain):
    centre = values - jnp.mean(values, axis=-1, keepdims=True)
    spread = jnp.mean(centre * centre, axis=-1, keepdims=True)
    return centre * lax.rsqrt(spread + 1e-05) * gain


def unit_rows(values):
    return values * lax.rsqrt(jnp.sum(values * values, axis=-1, keepdims=True) + 1e-06)


def exact_gelu(values):
    return jax.nn.gelu(values, approximate=False)


def dot_plain(left, right):
    return jnp.dot(left, right, preferred_element_type=jnp.float32)


def dot_left_t(left, right):
    return lax.dot_general(
        left, right, (((0,), (0,)), ((), ())), preferred_element_type=jnp.float32
    )


def dot_right_t(left, right):
    return lax.dot_general(
        left, right, (((1,), (1,)), ((), ())), preferred_element_type=jnp.float32
    )


def flat_rows(matrix):
    return matrix.reshape(-1, 128)


def per_device(
    patches,
    classes,
    slot_lengths,
    w_qkv,
    w_out,
    w_up,
    w_down,
    w_patch,
    w_class,
    norm1,
    norm2,
    mask_gain,
    d_masks,
):
    tok_rows = patches.shape[0]
    cls_rows = classes.shape[0]
    all_rows = tok_rows + cls_rows
    width = patches.shape[1]
    groups = lax.axis_size("head")
    my_group = lax.axis_index("head")
    local_heads = HEADS // groups
    head_size = width // HEADS
    lead_len = slot_lengths[0, 0]
    tail_len = slot_lengths[0, 1]

    def segment_of(source, offset):
        place = source * tok_rows + offset
        patch_seg = jnp.where(place < lead_len, 0, jnp.where(place < lead_len + tail_len, 1, -1))
        class_seg = (source * cls_rows + offset - tok_rows) // NCLS
        return jnp.where(offset < tok_rows, patch_seg, class_seg)

    tok_seg = segment_of(my_group, jnp.arange(tok_rows))
    spread_rows = jnp.arange(groups * all_rows)
    head_seg = segment_of(spread_rows // all_rows, spread_rows % all_rows)
    allowed = (head_seg[:, None] == head_seg[None, :]) & (head_seg[None, :] >= 0)
    shards = (w_qkv, w_out, w_up, w_down, w_patch, w_class, norm1, norm2)
    gathered = (
        lax.all_gather(shards[0], ("tok", "head"), axis=0, tiled=True),
        lax.all_gather(shards[1], ("tok", "head"), axis=0, tiled=True),
        lax.all_gather(shards[2], ("tok", "head"), axis=0, tiled=True),
        lax.all_gather(shards[3], ("tok", "head"), axis=0, tiled=True),
        lax.all_gather(shards[4], ("tok", "head"), axis=0, tiled=True),
        lax.all_gather(shards[5], ("tok", "head"), axis=0, tiled=True),
        lax.all_gather(shards[6], ("tok", "head"), axis=0, tiled=True),
        lax.all_gather(shards[7], ("tok", "head"), axis=0, tiled=True),
    )
    full_qkv, full_out, full_up, full_down, full_patch, full_class, gain_one, gain_two = gathered
    stacked = jnp.concatenate([patches, classes], axis=0).astype(jnp.float32)
    first_in = layer_norm(stacked, gain_one.astype(jnp.float32)).astype(jnp.bfloat16)
    qkv_rows = (
        dot_plain(first_in, full_qkv)
        .astype(jnp.bfloat16)
        .reshape(all_rows, 3, groups, local_heads * head_size)
    )
    moved = lax.all_to_all(qkv_rows, "head", split_axis=2, concat_axis=0, tiled=True)
    moved = moved.reshape(groups * all_rows, 3, local_heads, head_size)
    queries = jnp.transpose(moved[:, 0], (1, 0, 2))
    key_rows = jnp.transpose(moved[:, 1], (1, 0, 2))
    value_rows = jnp.transpose(moved[:, 2], (1, 0, 2))

    def attend(parts):
        query, key_part, value_part = parts
        scores = jnp.where(allowed, dot_right_t(query, key_part) * 0.125, -1e30)
        top_score = jnp.max(scores, axis=1, keepdims=True)
        expo = jnp.exp(scores - top_score)
        total = jnp.sum(expo, axis=1, keepdims=True)
        probs = (expo / total).astype(jnp.bfloat16)
        result = dot_plain(probs, value_part).astype(jnp.bfloat16)
        return (result, top_score[:, 0] + jnp.log(total[:, 0]))

    head_out, log_total = lax.map(attend, (queries, key_rows, value_rows))
    sending = jnp.transpose(head_out, (1, 0, 2)).reshape(
        groups * all_rows, 1, local_heads * head_size
    )
    attended = lax.all_to_all(sending, "head", split_axis=0, concat_axis=1, tiled=True).reshape(
        all_rows, width
    )
    hidden = stacked + dot_plain(attended, full_out)
    second_in = layer_norm(hidden, gain_two.astype(jnp.float32)).astype(jnp.bfloat16)
    up_rows = dot_plain(second_in, full_up)
    gelu_rows = exact_gelu(up_rows).astype(jnp.bfloat16)
    after = (hidden + dot_plain(gelu_rows, full_down)).astype(jnp.bfloat16)
    patch_proj = dot_plain(after[:tok_rows], full_patch)
    class_proj = dot_plain(after[tok_rows:], full_class)
    patch_unit = unit_rows(patch_proj).astype(jnp.bfloat16)
    class_unit = unit_rows(class_proj).astype(jnp.bfloat16)
    slot_classes = lax.all_gather(class_unit, "head", axis=0, tiled=True)
    raw_both = dot_right_t(patch_unit, slot_classes)
    first_image = tok_seg[:, None] == 0
    raw = jnp.where(first_image, raw_both[:, :NCLS], raw_both[:, NCLS:])
    centre = raw - jnp.mean(raw, axis=1, keepdims=True)
    inv_sigma = lax.rsqrt(jnp.mean(centre * centre, axis=1, keepdims=True) + 1e-05)
    normed = centre * inv_sigma
    valid = (tok_seg >= 0).astype(jnp.float32)[:, None]
    masks = normed * mask_gain * valid
    regathered = (
        lax.all_gather(shards[0], ("tok", "head"), axis=0, tiled=True),
        lax.all_gather(shards[1], ("tok", "head"), axis=0, tiled=True),
        lax.all_gather(shards[2], ("tok", "head"), axis=0, tiled=True),
        lax.all_gather(shards[3], ("tok", "head"), axis=0, tiled=True),
        lax.all_gather(shards[4], ("tok", "head"), axis=0, tiled=True),
        lax.all_gather(shards[5], ("tok", "head"), axis=0, tiled=True),
        lax.all_gather(shards[6], ("tok", "head"), axis=0, tiled=True),
        lax.all_gather(shards[7], ("tok", "head"), axis=0, tiled=True),
    )
    back_qkv, back_out, back_up, back_down, back_patch, back_class, back_one, back_two = regathered
    mask_cot = d_masks * valid
    grad_mask = lax.psum(jnp.sum(mask_cot * normed, axis=0), ("tok", "head"))
    scaled = mask_cot * mask_gain
    d_raw = inv_sigma * (
        scaled
        - jnp.mean(scaled, axis=1, keepdims=True)
        - normed * jnp.mean(scaled * normed, axis=1, keepdims=True)
    )
    zero_part = jnp.zeros_like(d_raw)
    d_raw_both = jnp.concatenate(
        [jnp.where(first_image, d_raw, zero_part), jnp.where(first_image, zero_part, d_raw)], axis=1
    ).astype(jnp.bfloat16)
    d_patch_unit = dot_plain(d_raw_both, slot_classes)
    d_slot_classes = dot_left_t(d_raw_both, patch_unit)
    d_class_unit = lax.psum_scatter(
        d_slot_classes.astype(jnp.bfloat16), "head", scatter_dimension=0, tiled=True
    ).astype(jnp.float32)
    _, patch_pull = jax.vjp(unit_rows, patch_proj)
    d_patch_proj = patch_pull(d_patch_unit)[0].astype(jnp.bfloat16)
    _, class_pull = jax.vjp(unit_rows, class_proj)
    d_class_proj = class_pull(d_class_unit)[0].astype(jnp.bfloat16)
    grad_patch_w = dot_left_t(after[:tok_rows], d_patch_proj)
    grad_class_w = dot_left_t(after[tok_rows:], d_class_proj)
    d_after = jnp.concatenate(
        [dot_right_t(d_patch_proj, back_patch), dot_right_t(d_class_proj, back_class)], axis=0
    )
    d_after_low = d_after.astype(jnp.bfloat16)
    grad_down_w = dot_left_t(gelu_rows, d_after_low)
    d_gelu = dot_right_t(d_after_low, back_down)
    _, gelu_pull = jax.vjp(exact_gelu, up_rows)
    d_up_rows = gelu_pull(d_gelu)[0].astype(jnp.bfloat16)
    grad_up_w = dot_left_t(second_in, d_up_rows)
    d_second_in = dot_right_t(d_up_rows, back_up)
    _, norm_two_pull = jax.vjp(layer_norm, hidden, back_two.astype(jnp.float32))
    d_hidden_norm, grad_gain_two = norm_two_pull(d_second_in)
    d_hidden = d_after + d_hidden_norm
    d_hidden_low = d_hidden.astype(jnp.bfloat16)
    grad_out_w = dot_left_t(attended, d_hidden_low)
    d_attended = (
        dot_right_t(d_hidden_low, back_out)
        .astype(jnp.bfloat16)
        .reshape(all_rows, groups, local_heads * head_size)
    )
    d_head_out = lax.all_to_all(d_attended, "head", split_axis=1, concat_axis=0, tiled=True)
    d_head_out = jnp.transpose(
        d_head_out.reshape(groups * all_rows, local_heads, head_size), (1, 0, 2)
    )

    def attend_back(parts):
        query, key_part, value_part, log_row, d_result = parts
        scores = jnp.where(allowed, dot_right_t(query, key_part) * 0.125, -1e30)
        probs = jnp.exp(scores - log_row[:, None])
        d_probs = dot_right_t(d_result, value_part)
        inner = jnp.sum(probs * d_probs, axis=1, keepdims=True)
        d_scores = jnp.where(allowed, probs * (d_probs - inner), 0.0).astype(jnp.bfloat16)
        d_query = (dot_plain(d_scores, key_part) * 0.125).astype(jnp.bfloat16)
        d_key = (dot_left_t(d_scores, query) * 0.125).astype(jnp.bfloat16)
        d_value = dot_left_t(probs.astype(jnp.bfloat16), d_result).astype(jnp.bfloat16)
        return jnp.stack([d_query, d_key, d_value], axis=0)

    d_moved = lax.map(attend_back, (queries, key_rows, value_rows, log_total, d_head_out))
    d_moved = jnp.transpose(d_moved, (2, 1, 0, 3)).reshape(
        groups * all_rows, 3, 1, local_heads * head_size
    )
    d_qkv = lax.all_to_all(d_moved, "head", split_axis=0, concat_axis=2, tiled=True).reshape(
        all_rows, 3 * width
    )
    grad_qkv_w = dot_left_t(first_in, d_qkv)
    d_first_in = dot_right_t(d_qkv, back_qkv)
    _, norm_one_pull = jax.vjp(layer_norm, stacked, back_one.astype(jnp.float32))
    d_stacked_norm, grad_gain_one = norm_one_pull(d_first_in)
    d_stacked = d_hidden + d_stacked_norm
    every_sum = (
        lax.psum_scatter(flat_rows(grad_qkv_w), ("tok", "head"), scatter_dimension=0, tiled=True),
        lax.psum_scatter(flat_rows(grad_out_w), ("tok", "head"), scatter_dimension=0, tiled=True),
        lax.psum_scatter(flat_rows(grad_up_w), ("tok", "head"), scatter_dimension=0, tiled=True),
        lax.psum_scatter(flat_rows(grad_down_w), ("tok", "head"), scatter_dimension=0, tiled=True),
        lax.psum_scatter(flat_rows(grad_patch_w), ("tok", "head"), scatter_dimension=0, tiled=True),
        lax.psum_scatter(flat_rows(grad_class_w), ("tok", "head"), scatter_dimension=0, tiled=True),
        lax.psum_scatter(grad_gain_one, ("tok", "head"), scatter_dimension=0, tiled=True),
        lax.psum_scatter(grad_gain_two, ("tok", "head"), scatter_dimension=0, tiled=True),
    )
    sum_qkv, sum_out, sum_up, sum_down, sum_patch, sum_class, sum_one, sum_two = every_sum
    sum_qkv = sum_qkv.reshape(-1, 3 * width)
    sum_out = sum_out.reshape(-1, width)
    sum_up = sum_up.reshape(-1, grad_up_w.shape[1])
    sum_down = sum_down.reshape(-1, width)
    sum_patch = sum_patch.reshape(-1, width)
    sum_class = sum_class.reshape(-1, width)
    return (
        masks,
        d_stacked[:tok_rows],
        d_stacked[tok_rows:],
        sum_qkv,
        sum_out,
        sum_up,
        sum_down,
        sum_patch,
        sum_class,
        sum_one,
        sum_two,
        grad_mask,
    )


ROWS = 336
SLOT_ROWS = 4 * ROWS
PATCH = 256
CLS = 80
REAL = 75
PIECE = 80
LEAD = 16
MESH = pl.DeviceIdType.MESH
BF = jnp.bfloat16
F32 = jnp.float32


def position():
    tok = lax.axis_index("tok")
    return lax.div(tok, 4), lax.rem(lax.div(tok, 2), 2), lax.rem(tok, 2), lax.axis_index("head")


def device(y, x, c, z):
    return {"tok": y * 4 + x * 2 + c, "head": z}


def enter(y, x, c, z):
    barrier = pltpu.get_barrier_semaphore()
    others = [device(1 - y, x, c, z)]
    for turn in range(1, 16):
        flip_x, flip_c, step = turn // 8, (turn // 4) % 2, turn % 4
        others.append(
            device(
                y,
                1 - x if flip_x else x,
                1 - c if flip_c else c,
                lax.rem(z + step, 4),
            )
        )
    for other in others:
        pl.semaphore_signal(barrier, inc=1, device_id=other, device_id_type=MESH)
    pl.semaphore_wait(barrier, len(others))


class Net:
    def __init__(self, send_sem, recv_sem, here):
        self.send_sem, self.recv_sem, self.here = send_sem, recv_sem, here
        self.sends, self.recvs, self.open = 0, 0, []

    def land(self, count=1):
        first = self.recvs
        self.recvs += count
        return first

    def send(self, src, dst, to, slot, skip=None):
        index = self.sends
        self.sends += 1
        copy = pltpu.make_async_remote_copy(
            src_ref=src,
            dst_ref=dst,
            send_sem=self.send_sem.at[index],
            recv_sem=self.recv_sem.at[slot],
            device_id=to,
            device_id_type=MESH,
        )
        if skip is None:
            copy.start()
            self.open.append((copy, None))
        else:
            pl.when(jnp.logical_not(skip))(copy.start)
            self.open.append((copy, skip))

            @pl.when(skip)
            def _():
                pltpu.make_async_copy(src, dst, self.recv_sem.at[slot]).start()

    def local(self, src, dst, slot):
        pltpu.make_async_copy(src, dst, self.recv_sem.at[slot]).start()

    def wait(self, ref, slot):
        pltpu.make_async_copy(ref, ref, self.recv_sem.at[slot]).wait()

    def take(self, mark):
        taken, self.open = self.open[mark:], self.open[:mark]
        return taken

    def finish_some(self, taken):
        for copy, _ in taken:
            copy.wait_send()

    def finish(self):
        for copy, skip in self.open:
            if skip is None:
                copy.wait_send()
            else:
                pl.when(jnp.logical_not(skip))(copy.wait_send)
        self.open = []


def rows_of(start, size):
    return pl.ds(pl.multiple_of(start, 16), size)


def lanes_of(start, size):
    return pl.ds(pl.multiple_of(start, 128), size)


def nn(left, right):
    return jnp.dot(left, right, preferred_element_type=F32)


def nt(left, right):
    return lax.dot_general(left, right, (((1,), (1,)), ((), ())), preferred_element_type=F32)


def tn(left, right):
    return lax.dot_general(left, right, (((0,), (0,)), ((), ())), preferred_element_type=F32)


def segments(row, lead_len, tail_len):
    source = (
        (row >= ROWS).astype(jnp.int32)
        + (row >= 2 * ROWS).astype(jnp.int32)
        + (row >= 3 * ROWS).astype(jnp.int32)
    )
    offset = row - source * ROWS
    patch = source * PATCH + offset
    patch_seg = jnp.where(patch < lead_len, 0, jnp.where(patch < lead_len + tail_len, 1, -1))
    number = offset - PATCH
    class_seg = jnp.where(source >= 2, 1, 0)
    filler = number >= REAL
    seg = jnp.where(offset < PATCH, patch_seg, jnp.where(filler, -1, class_seg))
    return seg, filler


def normalise(values):
    centre = values - jnp.mean(values, axis=-1, keepdims=True)
    scale = lax.rsqrt(jnp.mean(centre * centre, axis=-1, keepdims=True) + 1e-05)
    return centre * scale, scale


def own_lanes(c, head, shape):
    lane = lax.broadcasted_iota(jnp.int32, shape, len(shape) - 1)
    group = lane // 64 - c
    if head is None:
        return (group >= 0) & (group < 3)
    return group == head


def group_of(y, x, c, z):
    near = [(x, 1 - c), (1 - x, c), (1 - x, 1 - c)]
    return [(device(y, a, b, z), 2 * a + b, 2 * b + a) for a, b in near]


def spread_matrix(kind, shape, lane_axis):
    packed = lax.broadcasted_iota(jnp.int32, shape, 1 - lane_axis)
    padded = lax.broadcasted_iota(jnp.int32, shape, lane_axis)
    return jnp.where(padded == packed + jnp.where(packed >= REAL, CLS - REAL, 0), 1.0, 0.0).astype(
        kind
    )


def exact(left, right, dims):
    return lax.dot_general(
        left,
        right,
        (dims, ((), ())),
        precision=lax.Precision.HIGHEST,
        preferred_element_type=F32,
    )


def column(row):
    size = row.shape[1]
    first = lax.broadcasted_iota(jnp.int32, (size, size), 0)
    second = lax.broadcasted_iota(jnp.int32, (size, size), 1)
    spread = jnp.where(first == second, jnp.broadcast_to(row[...].astype(F32), (size, size)), 0.0)
    return jnp.sum(spread, axis=1, keepdims=True)


TILE = 256
PANEL = 384


class Pump:
    def __init__(self):
        self.todo = []

    def add(self, step):
        self.todo.append(step)

    def run(self, count=None):
        count = len(self.todo) if count is None else min(count, len(self.todo))
        for step in self.todo[:count]:
            step()
        self.todo = self.todo[count:]


def join(stage, block, start, size, width):
    def body(i, carry):
        cols = lanes_of(start + i * width, width)
        parts = [stage[src, :, cols].astype(F32) for src in range(4)]
        block[:, cols] = jnp.concatenate(parts, axis=0).astype(BF)
        return carry

    lax.fori_loop(0, size // width, body, 0)


OUT_AT, UP_AT, PATCH_AT, CLASS_AT = 0, 768, 3840, 4608


def front_kernel(
    patches, classes, lens, w_qkv, w_out_in, w_up, wd_in, w_patch_in, w_class_in, g1, g2, gain_in,
    d_masks,
    dpc, z2, znt, h_f, inv, att, masks, gain_part,
    gl_o, slope_o, wr_o, wd_o, xs_o, qr_o, kr_o, vr_o, out_o, stats_o, wp_o, aux_o,
    xs, zn, qr, kr, vr, out, stats, wp, wq, wr, wd, stq, str_, bq, pool0, pool1,
    dmh, aux, cls_in, dmx, aux_in, wqa, wra, obuf, zn2, pp_f, cn, dcn, dcbuf,
    send_sem, recv_sem,
):
    y, x, c, z = position()
    tok = y * 4 + x * 2 + c
    quarter, block_id = 2 * x + c, 2 * c + x
    wra[:, UP_AT : UP_AT + 3072] = (w_up[...].astype(F32) * column(g2)).astype(BF)
    wqa[...] = (w_qkv[...].astype(F32) * column(g1)).astype(BF)
    cls_in[...] = jnp.zeros_like(cls_in)
    cls_in[0:REAL, :] = classes[...]
    pair = lens[...]
    aux_row = lax.broadcasted_iota(jnp.int32, (8, 128), 0)
    aux_in[...] = jnp.where(aux_row == 0, pair[0:1, 0:1], pair[0:1, 1:2])
    enter(y, x, c, z)
    net = Net(send_sem, recv_sem, None)
    sib, xdev, ydev = device(y, x, 1 - c, z), device(y, 1 - x, c, z), device(1 - y, x, c, z)
    flip = 1 - 2 * c
    t_x, t_y = tok + 2 - 4 * x, tok + 4 - 8 * y
    t_xy = t_x + 4 - 8 * y
    other = quarter + 2 - 4 * x
    peers = [device(y, x, c, lax.rem(z + step, 4)) for step in (1, 3, 2)]
    outs = []

    def store(src, dst):
        slot = net.land()
        net.local(src, dst, slot)
        outs.append((dst, slot))

    def blk(t):
        return rows_of(t * 96, 96)

    def big(t):
        return rows_of(t * 384, 384)

    q_cols = [pl.ds(768 * part, 768) for part in range(3)]
    got_q = [net.land(4) for _ in range(3)]
    chunks = [
        (UP_AT, 768, 0),
        (UP_AT + 768, 768, 0),
        (UP_AT + 1536, 1536, 0),
        (OUT_AT, 768, 1),
        ("d", 0, 1),
        ("d", 256, 1),
        ("d", 512, 1),
        (PATCH_AT, 1536, 1),
    ]
    got_z = [net.land(4) for _ in chunks]

    def raw_send(k):
        at, size, _ = chunks[k]
        if at == "d":
            cols = pl.ds(size, 256)
            src, dst = wd_in.at[:, cols], wd.at[rows_of((tok * 4 + z) * 96, 96), cols]
            pieces = [(src, dst)]
        elif at == OUT_AT:
            pieces = [(w_out_in, str_.at[z, :, pl.ds(at, 768)])]
        elif at == PATCH_AT:
            pieces = [
                (w_patch_in, str_.at[z, :, pl.ds(PATCH_AT, 768)]),
                (w_class_in, str_.at[z, :, pl.ds(CLASS_AT, 768)]),
            ]
        else:
            cols = pl.ds(at, size)
            pieces = [(wra.at[:, cols], str_.at[z, :, cols])]
        got = [got_z[k] + z] if len(pieces) == 1 else [got_z[k] + z, got_p + z]
        for (src, dst), slot in zip(pieces, got):
            net.local(src, dst, slot)
            for peer in peers:
                net.send(src, dst, peer, slot)

    got_p = net.land(4)
    raw_send(0)
    raw_send(1)
    raw_send(2)
    home = 2 * c + x
    got_lead, got_piece, got_cls = net.land(4), net.land(4), net.land(4)
    got_dm, got_aux = net.land(), net.land()
    for q in (3, 2, 1, 0):
        to = device(y, q // 2, q % 2, home)
        mine = (z == home) & (quarter == q)
        off = LEAD + PIECE * q
        if q == 3:
            src = cls_in
        else:
            src = patches.at[pl.ds(off, PIECE)]
        net.send(src, xs.at[rows_of(z * ROWS + off, PIECE)], to, got_piece + z, mine)
        net.send(
            patches.at[pl.ds(0, LEAD)], xs.at[rows_of(z * ROWS, LEAD)], to, got_lead + z, mine
        )
    to_home = device(y, lax.rem(z, 2), lax.div(z, 2), home)
    at_home = z == home
    net.send(aux_in, aux, to_home, got_aux, at_home)
    for part in range(3):
        net.local(wqa.at[:, q_cols[part]], stq.at[z, :, q_cols[part]], got_q[part] + z)
        for peer in peers:
            net.send(wqa.at[:, q_cols[part]], stq.at[z, :, q_cols[part]], peer, got_q[part] + z)
    for k in range(3, len(chunks)):
        raw_send(k)
    dmx[...] = tn(d_masks[...].astype(BF), spread_matrix(BF, (2 * REAL, 256), 1)).astype(BF)
    net.send(dmx, dmh, to_home, got_dm, at_home)

    sx, sy, ss = [], [], []
    for _ in chunks:
        sx.append(net.land(3))
        sy.append(net.land(3))
        ss.append(net.land(4))

    def parts(k):
        at, size = chunks[k][0:2]
        if at == "d":
            return wd, big, pl.ds(size, 128), pl.ds(size + 128, 128), pl.ds(size, 256)
        return wr, blk, pl.ds(at, size // 2), pl.ds(at + size // 2, size // 2), pl.ds(at, size)

    def pass_on(ref, to, slot):
        net.send(ref, ref, to, slot)

    def stage_z(k):
        def step():
            at, size, split = chunks[k]
            ref, rows, a, b, both = parts(k)
            for src in range(4):
                if at == "d":
                    net.wait(wd.at[rows_of((tok * 4 + src) * 96, 96), both], got_z[k] + src)
                elif at == PATCH_AT:
                    net.wait(str_.at[src, :, pl.ds(PATCH_AT, 768)], got_z[k] + src)
                    net.wait(str_.at[src, :, pl.ds(CLASS_AT, 768)], got_p + src)
                else:
                    net.wait(str_.at[src, :, both], got_z[k] + src)
            if at != "d":
                join(str_, wr.at[blk(tok)], at, size, 384)
            own = ref.at[rows(tok)]
            if split:
                pass_on(own.at[:, a], xdev, sx[k])
                pass_on(own.at[:, b], ydev, sy[k])
                pass_on(own.at[:, b], xdev, sx[k] + 1)
                pass_on(own.at[:, a], ydev, sy[k] + 1)
            else:
                pass_on(own.at[:, both], xdev, sx[k])
                pass_on(own.at[:, both], ydev, sy[k])
            pass_on(own.at[:, both], sib, ss[k])

        return step

    def stage_one(k):
        def step():
            ref, rows, a, b, both = parts(k)
            got_x, got_y = ref.at[rows(t_x)], ref.at[rows(t_y)]
            if chunks[k][2]:
                net.wait(got_x.at[:, a], sx[k])
                pass_on(got_x.at[:, a], ydev, sy[k] + 2)
                net.wait(got_y.at[:, b], sy[k])
                pass_on(got_y.at[:, b], xdev, sx[k] + 2)
            else:
                net.wait(got_x.at[:, both], sx[k])
                pass_on(got_x.at[:, both], ydev, sy[k] + 1)
                pass_on(got_x.at[:, both], sib, ss[k] + 1)

        return step

    def stage_two(k):
        def step():
            ref, rows, a, b, both = parts(k)
            got_x, got_y = ref.at[rows(t_x)], ref.at[rows(t_y)]
            if chunks[k][2]:
                net.wait(got_x.at[:, b], sx[k] + 1)
                pass_on(got_x.at[:, both], sib, ss[k] + 1)
                net.wait(got_y.at[:, a], sy[k] + 1)
            else:
                net.wait(got_y.at[:, both], sy[k])
            pass_on(got_y.at[:, both], sib, ss[k] + 2)

        return step

    def stage_three(k):
        def step():
            ref, rows, a, b, both = parts(k)
            got = ref.at[rows(t_xy)]
            if chunks[k][2]:
                net.wait(got.at[:, a], sy[k] + 2)
                net.wait(got.at[:, b], sx[k] + 2)
            else:
                net.wait(got.at[:, both], sy[k] + 1)
            pass_on(got.at[:, both], sib, ss[k] + 3)

        return step

    def ready(k):
        ref, rows, a, b, both = parts(k)
        for i, t in enumerate((tok, t_x, t_y, t_xy)):
            net.wait(ref.at[rows(t + flip), both], ss[k] + i)

    def piece(source, owner):
        return xs.at[rows_of(source * ROWS + LEAD + PIECE * owner, PIECE)]

    fwd_s, fwd_x, fwd_xs = net.land(4), net.land(4), net.land(4)
    near = [lax.rem(z + step, 4) for step in (0, 1, 3, 2)]

    def row_step(i):
        src = near[i]
        net.wait(piece(src, quarter), got_piece + src)
        net.send(piece(src, quarter), piece(src, quarter), xdev, fwd_x + src)
        net.send(piece(src, quarter), piece(src, quarter), sib, fwd_s + src)

    def row_cross(i):
        src = near[i]
        net.wait(piece(src, other), fwd_x + src)
        net.send(piece(src, other), piece(src, other), sib, fwd_xs + src)

    stage_z(0)()
    row_step(0)
    stage_z(1)()
    stage_one(0)()
    stage_z(2)()
    stage_two(0)()
    stage_one(1)()
    row_step(1)
    stage_three(0)()
    row_step(2)
    stage_two(1)()
    stage_one(2)()
    row_step(3)
    stage_three(1)()

    q_x, q_y, q_xy, q_s = net.land(3), net.land(3), net.land(3), net.land(12)

    def q_join(part):
        for src in range(4):
            net.wait(stq.at[src, :, q_cols[part]], got_q[part] + src)
        join(stq, bq, 768 * part, 768, 384)
        own = lanes_of(768 * part + 384 * x, 384)
        far = lanes_of(768 * part + 384 * (1 - x), 384)
        cols = pl.ds(384 * part, 384)
        net.send(bq.at[:, far], wq.at[blk(tok), cols], xdev, q_x + part)
        net.send(bq.at[:, own], wq.at[blk(tok), cols], ydev, q_y + part)
        wq[blk(tok), cols] = bq[:, own]
        net.send(bq.at[:, own], wq.at[blk(tok), cols], sib, q_s + part)

    def q_cross(part):
        cols = pl.ds(384 * part, 384)
        ref = wq.at[blk(t_x), cols]
        net.wait(ref, q_x + part)
        net.send(ref, ref, ydev, q_xy + part)
        net.send(ref, ref, sib, q_s + 3 + part)

    def q_last(part):
        cols = pl.ds(384 * part, 384)
        net.wait(wq.at[blk(t_y), cols], q_y + part)
        net.send(wq.at[blk(t_y), cols], wq.at[blk(t_y), cols], sib, q_s + 6 + part)
        net.wait(wq.at[blk(t_xy), cols], q_xy + part)
        net.send(wq.at[blk(t_xy), cols], wq.at[blk(t_xy), cols], sib, q_s + 9 + part)

    q_join(0)
    row_cross(0)
    row_cross(1)
    q_join(1)
    q_cross(0)
    row_cross(2)
    q_join(2)
    q_cross(1)
    row_cross(3)
    stage_two(2)()
    q_cross(2)
    sibling = quarter + flip
    for src in range(4):
        net.wait(xs.at[rows_of(src * ROWS, LEAD)], got_lead + src)
        net.wait(piece(src, sibling), fwd_s + src)
    stage_three(2)()
    stage_z(3)()
    for part in range(3):
        q_last(part)
    for src in range(4):
        net.wait(piece(src, sibling + 2 - 4 * x), fwd_xs + src)
    net.wait(aux, got_aux)

    def norm_step(i, carry):
        rows = rows_of(i * ROWS, ROWS)
        zn[rows, :] = normalise(xs[rows, :].astype(F32))[0].astype(BF)
        return carry

    lax.fori_loop(0, 4, norm_step, 0)
    count = len(chunks)
    pump = Pump()
    z_, o_, t_, h_ = stage_z, stage_one, stage_two, stage_three
    order = [z_(4), o_(3), z_(5), t_(3), o_(4), z_(6), h_(3), t_(4), o_(5), z_(7), h_(4), t_(5)]
    order += [o_(6), h_(5), t_(6), o_(7), t_(7), h_(6), h_(7)]
    for step in order:
        pump.add(step)
    pump.run(2)
    for part in range(3):
        cols = pl.ds(384 * part, 384)
        for i, t in enumerate((tok, t_x, t_y, t_xy)):
            net.wait(wq.at[blk(t + flip), cols], q_s + 3 * i + part)

    lead_len, tail_len = aux[0:1, 0:1], aux[1:2, 0:1]
    keep = own_lanes(c, None, (768, 256))
    for part in range(3):
        cols = lanes_of(384 * part + 128 * c, 256)
        wp[:, 256 * part : 256 * part + 256] = jnp.where(keep, wq[:, cols], 0.0).astype(BF)

    def project(i, carry):
        rows = rows_of(i * ROWS, ROWS)
        normed = zn[rows, :]
        qr[rows, :] = (nn(normed, wp[:, 0:256]).astype(BF) * 0.125).astype(BF)
        kr[rows, :] = nn(normed, wp[:, 256:512]).astype(BF)
        vr[rows, :] = nn(normed, wp[:, 512:768]).astype(BF)
        return carry

    lax.fori_loop(0, 4, project, 0)
    pump.run(1)
    for head in range(3):
        mine = own_lanes(c, head, (SLOT_ROWS, 256))
        cols = pl.ds(256 * head, 256)
        pool0[:, cols] = jnp.where(mine, kr[...], 0.0).astype(BF)
        pool1[:, cols] = jnp.where(mine, vr[...], 0.0).astype(BF)
    own_rows = rows_of(block_id * ROWS, ROWS)
    store(xs, xs_o)
    store(qr, qr_o)
    store(kr, kr_o)
    store(vr, vr_o)
    store(wp, wp_o)
    store(aux, aux_o)
    key_row = lax.broadcasted_iota(jnp.int32, (1, SLOT_ROWS), 1)
    key_seg, key_filler = segments(key_row, lead_len, tail_len)
    key_seg = jnp.where(key_seg < 0, -5, key_seg)
    masked = jnp.where(key_filler, -3e38, -1e30)
    group = group_of(y, x, c, z)
    got_o, got_cn, got_dc = net.land(4), net.land(4), net.land(4)
    lane = lax.broadcasted_iota(jnp.int32, (ROWS, 128), 1)
    for to, _, q in group[::-1] + [(None, quarter, block_id)]:
        rows = rows_of(q * ROWS, ROWS)
        row = lax.broadcasted_iota(jnp.int32, (ROWS, 1), 0) + q * ROWS
        seg = segments(row, lead_len, tail_len)[0]
        query = qr[rows, :]
        total_out = jnp.zeros((ROWS, 256), F32)
        kept = jnp.zeros((ROWS, 128), F32)
        for head in range(3):
            cols = pl.ds(256 * head, 256)
            scores = jnp.where(seg == key_seg, nt(query, pool0[:, cols]), masked)
            top = jnp.max(scores, axis=1, keepdims=True)
            expo = jnp.exp(scores - top)
            total = jnp.sum(expo, axis=1, keepdims=True)
            probs = (expo * (1.0 / total)).astype(BF)
            total_out = total_out + nn(probs, pool1[:, cols])
            kept = jnp.where(lane == head, top + jnp.log(total), kept)
            pump.run(1)
        out[rows, :] = total_out.astype(BF)
        stats[rows, :] = kept
        if to is None:
            net.local(out.at[rows], obuf.at[quarter], got_o + quarter)
        else:
            net.send(out.at[rows], obuf.at[quarter], to, got_o + quarter)
    store(out, out_o)
    store(stats, stats_o)

    row = lax.broadcasted_iota(jnp.int32, (PATCH, 1), 0) + block_id * ROWS
    seg = segments(row, lead_len, tail_len)[0]
    first_image = seg == 0
    valid = jnp.where(seg >= 0, 1.0, 0.0)
    for q in range(4):
        net.wait(obuf.at[q], got_o + q)
    for side in range(2):
        a, b = obuf[2 * side], obuf[2 * side + 1]
        base = 384 * side
        att[:, base : base + 128] = a[:, 0:128]
        att[:, base + 128 : base + 256] = a[:, 128:256] + b[:, 0:128]
        att[:, base + 256 : base + 384] = b[:, 128:256]
    ready(3)
    store(wr.at[:, pl.ds(OUT_AT, 768)], wr_o.at[:, pl.ds(OUT_AT, 768)])
    w_out = wr.at[:, pl.ds(OUT_AT, 768)]
    w_patch, w_class = wr.at[:, pl.ds(PATCH_AT, 768)], wr.at[:, pl.ds(CLASS_AT, 768)]
    h_f[...] = xs[own_rows, :].astype(F32) + nn(att[...], w_out[...])
    normed, scale = normalise(h_f[...])
    inv[...] = jnp.broadcast_to(scale, inv.shape)
    zn2[...] = normed.astype(BF)
    znt[...] = normed.T.astype(BF)
    for k in range(3):
        ready(k)
    store(wr.at[:, pl.ds(UP_AT, 3072)], wr_o.at[:, pl.ds(UP_AT, 3072)])
    gl, slope = pool0, pool1

    def panel(i):
        return rows_of(lax.div(i, 3) * ROWS, ROWS), lanes_of(lax.rem(i, 3) * TILE, TILE)

    def up_step(i, carry):
        u = nn(zn2[...], wr[:, lanes_of(UP_AT + i * TILE, TILE)])
        cdf = 0.5 * (1.0 + lax.erf(u * 0.7071067811865476))
        rows, cols = panel(i)
        gl[rows, cols] = (u * cdf).astype(BF)
        slope[rows, cols] = (cdf + u * (jnp.exp(-0.5 * u * u) * 0.3989422804014327)).astype(BF)
        return carry

    for turn in range(4):
        lax.fori_loop(3 * turn, 3 * turn + 3, up_step, 0)
        pump.run(1)
    pump.run()
    store(gl, gl_o)
    store(slope, slope_o)
    for k in range(4, 7):
        ready(k)
    store(wd, wd_o)
    mlp = nn(gl[0:ROWS, :], wd[0:768, :])
    for p in range(1, 4):
        mlp = mlp + nn(gl[ROWS * p : ROWS * p + ROWS, :], wd[768 * p : 768 * p + 768, :])
    z2[...] = (h_f[...] + mlp).astype(BF)
    z2p, z2c = z2[0:PATCH, :], z2[PATCH:ROWS, :]

    def unit(values):
        return values * lax.rsqrt(jnp.sum(values * values, axis=-1, keepdims=True) + 1e-06)

    def unit_back(values, cot):
        r = lax.rsqrt(jnp.sum(values * values, axis=-1, keepdims=True) + 1e-06)
        return r * cot - values * (r * r * r * jnp.sum(values * cot, axis=-1, keepdims=True))

    ready(7)
    store(wr.at[:, pl.ds(PATCH_AT, 1536)], wr_o.at[:, pl.ds(PATCH_AT, 1536)])
    cc = nn(z2c, w_class[...])
    own_cls = rows_of(block_id * CLS, CLS)
    cn[own_cls, :] = unit(cc).astype(BF)
    for to, _, q in group:
        net.send(cn.at[own_cls], cn.at[own_cls], to, got_cn + block_id)
    pp = nn(z2p, w_patch[...])
    pp_f[...] = pp
    pn = unit(pp).astype(BF)
    net.wait(dmh, got_dm)
    for _, _, q in group:
        net.wait(cn.at[rows_of(q * CLS, CLS)], got_cn + q)
    low, high = cn[0 : 2 * CLS, :], cn[2 * CLS : 4 * CLS, :]
    wide = 2 * CLS
    lane = lax.broadcasted_iota(jnp.int32, (1, wide), 1)
    real = jnp.where(lane >= CLS, lane - CLS, lane) < REAL
    gain = exact(gain_in[...], spread_matrix(F32, (2 * REAL, 2 * CLS), 1), ((1,), (0,)))
    raw = jnp.where(first_image, nt(pn, low), nt(pn, high))

    def mean(values):
        return jnp.sum(jnp.where(real, values, 0.0), axis=1, keepdims=True) * (0.5 / REAL)

    centre = jnp.where(real, raw - mean(raw), 0.0)
    sigma = lax.rsqrt(mean(centre * centre) + 1e-05)
    xhat = centre * sigma
    mask_gain = gain[0:1, :]
    dm = dmh[:, 0:wide].astype(F32) * valid
    dx = jnp.where(real, dm * mask_gain, 0.0)
    d_raw = jnp.where(real, sigma * (dx - mean(dx) - xhat * mean(dx * xhat)), 0.0)
    d_low = jnp.where(first_image, d_raw, 0.0).astype(BF)
    d_high = jnp.where(first_image, 0.0, d_raw).astype(BF)
    dcn[0:wide, :] = tn(d_low, pn).astype(BF)
    dcn[wide : 2 * wide, :] = tn(d_high, pn).astype(BF)
    for to, _, q in group:
        net.send(dcn.at[rows_of(q * CLS, CLS)], dcbuf.at[quarter], to, got_dc + quarter)
    net.local(dcn.at[own_cls], dcbuf.at[quarter], got_dc + quarter)
    masks[:, wide:256] = jnp.zeros((PATCH, 256 - wide), BF)
    masks[:, 0:wide] = (xhat * mask_gain * valid).astype(BF)
    gain_part[...] = jnp.zeros_like(gain_part)
    gain_part[0:1, 0:wide] = jnp.sum(dm * xhat, axis=0, keepdims=True)
    d_pn = nn(d_low, low) + nn(d_high, high)
    dpc[0:PATCH, :] = unit_back(pp_f[...], d_pn).astype(BF)
    for q in range(4):
        net.wait(dcbuf.at[q], got_dc + q)
    d_cn = dcbuf[0].astype(F32) + dcbuf[1].astype(F32) + dcbuf[2].astype(F32) + dcbuf[3].astype(F32)
    dpc[PATCH:ROWS, :] = unit_back(cc, d_cn).astype(BF)
    for dst, slot in outs:
        net.wait(dst, slot)
    net.finish()


def add_into(total, part, width):
    def body(i, carry):
        cols = lanes_of(i * width, width)
        total[:, cols] = (total[:, cols].astype(F32) + part[:, cols].astype(F32)).astype(BF)
        return carry

    lax.fori_loop(0, total.shape[1] // width, body, 0)


def split_rows(block, stage, width):
    def body(i, carry):
        cols = lanes_of(i * width, width)
        values = block[:, cols].astype(F32)
        for part in range(4):
            stage[part, :, cols] = values[24 * part : 24 * part + 24].astype(BF)
        return carry

    lax.fori_loop(0, block.shape[1] // width, body, 0)


def sum_parts(stage, total, width):
    def body(i, carry):
        cols = lanes_of(i * width, width)
        total[:, cols] = (
            stage[0, :, cols].astype(F32)
            + stage[1, :, cols].astype(F32)
            + stage[2, :, cols].astype(F32)
            + stage[3, :, cols].astype(F32)
        )
        return carry

    lax.fori_loop(0, total.shape[1] // width, body, 0)


def back_kernel(
    dpc, z2, znt, h_f, inv, att, masks, gain_part, gl_in, slope_in, wr, wd, xs_in,
    qr, kr, vr, out, stats, wp, aux,
    d_rows, mask_rows, sum_q, sum_r, sum_d, gain_sum,
    pool0, pool1, wpo, wds, wus, gr, gd, rr, rd, ra_r, rb_r, ra_d, rb_d, sp, rz, rzd,
    rq, ryq, rxq, spq, rzq, fb, fc, back, gz, gh, dk, dv, d_out, dz_f, dzb, dzn,
    send_sem, recv_sem,
):
    y, x, c, z = position()
    quarter, block_id = 2 * x + c, 2 * c + x
    net = Net(send_sem, recv_sem, None)
    got_gl, got_sl, got_wpo, got_xb = net.land(), net.land(), net.land(), net.land()
    got_wd, got_wu = net.land(8), net.land(8)
    own_rows = rows_of(block_id * ROWS, ROWS)
    own_wpo = wpo.at[:, pl.ds(768, 1536)]
    got_wo = net.land()
    net.local(wr.at[:, pl.ds(PATCH_AT, 1536)], own_wpo, got_wpo)
    net.local(gl_in, pool0, got_gl)
    net.local(slope_in, pool1, got_sl)

    def load(i):
        net.local(wd.at[pl.ds(PANEL * i, PANEL)], wds.at[i % 2], got_wd + i)
        net.local(wr.at[:, pl.ds(UP_AT + PANEL * i, PANEL)], wus.at[i % 2], got_wu + i)

    load(0)
    load(1)
    net.local(wr.at[:, pl.ds(OUT_AT, 768)], wpo.at[:, pl.ds(0, 768)], got_wo)
    net.local(xs_in.at[own_rows], back, got_xb)
    enter(y, x, c, z)
    sib, xdev, ydev = device(y, x, 1 - c, z), device(y, 1 - x, c, z), device(1 - y, x, c, z)
    peers = [(device(y, x, c, lax.rem(z + s, 4)), lax.rem(z + s, 4)) for s in (1, 3, 2)]
    group = group_of(y, x, c, z)

    def tok_of(b, core):
        return (b // 2) * 4 + (b % 2) * 2 + core

    def tok_of2(q, core):
        return lax.div(q, 2) * 4 + lax.rem(q, 2) * 2 + core

    def blk(t):
        return rows_of(t * 96, 96)

    def big(t):
        return rows_of(t * 384, 384)

    chunks = [
        (PATCH_AT, 1536, 0),
        (UP_AT, 1536, 1),
        (UP_AT + 1536, 1536, 1),
        ("d", 0, 1),
        ("d", 256, 1),
        ("d", 512, 0),
        (OUT_AT, 768, 0),
    ]
    count = len(chunks)
    sib_in = [net.land(4) for _ in chunks]
    a_in = [net.land(2) for _ in chunks]
    b_in = [net.land() for _ in chunks]
    z_in = [net.land(4) for _ in chunks]

    def parts(k):
        at, size, y_first = chunks[k]
        if at == "d":
            cols = pl.ds(size, 256)
            grad, rows, width = gd, big, 256
            views = [ref.at[:, :, cols] for ref in (rd, ra_d)] + [rb_d.at[:, cols]]
        else:
            cols = pl.ds(at, size)
            grad, rows, width = gr, blk, 384
            views = [ref.at[:, :, cols] for ref in (rr, ra_r)] + [rb_r.at[:, cols]]

        def mine(a, b):
            return grad.at[rows(a * 4 + b * 2 + c), cols]

        return cols, mine, views, width, y_first

    def core_send(k):
        at = chunks[k][0]
        cols, mine, (new, _, _), _, _ = parts(k)
        for b in range(4):
            t = tok_of(b, 1 - c)
            src = gd.at[big(t), cols] if at == "d" else gr.at[blk(t), cols]
            net.send(src, new.at[b], sib, sib_in[k] + b)

    def stage_core(k):
        def step():
            cols, mine, (new, ra, rb), width, y_first = parts(k)
            for b in range(4):
                net.wait(new.at[b], sib_in[k] + b)
                add_into(mine(b // 2, b % 2), new.at[b], width)
            for i in range(2):
                far, to = (mine(1 - y, i), ydev) if y_first else (mine(i, 1 - x), xdev)
                net.send(far, ra.at[i], to, a_in[k] + i)

        return step

    def stage_one(k):
        def step():
            cols, mine, (new, ra, rb), width, y_first = parts(k)
            for i in range(2):
                net.wait(ra.at[i], a_in[k] + i)
                add_into(mine(y, i) if y_first else mine(i, x), ra.at[i], width)
            last, to = (mine(y, 1 - x), xdev) if y_first else (mine(1 - y, x), ydev)
            net.send(last, rb, to, b_in[k])

        return step

    def stage_two(k):
        def step():
            cols, mine, (new, ra, rb), width, y_first = parts(k)
            net.wait(rb, b_in[k])
            add_into(mine(y, x), rb, width)
            if chunks[k][0] == "d":
                base = (y * 4 + x * 2 + c) * 384
                for peer, pz in peers:
                    net.send(
                        gd.at[rows_of(base + 96 * pz, 96), cols], rzd.at[z, :, cols], peer, z_in[k] + z
                    )
                net.local(gd.at[rows_of(base + 96 * z, 96), cols], rzd.at[z, :, cols], z_in[k] + z)
            else:
                split_rows(mine(y, x), sp.at[:, :, cols], width)
                for peer, pz in peers:
                    net.send(sp.at[pz, :, cols], rz.at[z, :, cols], peer, z_in[k] + z)
                net.local(sp.at[z, :, cols], rz.at[z, :, cols], z_in[k] + z)

        return step

    def stage_sum(k):
        def step():
            cols, _, _, width, _ = parts(k)
            if chunks[k][0] == "d":
                stage, total = rzd, sum_d
            else:
                stage, total = rz, sum_r
            for part in range(4):
                net.wait(stage.at[part, :, cols], z_in[k] + part)
            sum_parts(stage.at[:, :, cols], total.at[:, cols], width)

        return step

    pump = Pump()
    c_, o_, t_, s_ = stage_core, stage_one, stage_two, stage_sum
    order = [
        [c_(0)],
        [c_(1)],
        [],
        [o_(0), c_(5), c_(4)],
        [],
        [],
        [o_(1)],
        [],
        [c_(6), c_(3)],
        [t_(0), t_(1)],
        [o_(4)],
        [o_(5), o_(6)],
        [c_(2), o_(3), t_(4)],
        [],
        [t_(5), t_(3), t_(6)],
        [],
        [o_(2), t_(2)],
        [s_(5)],
        [s_(2), s_(0), s_(1), s_(3), s_(4), s_(6)],
    ]
    for steps in order:
        pump.add(lambda steps=steps: [step() for step in steps])

    got_mask, got_back = net.land(), net.land(2)
    owner = device(y, lax.rem(z, 2), lax.div(z, 2), block_id)
    is_owner = block_id == z
    net.send(masks, mask_rows, owner, got_mask, is_owner)
    gz_in = net.land(4)
    for peer, pz in peers:
        net.send(gain_part, gz.at[z], peer, gz_in + z)
    net.local(gain_part, gz.at[z], gz_in + z)
    gh_in = net.land(3)

    def gain_first():
        for part in range(4):
            net.wait(gz.at[part], gz_in + part)
        gain_sum[...] = gz[0] + gz[1] + gz[2] + gz[3]
        gh[0] = gain_sum[...]
        net.send(gh.at[0], gh.at[3], xdev, gh_in)

    def gain_next(i, to):
        net.wait(gh.at[2 + i], gh_in + i - 1)
        gain_sum[...] += gh[2 + i]
        if to is not None:
            gh[i] = gain_sum[...]
            net.send(gh.at[i], gh.at[3 + i], to, gh_in + i)

    net.wait(own_wpo, got_wpo)
    z2p, z2c = z2[0:PATCH, :], z2[PATCH:ROWS, :]
    d_pp, d_cc = dpc[0:PATCH, :], dpc[PATCH:ROWS, :]
    gr[:, PATCH_AT : PATCH_AT + 768] = tn(z2p, d_pp).astype(BF)
    gr[:, CLASS_AT : CLASS_AT + 768] = tn(z2c, d_cc).astype(BF)
    core_send(0)
    dz_f[0:PATCH, :] = nt(d_pp, wpo[:, 768:1536])
    dz_f[PATCH:ROWS, :] = nt(d_cc, wpo[:, 1536:2304])
    dzb[...] = dz_f[...].astype(BF)
    net.wait(pool0, got_gl)
    net.wait(pool1, got_sl)
    for i in range(8):
        net.wait(wds.at[i % 2], got_wd + i)
        net.wait(wus.at[i % 2], got_wu + i)
        rows = pl.ds(ROWS * (i // 2), ROWS)
        cols = pl.ds(PANEL * (i % 2), PANEL)
        d_u = (nt(dzb[...], wds[i % 2]) * pool1[rows, cols].astype(F32)).astype(BF)
        gd[PANEL * i : PANEL * i + PANEL, :] = tn(pool0[rows, cols], dzb[...]).astype(BF)
        gr[:, UP_AT + PANEL * i : UP_AT + PANEL * i + PANEL] = nn(znt[...], d_u).astype(BF)
        part = nt(d_u, wus[i % 2])
        if i == 0:
            dzn[...] = part
        else:
            dzn[...] += part
        if i + 2 < 8:
            load(i + 2)
        if i == 0:
            gain_first()
        if i == 2:
            gain_next(1, ydev)
        if i == 4:
            gain_next(2, sib)
        if i == 6:
            gain_next(3, None)
        if i == 3:
            core_send(1)
            pump.run(1)
        if i == 7:
            core_send(2)
            pump.run(1)
    mark = len(net.open)
    for k in (3, 4, 5):
        core_send(k)
    dsent = net.take(mark)
    d_zn = dzn[...]
    normed = h_f[...]
    normed = (normed - jnp.mean(normed, axis=-1, keepdims=True)) * inv[:, 0:1]
    d_h = dz_f[...] + inv[:, 0:1] * (
        d_zn
        - jnp.mean(d_zn, axis=-1, keepdims=True)
        - normed * jnp.mean(d_zn * normed, axis=-1, keepdims=True)
    )
    dz_f[...] = d_h
    d_hb = d_h.astype(BF)
    net.wait(wpo.at[:, pl.ds(0, 768)], got_wo)
    dob, dh = dzb, dz_f
    dob[...] = nt(d_hb, wpo[:, 0:768]).astype(BF)

    got_do = net.land(4)

    def piece(q):
        return dob.at[:, lanes_of(384 * lax.div(q, 2) + 128 * lax.rem(q, 2), 256)]

    net.local(piece(quarter), d_out.at[own_rows], got_do + block_id)
    for to, q, _ in group:
        net.send(piece(q), d_out.at[own_rows], to, got_do + block_id)
    gr[:, OUT_AT : OUT_AT + 768] = tn(att[...], d_hb).astype(BF)
    core_send(6)
    pump.run(1)
    kh, vh = pool0, pool1

    lead_len, tail_len = aux[0:1, 0:1], aux[1:2, 0:1]
    key_col = lax.broadcasted_iota(jnp.int32, (SLOT_ROWS, 1), 0)
    key_seg, key_filler = segments(key_col, lead_len, tail_len)
    key_seg = jnp.where(key_seg < 0, -5, key_seg)
    masked = jnp.where(key_filler, -3e38, -1e30)
    def dqkv(q):
        return gd.at[rows_of(384 * tok_of2(q, 1 - c), ROWS)]

    for head in range(3):
        mine = own_lanes(c, head, (SLOT_ROWS, 256))
        cols = pl.ds(256 * head, 256)
        kh[:, cols] = jnp.where(mine, kr[...], 0.0).astype(BF)
        vh[:, cols] = jnp.where(mine, vr[...], 0.0).astype(BF)
    lane = lax.broadcasted_iota(jnp.int32, (8, 256), 1)
    row8 = lax.broadcasted_iota(jnp.int32, (8, 256), 0)
    picker = jnp.where((row8 < 3) & (lane // 64 - c == row8), 1.0, 0.0)
    for n, q in enumerate([block_id] + [q for _, _, q in group]):
        rows = rows_of(q * ROWS, ROWS)
        net.wait(d_out.at[rows], got_do + q)
        query, d_result = qr[rows, :], d_out[rows, :]
        stat = stats[rows, :].T
        product = d_result.astype(F32) * out[rows, :].astype(F32)
        delta = lax.dot_general(
            picker,
            product,
            (((1,), (1,)), ((), ())),
            precision=lax.Precision.HIGHEST,
            preferred_element_type=F32,
        )
        query_row = lax.broadcasted_iota(jnp.int32, (1, ROWS), 1) + q * ROWS
        query_seg = segments(query_row, lead_len, tail_len)[0]
        d_query = jnp.zeros((ROWS, 256), F32)
        for head in range(3):
            mine = own_lanes(c, head, (ROWS, 256))
            cols = pl.ds(256 * head, 256)
            own_query = jnp.where(mine, query, 0.0).astype(BF)
            own_result = jnp.where(mine, d_result, 0.0).astype(BF)
            for side in range(2):
                low, high = side * SLOT_ROWS // 2, (side + 1) * SLOT_ROWS // 2
                keys = pl.ds(low, SLOT_ROWS // 2)
                key = kh[keys, cols]
                allowed = key_seg[low:high] == query_seg
                scores = jnp.where(allowed, nt(key, query), masked[low:high])
                probs = jnp.exp(scores - stat[head : head + 1, :])
                d_probs = nt(vh[keys, cols], d_result)
                d_scores = jnp.where(allowed, probs * (d_probs - delta[head : head + 1, :]), 0.0)
                d_scores = d_scores.astype(BF)
                d_query = d_query + tn(d_scores, key)
                d_key = nn(d_scores, own_query)
                d_value = nn(probs.astype(BF), own_result)
                if n == 0 and head == 0:
                    dk[keys, :] = d_key
                    dv[keys, :] = d_value
                else:
                    dk[keys, :] += d_key
                    dv[keys, :] += d_value
            pump.run(1)
        if n == 0:
            net.finish_some(dsent)
        dqkv(q)[:, 0:256] = (d_query * 0.125).astype(BF)
    for q in range(4):
        rows = pl.ds(ROWS * q, ROWS)
        dqkv(q)[:, 256:512] = dk[rows, :].astype(BF)
        dqkv(q)[:, 512:768] = dv[rows, :].astype(BF)
    got_xs = net.land()
    net.local(xs_in, pool1, got_xs)

    fb_in, fc_in = net.land(2), net.land(2)
    halves = (pl.ds(0, 176), pl.ds(176, 160))
    (_, _, sib_q), (_, _, cross_q), (_, _, diag_q) = group

    def first(q):
        rows = rows_of(q * ROWS, ROWS)
        pool0[rows, :] = nt(dqkv(q)[...], wp[...]).astype(BF)
        return pool0.at[rows]

    net.send(first(diag_q), fb.at[0], sib, fb_in)
    net.send(first(sib_q), fb.at[1], sib, fb_in + 1)
    far = first(cross_q)
    net.wait(fb.at[0], fb_in)
    for i, part in enumerate(halves):
        add_into(far.at[part], fb.at[0, part], 256)
        net.send(far.at[part], fc.at[part], xdev, fc_in + i)
    near = first(block_id)

    qb_in = [net.land(4) for _ in range(3)]
    qy_in, qx_in, qz_in = net.land(6), net.land(3), [net.land(4) for _ in range(3)]
    first_core = c == 0

    gq = wpo.at[:, pl.ds(0, 768)]

    def hq(b):
        return wpo.at[rows_of(96 * b, 96), pl.ds(768, 1152)]

    def fq(part):
        return wds.at[0, pl.ds(96 * part, 96)]

    def q_make(part):
        cols = pl.ds(256 * part, 256)
        total = tn(pool1[0:ROWS, :], dqkv(0)[:, cols])
        for q in range(1, 4):
            total = total + tn(pool1[ROWS * q : ROWS * q + ROWS, :], dqkv(q)[:, cols])
        gq[:, cols] = total.astype(BF)
        for b in range(4):
            net.send(gq.at[blk(tok_of(b, 1 - c)), cols], rq.at[b, :, cols], sib, qb_in[part] + b)

    def q_core(part):
        cols = pl.ds(256 * part, 256)
        half = pl.ds(384 * part, 384)
        base = 384 * part
        for b in range(4):
            net.wait(rq.at[b, :, cols], qb_in[part] + b)
            own = gq[blk(tok_of(b, c)), cols].astype(F32)
            new = rq[b, :, cols].astype(F32)
            left, right = jnp.where(first_core, own, new), jnp.where(first_core, new, own)
            hq(b)[:, base : base + 128] = left[:, 0:128].astype(BF)
            hq(b)[:, base + 128 : base + 256] = (left[:, 128:256] + right[:, 0:128]).astype(BF)
            hq(b)[:, base + 256 : base + 384] = right[:, 128:256].astype(BF)
        for side in range(2):
            net.send(
                hq(2 * (1 - y) + side).at[:, half], ryq.at[side, :, half], ydev, qy_in + 2 * part + side
            )

    def q_one(part):
        half = pl.ds(384 * part, 384)
        for side in range(2):
            net.wait(ryq.at[side, :, half], qy_in + 2 * part + side)
            add_into(hq(2 * y + side).at[:, half], ryq.at[side, :, half], 384)
        net.send(hq(2 * y + 1 - x).at[:, half], rxq.at[:, half], xdev, qx_in + part)

    def q_two(part):
        half = pl.ds(384 * part, 384)
        both = pl.ds(768 * part, 768)
        net.wait(rxq.at[:, half], qx_in + part)
        fq(part)[:, lanes_of(384 * x, 384)] = hq(2 * y + x)[:, half]
        fq(part)[:, lanes_of(384 * (1 - x), 384)] = rxq[:, half]
        split_rows(fq(part), spq.at[:, :, both], 384)
        for peer, pz in peers:
            net.send(spq.at[pz, :, both], rzq.at[z, :, both], peer, qz_in[part] + z)
        net.local(spq.at[z, :, both], rzq.at[z, :, both], qz_in[part] + z)

    def q_sum(part):
        both = pl.ds(768 * part, 768)
        for src in range(4):
            net.wait(rzq.at[src, :, both], qz_in[part] + src)
        sum_parts(rzq.at[:, :, both], sum_q.at[:, both], 384)

    def finish_rows(i):
        part = halves[i]
        net.wait(fc.at[part], fc_in + i)
        d_zn = near[part, :].astype(F32) + fc[part, :].astype(F32)
        normed, scale = normalise(back[part, :].astype(F32))
        d_x = dh[part, :] + scale * (
            d_zn
            - jnp.mean(d_zn, axis=-1, keepdims=True)
            - normed * jnp.mean(d_zn * normed, axis=-1, keepdims=True)
        )
        back[part, :] = d_x.astype(BF)
        net.send(back.at[part], d_rows.at[part], owner, got_back + i, is_owner)

    net.wait(pool1, got_xs)

    def norm_step(i, carry):
        rows = rows_of(i * ROWS, ROWS)
        pool1[rows, :] = normalise(pool1[rows, :].astype(F32))[0].astype(BF)
        return carry

    lax.fori_loop(0, 4, norm_step, 0)
    q_make(0)
    q_make(1)
    q_core(0)
    q_make(2)
    q_core(1)
    q_core(2)
    net.wait(back, got_xb)
    net.wait(fb.at[1], fb_in + 1)
    add_into(near, fb.at[1], 256)
    pump.run(1)
    finish_rows(0)
    finish_rows(1)
    pump.run(1)
    for part in range(3):
        q_one(part)
    pump.run(1)
    for part in range(3):
        q_two(part)
    pump.run()
    for part in range(3):
        q_sum(part)
    net.wait(mask_rows, got_mask)
    for i, part in enumerate(halves):
        net.wait(d_rows.at[part], got_back + i)
    net.finish()


def last_kernel(
    d_rows, mask_rows, sum_q, sum_r, sum_d, gain_sum, w_qkv, w_up, g1, g2,
    masks, d_patches, d_classes, d_qkv, d_out, d_up, d_down, d_patch, d_class, d_one, d_two, d_gain,
):
    masks[...] = nt(spread_matrix(BF, (2 * REAL, 256), 1), mask_rows[...])
    d_patches[...] = d_rows[0:PATCH, :].astype(F32)
    d_classes[...] = d_rows[PATCH : PATCH + REAL, :].astype(F32)
    total = sum_q[...]
    d_qkv[...] = total * column(g1)
    ones = jnp.ones((8, total.shape[1]), F32)
    d_one[...] = exact(ones, total * w_qkv[...].astype(F32), ((1,), (1,)))[0:1, :]
    total = sum_r[:, UP_AT : UP_AT + 3072]
    d_up[...] = total * column(g2)
    ones = jnp.ones((8, total.shape[1]), F32)
    d_two[...] = exact(ones, total * w_up[...].astype(F32), ((1,), (1,)))[0:1, :]
    d_out[...] = sum_r[:, OUT_AT : OUT_AT + 768]
    d_down[...] = sum_d[...]
    d_patch[...] = sum_r[:, PATCH_AT : PATCH_AT + 768]
    d_class[...] = sum_r[:, CLASS_AT : CLASS_AT + 768]
    d_gain[...] = exact(gain_sum[...], spread_matrix(F32, (256, 2 * REAL), 0), ((1,), (0,)))[0:1, :]


VMEM_SPEC = pl.BlockSpec(memory_space=pltpu.VMEM)
ANY_SPEC = pl.BlockSpec(memory_space=pl.ANY)


def call(body, ident, specs, outs, scratch, sems, args, cost):
    out_shape = tuple(jax.ShapeDtypeStruct(shape, kind) for shape, kind, _ in outs)
    scratch_shapes = [pltpu.VMEM(shape, kind) for shape, kind in scratch]
    if sems:
        scratch_shapes += [pltpu.SemaphoreType.DMA((n,)) for n in sems]
    extra = {} if ident is None else dict(collective_id=ident, has_side_effects=True)
    return pl.pallas_call(
        body,
        out_shape=out_shape,
        in_specs=list(specs),
        out_specs=tuple(spec for _, _, spec in outs),
        scratch_shapes=scratch_shapes,
        compiler_params=pltpu.CompilerParams(vmem_limit_bytes=63 * 2**20, **extra),
        cost_estimate=pl.CostEstimate(flops=cost, bytes_accessed=2**24, transcendentals=0),
    )(*args)


def home_plan(
    patches,
    classes,
    slot_lengths,
    w_qkv,
    w_out,
    w_up,
    w_down,
    w_patch,
    w_class,
    norm1,
    norm2,
    mask_gain,
    d_masks,
):
    V, A = VMEM_SPEC, ANY_SPEC
    wide = 3 * w_out.shape[1] + w_up.shape[1]
    rows = w_qkv.shape[0]
    g1, g2 = norm1.reshape(1, rows), norm2.reshape(1, rows)
    slot, part = (SLOT_ROWS, 768), (SLOT_ROWS, 256)
    row_shape = (ROWS, 768)
    kept = call(
        front_kernel,
        1,
        [V] * 13,
        [
            (row_shape, BF, V),
            (row_shape, BF, V),
            ((768, ROWS), BF, V),
            (row_shape, F32, V),
            ((ROWS, 128), F32, V),
            (row_shape, BF, V),
            ((PATCH, 256), BF, V),
            ((8, 256), F32, V),
            (slot, BF, A),
            (slot, BF, A),
            ((768, wide), BF, A),
            ((3072, 768), BF, A),
            (slot, BF, A),
            (part, BF, A),
            (part, BF, A),
            (part, BF, A),
            (part, BF, A),
            ((SLOT_ROWS, 128), F32, A),
            ((768, 768), BF, A),
            ((8, 128), jnp.int32, A),
        ],
        [
            (slot, BF),
            (slot, BF),
            (part, BF),
            (part, BF),
            (part, BF),
            (part, BF),
            ((SLOT_ROWS, 128), F32),
            ((768, 768), BF),
            ((768, 1152), BF),
            ((768, wide), BF),
            ((3072, 768), BF),
            ((4, 24, 2304), BF),
            ((4, 24, wide), BF),
            ((96, 2304), BF),
            (slot, BF),
            (slot, BF),
            ((PATCH, 256), BF),
            ((8, 128), jnp.int32),
            ((CLS, 768), BF),
            ((PATCH, 256), BF),
            ((8, 128), jnp.int32),
            ((24, 2304), BF),
            ((24, wide), BF),
            ((4, ROWS, 256), BF),
            (row_shape, BF),
            ((PATCH, 768), F32),
            ((4 * CLS, 768), BF),
            ((4 * CLS, 768), BF),
            ((4, CLS, 768), BF),
        ],
        (200, 260),
        (
            patches,
            classes,
            slot_lengths,
            w_qkv,
            w_out,
            w_up,
            w_down,
            w_patch,
            w_class,
            g1,
            g2,
            mask_gain.reshape(1, -1),
            d_masks.T,
        ),
        10**10,
    )
    d_rows, mask_rows, sum_q, sum_r, sum_d, gain_sum = call(
        back_kernel,
        2,
        [V] * 6 + [A, V] + [A] * 5 + [V] * 7,
        [
            (row_shape, BF, A),
            ((PATCH, 256), BF, A),
            ((24, 2304), F32, V),
            ((24, wide), F32, V),
            ((96, 768), F32, V),
            ((8, 256), F32, V),
        ],
        [
            (slot, BF),
            (slot, BF),
            ((768, 2304), BF),
            ((2, PANEL, 768), BF),
            ((2, 768, PANEL), BF),
            ((768, wide), BF),
            ((3072, 768), BF),
            ((4, 96, wide), BF),
            ((4, 384, 768), BF),
            ((2, 96, wide), BF),
            ((96, wide), BF),
            ((2, 384, 768), BF),
            ((384, 768), BF),
            ((4, 24, wide), BF),
            ((4, 24, wide), BF),
            ((4, 96, 768), BF),
            ((4, 96, 768), BF),
            ((2, 96, 1152), BF),
            ((96, 1152), BF),
            ((4, 24, 2304), BF),
            ((4, 24, 2304), BF),
            ((2, ROWS, 768), BF),
            (row_shape, BF),
            (row_shape, BF),
            ((4, 8, 256), F32),
            ((6, 8, 256), F32),
            (part, F32),
            (part, F32),
            (part, BF),
            (row_shape, F32),
            (row_shape, BF),
            (row_shape, F32),
        ],
        (160, 240),
        kept,
        10**10,
    )
    square = ((rows, 768), F32, V)
    masks, d_patches, d_classes, d_qkv, d_w_out, d_up, d_down, d_patch, d_class, d_one, d_two, d_gain = call(
        last_kernel,
        None,
        [V] * 10,
        [
            (d_masks.shape[::-1], F32, V),
            (patches.shape, F32, V),
            (classes.shape, F32, V),
            (w_qkv.shape, F32, V),
            square,
            (w_up.shape, F32, V),
            (w_down.shape, F32, V),
            square,
            square,
            ((1, rows), F32, V),
            ((1, rows), F32, V),
            ((1, 2 * REAL), F32, V),
        ],
        [],
        (),
        (d_rows, mask_rows, sum_q, sum_r, sum_d, gain_sum, w_qkv, w_up, g1, g2),
        10**7,
    )
    return (
        masks.T,
        d_patches,
        d_classes,
        d_qkv,
        d_w_out,
        d_up,
        d_down,
        d_patch,
        d_class,
        d_one.reshape(-1),
        d_two.reshape(-1),
        d_gain.reshape(-1),
    )


def solution(mesh):
    placed = (
        P(("tok", "head"), None),
        P(("tok", "head"), None),
        P("tok", None),
        P(("tok", "head"), None),
        P(("tok", "head"), None),
        P(("tok", "head"), None),
        P(("tok", "head"), None),
        P(("tok", "head"), None),
        P(("tok", "head"), None),
        P(("tok", "head")),
        P(("tok", "head")),
        P(),
        P(("tok", "head"), None),
    )
    fits = mesh.shape["tok"] == 8 and mesh.shape["head"] == 4
    return jax.shard_map(
        home_plan if fits else per_device,
        mesh=mesh,
        in_specs=placed,
        out_specs=(
            P(("tok", "head"), None),
            P(("tok", "head"), None),
            P(("tok", "head"), None),
            P(("tok", "head"), None),
            P(("tok", "head"), None),
            P(("tok", "head"), None),
            P(("tok", "head"), None),
            P(("tok", "head"), None),
            P(("tok", "head"), None),
            P(("tok", "head")),
            P(("tok", "head")),
            P(),
        ),
        check_vma=False,
    )
```

```python
import jax
import jax.numpy as jnp
from jax import lax
from jax.experimental import pallas as pl
from jax.experimental.pallas import tpu as pltpu
from jax.sharding import PartitionSpec as P

HEADS = 12
NCLS = 150


def layer_norm(values, gain):
    centre = values - jnp.mean(values, axis=-1, keepdims=True)
    spread = jnp.mean(centre * centre, axis=-1, keepdims=True)
    return centre * lax.rsqrt(spread + 1e-05) * gain


def unit_rows(values):
    return values * lax.rsqrt(jnp.sum(values * values, axis=-1, keepdims=True) + 1e-06)


def exact_gelu(values):
    return jax.nn.gelu(values, approximate=False)


def dot_plain(left, right):
    return jnp.dot(left, right, preferred_element_type=jnp.float32)


def dot_left_t(left, right):
    return lax.dot_general(
        left, right, (((0,), (0,)), ((), ())), preferred_element_type=jnp.float32
    )


def dot_right_t(left, right):
    return lax.dot_general(
        left, right, (((1,), (1,)), ((), ())), preferred_element_type=jnp.float32
    )


def flat_rows(matrix):
    return matrix.reshape(-1, 128)


def per_device(
    patches,
    classes,
    slot_lengths,
    w_qkv,
    w_out,
    w_up,
    w_down,
    w_patch,
    w_class,
    norm1,
    norm2,
    mask_gain,
    d_masks,
):
    tok_rows = patches.shape[0]
    cls_rows = classes.shape[0]
    all_rows = tok_rows + cls_rows
    width = patches.shape[1]
    groups = lax.axis_size("head")
    my_group = lax.axis_index("head")
    local_heads = HEADS // groups
    head_size = width // HEADS
    lead_len = slot_lengths[0, 0]
    tail_len = slot_lengths[0, 1]

    def segment_of(source, offset):
        place = source * tok_rows + offset
        patch_seg = jnp.where(place < lead_len, 0, jnp.where(place < lead_len + tail_len, 1, -1))
        class_seg = (source * cls_rows + offset - tok_rows) // NCLS
        return jnp.where(offset < tok_rows, patch_seg, class_seg)

    tok_seg = segment_of(my_group, jnp.arange(tok_rows))
    spread_rows = jnp.arange(groups * all_rows)
    head_seg = segment_of(spread_rows // all_rows, spread_rows % all_rows)
    allowed = (head_seg[:, None] == head_seg[None, :]) & (head_seg[None, :] >= 0)
    shards = (w_qkv, w_out, w_up, w_down, w_patch, w_class, norm1, norm2)
    gathered = (
        lax.all_gather(shards[0], ("tok", "head"), axis=0, tiled=True),
        lax.all_gather(shards[1], ("tok", "head"), axis=0, tiled=True),
        lax.all_gather(shards[2], ("tok", "head"), axis=0, tiled=True),
        lax.all_gather(shards[3], ("tok", "head"), axis=0, tiled=True),
        lax.all_gather(shards[4], ("tok", "head"), axis=0, tiled=True),
        lax.all_gather(shards[5], ("tok", "head"), axis=0, tiled=True),
        lax.all_gather(shards[6], ("tok", "head"), axis=0, tiled=True),
        lax.all_gather(shards[7], ("tok", "head"), axis=0, tiled=True),
    )
    full_qkv, full_out, full_up, full_down, full_patch, full_class, gain_one, gain_two = gathered
    stacked = jnp.concatenate([patches, classes], axis=0).astype(jnp.float32)
    first_in = layer_norm(stacked, gain_one.astype(jnp.float32)).astype(jnp.bfloat16)
    qkv_rows = (
        dot_plain(first_in, full_qkv)
        .astype(jnp.bfloat16)
        .reshape(all_rows, 3, groups, local_heads * head_size)
    )
    moved = lax.all_to_all(qkv_rows, "head", split_axis=2, concat_axis=0, tiled=True)
    moved = moved.reshape(groups * all_rows, 3, local_heads, head_size)
    queries = jnp.transpose(moved[:, 0], (1, 0, 2))
    key_rows = jnp.transpose(moved[:, 1], (1, 0, 2))
    value_rows = jnp.transpose(moved[:, 2], (1, 0, 2))

    def attend(parts):
        query, key_part, value_part = parts
        scores = jnp.where(allowed, dot_right_t(query, key_part) * 0.125, -1e30)
        top_score = jnp.max(scores, axis=1, keepdims=True)
        expo = jnp.exp(scores - top_score)
        total = jnp.sum(expo, axis=1, keepdims=True)
        probs = (expo / total).astype(jnp.bfloat16)
        result = dot_plain(probs, value_part).astype(jnp.bfloat16)
        return (result, top_score[:, 0] + jnp.log(total[:, 0]))

    head_out, log_total = lax.map(attend, (queries, key_rows, value_rows))
    sending = jnp.transpose(head_out, (1, 0, 2)).reshape(
        groups * all_rows, 1, local_heads * head_size
    )
    attended = lax.all_to_all(sending, "head", split_axis=0, concat_axis=1, tiled=True).reshape(
        all_rows, width
    )
    hidden = stacked + dot_plain(attended, full_out)
    second_in = layer_norm(hidden, gain_two.astype(jnp.float32)).astype(jnp.bfloat16)
    up_rows = dot_plain(second_in, full_up)
    gelu_rows = exact_gelu(up_rows).astype(jnp.bfloat16)
    after = (hidden + dot_plain(gelu_rows, full_down)).astype(jnp.bfloat16)
    patch_proj = dot_plain(after[:tok_rows], full_patch)
    class_proj = dot_plain(after[tok_rows:], full_class)
    patch_unit = unit_rows(patch_proj).astype(jnp.bfloat16)
    class_unit = unit_rows(class_proj).astype(jnp.bfloat16)
    slot_classes = lax.all_gather(class_unit, "head", axis=0, tiled=True)
    raw_both = dot_right_t(patch_unit, slot_classes)
    first_image = tok_seg[:, None] == 0
    raw = jnp.where(first_image, raw_both[:, :NCLS], raw_both[:, NCLS:])
    centre = raw - jnp.mean(raw, axis=1, keepdims=True)
    inv_sigma = lax.rsqrt(jnp.mean(centre * centre, axis=1, keepdims=True) + 1e-05)
    normed = centre * inv_sigma
    valid = (tok_seg >= 0).astype(jnp.float32)[:, None]
    masks = normed * mask_gain * valid
    regathered = (
        lax.all_gather(shards[0], ("tok", "head"), axis=0, tiled=True),
        lax.all_gather(shards[1], ("tok", "head"), axis=0, tiled=True),
        lax.all_gather(shards[2], ("tok", "head"), axis=0, tiled=True),
        lax.all_gather(shards[3], ("tok", "head"), axis=0, tiled=True),
        lax.all_gather(shards[4], ("tok", "head"), axis=0, tiled=True),
        lax.all_gather(shards[5], ("tok", "head"), axis=0, tiled=True),
        lax.all_gather(shards[6], ("tok", "head"), axis=0, tiled=True),
        lax.all_gather(shards[7], ("tok", "head"), axis=0, tiled=True),
    )
    back_qkv, back_out, back_up, back_down, back_patch, back_class, back_one, back_two = regathered
    mask_cot = d_masks * valid
    grad_mask = lax.psum(jnp.sum(mask_cot * normed, axis=0), ("tok", "head"))
    scaled = mask_cot * mask_gain
    d_raw = inv_sigma * (
        scaled
        - jnp.mean(scaled, axis=1, keepdims=True)
        - normed * jnp.mean(scaled * normed, axis=1, keepdims=True)
    )
    zero_part = jnp.zeros_like(d_raw)
    d_raw_both = jnp.concatenate(
        [jnp.where(first_image, d_raw, zero_part), jnp.where(first_image, zero_part, d_raw)], axis=1
    ).astype(jnp.bfloat16)
    d_patch_unit = dot_plain(d_raw_both, slot_classes)
    d_slot_classes = dot_left_t(d_raw_both, patch_unit)
    d_class_unit = lax.psum_scatter(
        d_slot_classes.astype(jnp.bfloat16), "head", scatter_dimension=0, tiled=True
    ).astype(jnp.float32)
    _, patch_pull = jax.vjp(unit_rows, patch_proj)
    d_patch_proj = patch_pull(d_patch_unit)[0].astype(jnp.bfloat16)
    _, class_pull = jax.vjp(unit_rows, class_proj)
    d_class_proj = class_pull(d_class_unit)[0].astype(jnp.bfloat16)
    grad_patch_w = dot_left_t(after[:tok_rows], d_patch_proj)
    grad_class_w = dot_left_t(after[tok_rows:], d_class_proj)
    d_after = jnp.concatenate(
        [dot_right_t(d_patch_proj, back_patch), dot_right_t(d_class_proj, back_class)], axis=0
    )
    d_after_low = d_after.astype(jnp.bfloat16)
    grad_down_w = dot_left_t(gelu_rows, d_after_low)
    d_gelu = dot_right_t(d_after_low, back_down)
    _, gelu_pull = jax.vjp(exact_gelu, up_rows)
    d_up_rows = gelu_pull(d_gelu)[0].astype(jnp.bfloat16)
    grad_up_w = dot_left_t(second_in, d_up_rows)
    d_second_in = dot_right_t(d_up_rows, back_up)
    _, norm_two_pull = jax.vjp(layer_norm, hidden, back_two.astype(jnp.float32))
    d_hidden_norm, grad_gain_two = norm_two_pull(d_second_in)
    d_hidden = d_after + d_hidden_norm
    d_hidden_low = d_hidden.astype(jnp.bfloat16)
    grad_out_w = dot_left_t(attended, d_hidden_low)
    d_attended = (
        dot_right_t(d_hidden_low, back_out)
        .astype(jnp.bfloat16)
        .reshape(all_rows, groups, local_heads * head_size)
    )
    d_head_out = lax.all_to_all(d_attended, "head", split_axis=1, concat_axis=0, tiled=True)
    d_head_out = jnp.transpose(
        d_head_out.reshape(groups * all_rows, local_heads, head_size), (1, 0, 2)
    )

    def attend_back(parts):
        query, key_part, value_part, log_row, d_result = parts
        scores = jnp.where(allowed, dot_right_t(query, key_part) * 0.125, -1e30)
        probs = jnp.exp(scores - log_row[:, None])
        d_probs = dot_right_t(d_result, value_part)
        inner = jnp.sum(probs * d_probs, axis=1, keepdims=True)
        d_scores = jnp.where(allowed, probs * (d_probs - inner), 0.0).astype(jnp.bfloat16)
        d_query = (dot_plain(d_scores, key_part) * 0.125).astype(jnp.bfloat16)
        d_key = (dot_left_t(d_scores, query) * 0.125).astype(jnp.bfloat16)
        d_value = dot_left_t(probs.astype(jnp.bfloat16), d_result).astype(jnp.bfloat16)
        return jnp.stack([d_query, d_key, d_value], axis=0)

    d_moved = lax.map(attend_back, (queries, key_rows, value_rows, log_total, d_head_out))
    d_moved = jnp.transpose(d_moved, (2, 1, 0, 3)).reshape(
        groups * all_rows, 3, 1, local_heads * head_size
    )
    d_qkv = lax.all_to_all(d_moved, "head", split_axis=0, concat_axis=2, tiled=True).reshape(
        all_rows, 3 * width
    )
    grad_qkv_w = dot_left_t(first_in, d_qkv)
    d_first_in = dot_right_t(d_qkv, back_qkv)
    _, norm_one_pull = jax.vjp(layer_norm, stacked, back_one.astype(jnp.float32))
    d_stacked_norm, grad_gain_one = norm_one_pull(d_first_in)
    d_stacked = d_hidden + d_stacked_norm
    every_sum = (
        lax.psum_scatter(flat_rows(grad_qkv_w), ("tok", "head"), scatter_dimension=0, tiled=True),
        lax.psum_scatter(flat_rows(grad_out_w), ("tok", "head"), scatter_dimension=0, tiled=True),
        lax.psum_scatter(flat_rows(grad_up_w), ("tok", "head"), scatter_dimension=0, tiled=True),
        lax.psum_scatter(flat_rows(grad_down_w), ("tok", "head"), scatter_dimension=0, tiled=True),
        lax.psum_scatter(flat_rows(grad_patch_w), ("tok", "head"), scatter_dimension=0, tiled=True),
        lax.psum_scatter(flat_rows(grad_class_w), ("tok", "head"), scatter_dimension=0, tiled=True),
        lax.psum_scatter(grad_gain_one, ("tok", "head"), scatter_dimension=0, tiled=True),
        lax.psum_scatter(grad_gain_two, ("tok", "head"), scatter_dimension=0, tiled=True),
    )
    sum_qkv, sum_out, sum_up, sum_down, sum_patch, sum_class, sum_one, sum_two = every_sum
    sum_qkv = sum_qkv.reshape(-1, 3 * width)
    sum_out = sum_out.reshape(-1, width)
    sum_up = sum_up.reshape(-1, grad_up_w.shape[1])
    sum_down = sum_down.reshape(-1, width)
    sum_patch = sum_patch.reshape(-1, width)
    sum_class = sum_class.reshape(-1, width)
    return (
        masks,
        d_stacked[:tok_rows],
        d_stacked[tok_rows:],
        sum_qkv,
        sum_out,
        sum_up,
        sum_down,
        sum_patch,
        sum_class,
        sum_one,
        sum_two,
        grad_mask,
    )


ROWS = 336
SLOT_ROWS = 4 * ROWS
PATCH = 256
CLS = 80
REAL = 75
PIECE = 80
LEAD = 16
MESH = pl.DeviceIdType.MESH
BF = jnp.bfloat16
F32 = jnp.float32


def position():
    tok = lax.axis_index("tok")
    return lax.div(tok, 4), lax.rem(lax.div(tok, 2), 2), lax.rem(tok, 2), lax.axis_index("head")


def device(y, x, c, z):
    return {"tok": y * 4 + x * 2 + c, "head": z}


def enter(y, x, c, z):
    barrier = pltpu.get_barrier_semaphore()
    others = [device(1 - y, x, c, z)]
    for turn in range(1, 16):
        flip_x, flip_c, step = turn // 8, (turn // 4) % 2, turn % 4
        others.append(
            device(
                y,
                1 - x if flip_x else x,
                1 - c if flip_c else c,
                lax.rem(z + step, 4),
            )
        )
    for other in others:
        pl.semaphore_signal(barrier, inc=1, device_id=other, device_id_type=MESH)
    pl.semaphore_wait(barrier, len(others))


class Net:
    def __init__(self, send_sem, recv_sem, here):
        self.send_sem, self.recv_sem, self.here = send_sem, recv_sem, here
        self.sends, self.recvs, self.open = 0, 0, []

    def land(self, count=1):
        first = self.recvs
        self.recvs += count
        return first

    def send(self, src, dst, to, slot, skip=None):
        index = self.sends
        self.sends += 1
        copy = pltpu.make_async_remote_copy(
            src_ref=src,
            dst_ref=dst,
            send_sem=self.send_sem.at[index],
            recv_sem=self.recv_sem.at[slot],
            device_id=to,
            device_id_type=MESH,
        )
        if skip is None:
            copy.start()
            self.open.append((copy, None))
        else:
            pl.when(jnp.logical_not(skip))(copy.start)
            self.open.append((copy, skip))

            @pl.when(skip)
            def _():
                pltpu.make_async_copy(src, dst, self.recv_sem.at[slot]).start()

    def local(self, src, dst, slot):
        pltpu.make_async_copy(src, dst, self.recv_sem.at[slot]).start()

    def wait(self, ref, slot):
        pltpu.make_async_copy(ref, ref, self.recv_sem.at[slot]).wait()

    def take(self, mark):
        taken, self.open = self.open[mark:], self.open[:mark]
        return taken

    def finish_some(self, taken):
        for copy, _ in taken:
            copy.wait_send()

    def finish(self):
        for copy, skip in self.open:
            if skip is None:
                copy.wait_send()
            else:
                pl.when(jnp.logical_not(skip))(copy.wait_send)
        self.open = []


def rows_of(start, size):
    return pl.ds(pl.multiple_of(start, 16), size)


def lanes_of(start, size):
    return pl.ds(pl.multiple_of(start, 128), size)


def nn(left, right):
    return jnp.dot(left, right, preferred_element_type=F32)


def nt(left, right):
    return lax.dot_general(left, right, (((1,), (1,)), ((), ())), preferred_element_type=F32)


def tn(left, right):
    return lax.dot_general(left, right, (((0,), (0,)), ((), ())), preferred_element_type=F32)


def segments(row, lead_len, tail_len):
    source = (
        (row >= ROWS).astype(jnp.int32)
        + (row >= 2 * ROWS).astype(jnp.int32)
        + (row >= 3 * ROWS).astype(jnp.int32)
    )
    offset = row - source * ROWS
    patch = source * PATCH + offset
    patch_seg = jnp.where(patch < lead_len, 0, jnp.where(patch < lead_len + tail_len, 1, -1))
    number = offset - PATCH
    class_seg = jnp.where(source >= 2, 1, 0)
    filler = number >= REAL
    seg = jnp.where(offset < PATCH, patch_seg, jnp.where(filler, -1, class_seg))
    return seg, filler


def normalise(values):
    centre = values - jnp.mean(values, axis=-1, keepdims=True)
    scale = lax.rsqrt(jnp.mean(centre * centre, axis=-1, keepdims=True) + 1e-05)
    return centre * scale, scale


def own_lanes(c, head, shape):
    lane = lax.broadcasted_iota(jnp.int32, shape, len(shape) - 1)
    group = lane // 64 - c
    if head is None:
        return (group >= 0) & (group < 3)
    return group == head


def group_of(y, x, c, z):
    near = [(x, 1 - c), (1 - x, c), (1 - x, 1 - c)]
    return [(device(y, a, b, z), 2 * a + b, 2 * b + a) for a, b in near]


def spread_matrix(kind, shape, lane_axis):
    packed = lax.broadcasted_iota(jnp.int32, shape, 1 - lane_axis)
    padded = lax.broadcasted_iota(jnp.int32, shape, lane_axis)
    return jnp.where(padded == packed + jnp.where(packed >= REAL, CLS - REAL, 0), 1.0, 0.0).astype(
        kind
    )


def exact(left, right, dims):
    return lax.dot_general(
        left,
        right,
        (dims, ((), ())),
        precision=lax.Precision.HIGHEST,
        preferred_element_type=F32,
    )


def column(row):
    size = row.shape[1]
    first = lax.broadcasted_iota(jnp.int32, (size, size), 0)
    second = lax.broadcasted_iota(jnp.int32, (size, size), 1)
    spread = jnp.where(first == second, jnp.broadcast_to(row[...].astype(F32), (size, size)), 0.0)
    return jnp.sum(spread, axis=1, keepdims=True)


TILE = 256
PANEL = 384


class Pump:
    def __init__(self):
        self.todo = []

    def add(self, step):
        self.todo.append(step)

    def run(self, count=None):
        count = len(self.todo) if count is None else min(count, len(self.todo))
        for step in self.todo[:count]:
            step()
        self.todo = self.todo[count:]


def join(stage, block, start, size, width):
    def body(i, carry):
        cols = lanes_of(start + i * width, width)
        parts = [stage[src, :, cols].astype(F32) for src in range(4)]
        block[:, cols] = jnp.concatenate(parts, axis=0).astype(BF)
        return carry

    lax.fori_loop(0, size // width, body, 0)


OUT_AT, UP_AT, PATCH_AT, CLASS_AT = 0, 768, 3840, 4608


def front_kernel(
    patches, classes, lens, w_qkv, w_out_in, w_up, wd_in, w_patch_in, w_class_in, g1, g2, gain_in,
    d_masks,
    dpc, z2, znt_o, h_o, inv_o, att_o, masks, gain_part,
    gl_o, slope_o, wr_o, wd_o, xs_o, qr_o, kr_o, vr_o, out_o, stats_o, wp_o, aux_o,
    xs, zn, qr, kr, vr, out, stats, wp, wq, wr, wd, stq, str_, bq, pool0, pool1,
    dmh, aux, cls_in, dmx, aux_in, wqa, wra, obuf, zn2, pp_f, cn, dcn, dcbuf, znt, h_f, inv, att,
    send_sem, recv_sem,
):
    y, x, c, z = position()
    tok = y * 4 + x * 2 + c
    quarter, block_id = 2 * x + c, 2 * c + x
    wra[:, UP_AT : UP_AT + 3072] = (w_up[...].astype(F32) * column(g2)).astype(BF)
    wqa[...] = (w_qkv[...].astype(F32) * column(g1)).astype(BF)
    cls_in[...] = jnp.zeros_like(cls_in)
    cls_in[0:REAL, :] = classes[...]
    pair = lens[...]
    aux_row = lax.broadcasted_iota(jnp.int32, (8, 128), 0)
    aux_in[...] = jnp.where(aux_row == 0, pair[0:1, 0:1], pair[0:1, 1:2])
    enter(y, x, c, z)
    net = Net(send_sem, recv_sem, None)
    sib, xdev, ydev = device(y, x, 1 - c, z), device(y, 1 - x, c, z), device(1 - y, x, c, z)
    flip = 1 - 2 * c
    t_x, t_y = tok + 2 - 4 * x, tok + 4 - 8 * y
    t_xy = t_x + 4 - 8 * y
    other = quarter + 2 - 4 * x
    peers = [device(y, x, c, lax.rem(z + step, 4)) for step in (1, 3, 2)]
    outs = []

    def store(src, dst):
        slot = net.land()
        net.local(src, dst, slot)
        outs.append((dst, slot))

    def blk(t):
        return rows_of(t * 96, 96)

    def big(t):
        return rows_of(t * 384, 384)

    q_cols = [pl.ds(768 * part, 768) for part in range(3)]
    got_q = [net.land(4) for _ in range(3)]
    chunks = [
        (UP_AT, 768, 0),
        (UP_AT + 768, 768, 0),
        (UP_AT + 1536, 1536, 0),
        (OUT_AT, 768, 1),
        ("d", 0, 1),
        ("d", 256, 1),
        ("d", 512, 1),
        (PATCH_AT, 1536, 1),
    ]
    got_z = [net.land(4) for _ in chunks]

    def raw_send(k):
        at, size, _ = chunks[k]
        if at == "d":
            cols = pl.ds(size, 256)
            src, dst = wd_in.at[:, cols], wd.at[rows_of((tok * 4 + z) * 96, 96), cols]
            pieces = [(src, dst)]
        elif at == OUT_AT:
            pieces = [(w_out_in, str_.at[z, :, pl.ds(at, 768)])]
        elif at == PATCH_AT:
            pieces = [
                (w_patch_in, str_.at[z, :, pl.ds(PATCH_AT, 768)]),
                (w_class_in, str_.at[z, :, pl.ds(CLASS_AT, 768)]),
            ]
        else:
            cols = pl.ds(at, size)
            pieces = [(wra.at[:, cols], str_.at[z, :, cols])]
        got = [got_z[k] + z] if len(pieces) == 1 else [got_z[k] + z, got_p + z]
        for (src, dst), slot in zip(pieces, got):
            net.local(src, dst, slot)
            for peer in peers:
                net.send(src, dst, peer, slot)

    got_p = net.land(4)
    raw_send(0)
    raw_send(1)
    raw_send(2)
    home = 2 * c + x
    got_lead, got_piece, got_cls = net.land(4), net.land(4), net.land(4)
    got_dm, got_aux = net.land(), net.land()
    for q in (3, 2, 1, 0):
        to = device(y, q // 2, q % 2, home)
        mine = (z == home) & (quarter == q)
        off = LEAD + PIECE * q
        if q == 3:
            src = cls_in
        else:
            src = patches.at[pl.ds(off, PIECE)]
        net.send(src, xs.at[rows_of(z * ROWS + off, PIECE)], to, got_piece + z, mine)
        net.send(
            patches.at[pl.ds(0, LEAD)], xs.at[rows_of(z * ROWS, LEAD)], to, got_lead + z, mine
        )
    to_home = device(y, lax.rem(z, 2), lax.div(z, 2), home)
    at_home = z == home
    net.send(aux_in, aux, to_home, got_aux, at_home)
    for part in range(3):
        net.local(wqa.at[:, q_cols[part]], stq.at[z, :, q_cols[part]], got_q[part] + z)
        for peer in peers:
            net.send(wqa.at[:, q_cols[part]], stq.at[z, :, q_cols[part]], peer, got_q[part] + z)
    for k in range(3, len(chunks)):
        raw_send(k)
    dmx[...] = tn(d_masks[...].astype(BF), spread_matrix(BF, (2 * REAL, 256), 1)).astype(BF)
    net.send(dmx, dmh, to_home, got_dm, at_home)

    sx, sy, ss = [], [], []
    for _ in chunks:
        sx.append(net.land(3))
        sy.append(net.land(3))
        ss.append(net.land(4))

    def parts(k):
        at, size = chunks[k][0:2]
        if at == "d":
            return wd, big, pl.ds(size, 128), pl.ds(size + 128, 128), pl.ds(size, 256)
        return wr, blk, pl.ds(at, size // 2), pl.ds(at + size // 2, size // 2), pl.ds(at, size)

    def pass_on(ref, to, slot):
        net.send(ref, ref, to, slot)

    def stage_z(k):
        def step():
            at, size, split = chunks[k]
            ref, rows, a, b, both = parts(k)
            for src in range(4):
                if at == "d":
                    net.wait(wd.at[rows_of((tok * 4 + src) * 96, 96), both], got_z[k] + src)
                elif at == PATCH_AT:
                    net.wait(str_.at[src, :, pl.ds(PATCH_AT, 768)], got_z[k] + src)
                    net.wait(str_.at[src, :, pl.ds(CLASS_AT, 768)], got_p + src)
                else:
                    net.wait(str_.at[src, :, both], got_z[k] + src)
            if at != "d":
                join(str_, wr.at[blk(tok)], at, size, 384)
            own = ref.at[rows(tok)]
            if split:
                pass_on(own.at[:, a], xdev, sx[k])
                pass_on(own.at[:, b], ydev, sy[k])
                pass_on(own.at[:, b], xdev, sx[k] + 1)
                pass_on(own.at[:, a], ydev, sy[k] + 1)
            else:
                pass_on(own.at[:, both], xdev, sx[k])
                pass_on(own.at[:, both], ydev, sy[k])
            pass_on(own.at[:, both], sib, ss[k])

        return step

    def stage_one(k):
        def step():
            ref, rows, a, b, both = parts(k)
            got_x, got_y = ref.at[rows(t_x)], ref.at[rows(t_y)]
            if chunks[k][2]:
                net.wait(got_x.at[:, a], sx[k])
                pass_on(got_x.at[:, a], ydev, sy[k] + 2)
                net.wait(got_y.at[:, b], sy[k])
                pass_on(got_y.at[:, b], xdev, sx[k] + 2)
            else:
                net.wait(got_x.at[:, both], sx[k])
                pass_on(got_x.at[:, both], ydev, sy[k] + 1)
                pass_on(got_x.at[:, both], sib, ss[k] + 1)

        return step

    def stage_two(k):
        def step():
            ref, rows, a, b, both = parts(k)
            got_x, got_y = ref.at[rows(t_x)], ref.at[rows(t_y)]
            if chunks[k][2]:
                net.wait(got_x.at[:, b], sx[k] + 1)
                pass_on(got_x.at[:, both], sib, ss[k] + 1)
                net.wait(got_y.at[:, a], sy[k] + 1)
            else:
                net.wait(got_y.at[:, both], sy[k])
            pass_on(got_y.at[:, both], sib, ss[k] + 2)

        return step

    def stage_three(k):
        def step():
            ref, rows, a, b, both = parts(k)
            got = ref.at[rows(t_xy)]
            if chunks[k][2]:
                net.wait(got.at[:, a], sy[k] + 2)
                net.wait(got.at[:, b], sx[k] + 2)
            else:
                net.wait(got.at[:, both], sy[k] + 1)
            pass_on(got.at[:, both], sib, ss[k] + 3)

        return step

    def ready(k):
        ref, rows, a, b, both = parts(k)
        for i, t in enumerate((tok, t_x, t_y, t_xy)):
            net.wait(ref.at[rows(t + flip), both], ss[k] + i)

    def piece(source, owner):
        return xs.at[rows_of(source * ROWS + LEAD + PIECE * owner, PIECE)]

    fwd_s, fwd_x, fwd_xs = net.land(4), net.land(4), net.land(4)
    near = [lax.rem(z + step, 4) for step in (0, 1, 3, 2)]

    def row_step(i):
        src = near[i]
        net.wait(piece(src, quarter), got_piece + src)
        net.send(piece(src, quarter), piece(src, quarter), xdev, fwd_x + src)
        net.send(piece(src, quarter), piece(src, quarter), sib, fwd_s + src)

    def row_cross(i):
        src = near[i]
        net.wait(piece(src, other), fwd_x + src)
        net.send(piece(src, other), piece(src, other), sib, fwd_xs + src)

    stage_z(0)()
    row_step(0)
    stage_z(1)()
    stage_one(0)()
    stage_z(2)()
    stage_two(0)()
    stage_one(1)()
    row_step(1)
    stage_three(0)()
    row_step(2)
    stage_two(1)()
    stage_one(2)()
    row_step(3)
    stage_three(1)()

    q_x, q_y, q_xy, q_s = net.land(3), net.land(3), net.land(3), net.land(12)

    def q_join(part):
        for src in range(4):
            net.wait(stq.at[src, :, q_cols[part]], got_q[part] + src)
        join(stq, bq, 768 * part, 768, 384)
        own = lanes_of(768 * part + 384 * x, 384)
        far = lanes_of(768 * part + 384 * (1 - x), 384)
        cols = pl.ds(384 * part, 384)
        net.send(bq.at[:, far], wq.at[blk(tok), cols], xdev, q_x + part)
        net.send(bq.at[:, own], wq.at[blk(tok), cols], ydev, q_y + part)
        wq[blk(tok), cols] = bq[:, own]
        net.send(bq.at[:, own], wq.at[blk(tok), cols], sib, q_s + part)

    def q_cross(part):
        cols = pl.ds(384 * part, 384)
        ref = wq.at[blk(t_x), cols]
        net.wait(ref, q_x + part)
        net.send(ref, ref, ydev, q_xy + part)
        net.send(ref, ref, sib, q_s + 3 + part)

    def q_last(part):
        cols = pl.ds(384 * part, 384)
        net.wait(wq.at[blk(t_y), cols], q_y + part)
        net.send(wq.at[blk(t_y), cols], wq.at[blk(t_y), cols], sib, q_s + 6 + part)
        net.wait(wq.at[blk(t_xy), cols], q_xy + part)
        net.send(wq.at[blk(t_xy), cols], wq.at[blk(t_xy), cols], sib, q_s + 9 + part)

    q_join(0)
    row_cross(0)
    row_cross(1)
    q_join(1)
    q_cross(0)
    row_cross(2)
    q_join(2)
    q_cross(1)
    row_cross(3)
    stage_two(2)()
    q_cross(2)
    sibling = quarter + flip
    for src in range(4):
        net.wait(xs.at[rows_of(src * ROWS, LEAD)], got_lead + src)
        net.wait(piece(src, sibling), fwd_s + src)
    stage_three(2)()
    stage_z(3)()
    for part in range(3):
        q_last(part)
    for src in range(4):
        net.wait(piece(src, sibling + 2 - 4 * x), fwd_xs + src)
    net.wait(aux, got_aux)

    def norm_step(i, carry):
        rows = rows_of(i * ROWS, ROWS)
        zn[rows, :] = normalise(xs[rows, :].astype(F32))[0].astype(BF)
        return carry

    lax.fori_loop(0, 4, norm_step, 0)
    count = len(chunks)
    pump = Pump()
    z_, o_, t_, h_ = stage_z, stage_one, stage_two, stage_three
    order = [z_(4), o_(3), z_(5), t_(3), o_(4), z_(6), h_(3), t_(4), o_(5), z_(7), h_(4), t_(5)]
    order += [o_(6), h_(5), t_(6), o_(7), t_(7), h_(6), h_(7)]
    for step in order:
        pump.add(step)
    pump.run(2)
    for part in range(3):
        cols = pl.ds(384 * part, 384)
        for i, t in enumerate((tok, t_x, t_y, t_xy)):
            net.wait(wq.at[blk(t + flip), cols], q_s + 3 * i + part)

    lead_len, tail_len = aux[0:1, 0:1], aux[1:2, 0:1]
    keep = own_lanes(c, None, (768, 256))
    for part in range(3):
        cols = lanes_of(384 * part + 128 * c, 256)
        wp[:, 256 * part : 256 * part + 256] = jnp.where(keep, wq[:, cols], 0.0).astype(BF)

    def project(i, carry):
        rows = rows_of(i * ROWS, ROWS)
        normed = zn[rows, :]
        qr[rows, :] = (nn(normed, wp[:, 0:256]).astype(BF) * 0.125).astype(BF)
        kr[rows, :] = nn(normed, wp[:, 256:512]).astype(BF)
        vr[rows, :] = nn(normed, wp[:, 512:768]).astype(BF)
        return carry

    lax.fori_loop(0, 4, project, 0)
    pump.run(1)
    for head in range(3):
        mine = own_lanes(c, head, (SLOT_ROWS, 256))
        cols = pl.ds(256 * head, 256)
        pool0[:, cols] = jnp.where(mine, kr[...], 0.0).astype(BF)
        pool1[:, cols] = jnp.where(mine, vr[...], 0.0).astype(BF)
    own_rows = rows_of(block_id * ROWS, ROWS)
    store(xs, xs_o)
    store(qr, qr_o)
    store(kr, kr_o)
    store(vr, vr_o)
    store(wp, wp_o)
    store(aux, aux_o)
    key_row = lax.broadcasted_iota(jnp.int32, (1, SLOT_ROWS), 1)
    key_seg, key_filler = segments(key_row, lead_len, tail_len)
    key_seg = jnp.where(key_seg < 0, -5, key_seg)
    masked = jnp.where(key_filler, -3e38, -1e30)
    group = group_of(y, x, c, z)
    got_o, got_cn, got_dc = net.land(4), net.land(4), net.land(4)
    lane = lax.broadcasted_iota(jnp.int32, (ROWS, 128), 1)
    for to, _, q in group[::-1] + [(None, quarter, block_id)]:
        rows = rows_of(q * ROWS, ROWS)
        row = lax.broadcasted_iota(jnp.int32, (ROWS, 1), 0) + q * ROWS
        seg = segments(row, lead_len, tail_len)[0]
        query = qr[rows, :]
        total_out = jnp.zeros((ROWS, 256), F32)
        kept = jnp.zeros((ROWS, 128), F32)
        for head in range(3):
            cols = pl.ds(256 * head, 256)
            scores = jnp.where(seg == key_seg, nt(query, pool0[:, cols]), masked)
            top = jnp.max(scores, axis=1, keepdims=True)
            expo = jnp.exp(scores - top)
            total = jnp.sum(expo, axis=1, keepdims=True)
            probs = (expo * (1.0 / total)).astype(BF)
            total_out = total_out + nn(probs, pool1[:, cols])
            kept = jnp.where(lane == head, top + jnp.log(total), kept)
            pump.run(1)
        out[rows, :] = total_out.astype(BF)
        stats[rows, :] = kept
        if to is None:
            net.local(out.at[rows], obuf.at[quarter], got_o + quarter)
        else:
            net.send(out.at[rows], obuf.at[quarter], to, got_o + quarter)
    store(out, out_o)
    store(stats, stats_o)

    row = lax.broadcasted_iota(jnp.int32, (PATCH, 1), 0) + block_id * ROWS
    seg = segments(row, lead_len, tail_len)[0]
    first_image = seg == 0
    valid = jnp.where(seg >= 0, 1.0, 0.0)
    for q in range(4):
        net.wait(obuf.at[q], got_o + q)
    for side in range(2):
        a, b = obuf[2 * side], obuf[2 * side + 1]
        base = 384 * side
        att[:, base : base + 128] = a[:, 0:128]
        att[:, base + 128 : base + 256] = a[:, 128:256] + b[:, 0:128]
        att[:, base + 256 : base + 384] = b[:, 128:256]
    ready(3)
    store(wr.at[:, pl.ds(OUT_AT, 768)], wr_o.at[:, pl.ds(OUT_AT, 768)])
    w_out = wr.at[:, pl.ds(OUT_AT, 768)]
    w_patch, w_class = wr.at[:, pl.ds(PATCH_AT, 768)], wr.at[:, pl.ds(CLASS_AT, 768)]
    h_f[...] = xs[own_rows, :].astype(F32) + nn(att[...], w_out[...])
    normed, scale = normalise(h_f[...])
    inv[...] = jnp.broadcast_to(scale, inv.shape)
    zn2[...] = normed.astype(BF)
    znt[...] = normed.T.astype(BF)
    for src, dst in ((znt, znt_o), (h_f, h_o), (inv, inv_o), (att, att_o)):
        store(src, dst)
    for k in range(3):
        ready(k)
    store(wr.at[:, pl.ds(UP_AT, 3072)], wr_o.at[:, pl.ds(UP_AT, 3072)])
    gl, slope = pool0, pool1

    def panel(i):
        return rows_of(lax.div(i, 3) * ROWS, ROWS), lanes_of(lax.rem(i, 3) * TILE, TILE)

    def up_step(i, carry):
        u = nn(zn2[...], wr[:, lanes_of(UP_AT + i * TILE, TILE)])
        cdf = 0.5 * (1.0 + lax.erf(u * 0.7071067811865476))
        rows, cols = panel(i)
        gl[rows, cols] = (u * cdf).astype(BF)
        slope[rows, cols] = (cdf + u * (jnp.exp(-0.5 * u * u) * 0.3989422804014327)).astype(BF)
        return carry

    for turn in range(4):
        lax.fori_loop(3 * turn, 3 * turn + 3, up_step, 0)
        pump.run(1)
    pump.run()
    store(gl, gl_o)
    store(slope, slope_o)
    for k in range(4, 7):
        ready(k)
    store(wd, wd_o)
    mlp = nn(gl[0:ROWS, :], wd[0:768, :])
    for p in range(1, 4):
        mlp = mlp + nn(gl[ROWS * p : ROWS * p + ROWS, :], wd[768 * p : 768 * p + 768, :])
    z2[...] = (h_f[...] + mlp).astype(BF)
    z2p, z2c = z2[0:PATCH, :], z2[PATCH:ROWS, :]

    def unit(values):
        return values * lax.rsqrt(jnp.sum(values * values, axis=-1, keepdims=True) + 1e-06)

    def unit_back(values, cot):
        r = lax.rsqrt(jnp.sum(values * values, axis=-1, keepdims=True) + 1e-06)
        return r * cot - values * (r * r * r * jnp.sum(values * cot, axis=-1, keepdims=True))

    ready(7)
    store(wr.at[:, pl.ds(PATCH_AT, 1536)], wr_o.at[:, pl.ds(PATCH_AT, 1536)])
    cc = nn(z2c, w_class[...])
    own_cls = rows_of(block_id * CLS, CLS)
    cn[own_cls, :] = unit(cc).astype(BF)
    for to, _, q in group:
        net.send(cn.at[own_cls], cn.at[own_cls], to, got_cn + block_id)
    pp = nn(z2p, w_patch[...])
    pp_f[...] = pp
    pn = unit(pp).astype(BF)
    net.wait(dmh, got_dm)
    for _, _, q in group:
        net.wait(cn.at[rows_of(q * CLS, CLS)], got_cn + q)
    low, high = cn[0 : 2 * CLS, :], cn[2 * CLS : 4 * CLS, :]
    wide = 2 * CLS
    lane = lax.broadcasted_iota(jnp.int32, (1, wide), 1)
    real = jnp.where(lane >= CLS, lane - CLS, lane) < REAL
    gain = exact(gain_in[...], spread_matrix(F32, (2 * REAL, 2 * CLS), 1), ((1,), (0,)))
    raw = jnp.where(first_image, nt(pn, low), nt(pn, high))

    def mean(values):
        return jnp.sum(jnp.where(real, values, 0.0), axis=1, keepdims=True) * (0.5 / REAL)

    centre = jnp.where(real, raw - mean(raw), 0.0)
    sigma = lax.rsqrt(mean(centre * centre) + 1e-05)
    xhat = centre * sigma
    mask_gain = gain[0:1, :]
    dm = dmh[:, 0:wide].astype(F32) * valid
    dx = jnp.where(real, dm * mask_gain, 0.0)
    d_raw = jnp.where(real, sigma * (dx - mean(dx) - xhat * mean(dx * xhat)), 0.0)
    d_low = jnp.where(first_image, d_raw, 0.0).astype(BF)
    d_high = jnp.where(first_image, 0.0, d_raw).astype(BF)
    dcn[0:wide, :] = tn(d_low, pn).astype(BF)
    dcn[wide : 2 * wide, :] = tn(d_high, pn).astype(BF)
    for to, _, q in group:
        net.send(dcn.at[rows_of(q * CLS, CLS)], dcbuf.at[quarter], to, got_dc + quarter)
    net.local(dcn.at[own_cls], dcbuf.at[quarter], got_dc + quarter)
    masks[:, wide:256] = jnp.zeros((PATCH, 256 - wide), BF)
    masks[:, 0:wide] = (xhat * mask_gain * valid).astype(BF)
    gain_part[...] = jnp.zeros_like(gain_part)
    gain_part[0:1, 0:wide] = jnp.sum(dm * xhat, axis=0, keepdims=True)
    d_pn = nn(d_low, low) + nn(d_high, high)
    dpc[0:PATCH, :] = unit_back(pp_f[...], d_pn).astype(BF)
    for q in range(4):
        net.wait(dcbuf.at[q], got_dc + q)
    d_cn = dcbuf[0].astype(F32) + dcbuf[1].astype(F32) + dcbuf[2].astype(F32) + dcbuf[3].astype(F32)
    dpc[PATCH:ROWS, :] = unit_back(cc, d_cn).astype(BF)
    for dst, slot in outs:
        net.wait(dst, slot)
    net.finish()


def add_into(total, part, width):
    def body(i, carry):
        cols = lanes_of(i * width, width)
        total[:, cols] = (total[:, cols].astype(F32) + part[:, cols].astype(F32)).astype(BF)
        return carry

    lax.fori_loop(0, total.shape[1] // width, body, 0)


def split_rows(block, stage, width):
    def body(i, carry):
        cols = lanes_of(i * width, width)
        values = block[:, cols].astype(F32)
        for part in range(4):
            stage[part, :, cols] = values[24 * part : 24 * part + 24].astype(BF)
        return carry

    lax.fori_loop(0, block.shape[1] // width, body, 0)


def sum_parts(stage, total, width):
    def body(i, carry):
        cols = lanes_of(i * width, width)
        total[:, cols] = (
            stage[0, :, cols].astype(F32)
            + stage[1, :, cols].astype(F32)
            + stage[2, :, cols].astype(F32)
            + stage[3, :, cols].astype(F32)
        )
        return carry

    lax.fori_loop(0, total.shape[1] // width, body, 0)


def back_kernel(
    dpc, z2, znt_in, h_in, inv_in, att_in, masks, gain_part, gl_in, slope_in, wr, wd, xs_in,
    qr_in, kr_in, vr_in, out_in, stats_in, wp_in, aux,
    d_rows, mask_rows, sum_q, sum_r, sum_d, gain_sum,
    pool0, pool1, wpo, wds, wus, gr, gd, rr, rd, ra_r, rb_r, ra_d, rb_d, sp, rz, rzd,
    rq, ryq, rxq, spq, rzq, fb, fc, back, gz, gh, dk, dv, d_out, dz_f, dzb, dzn, qr, kr, vr, out, stats, wp, znt, h_f, inv, att,
    send_sem, recv_sem,
):
    y, x, c, z = position()
    quarter, block_id = 2 * x + c, 2 * c + x
    net = Net(send_sem, recv_sem, None)
    got_gl, got_sl, got_wpo, got_xb = net.land(), net.land(), net.land(), net.land()
    got_wd, got_wu = net.land(8), net.land(8)
    own_rows = rows_of(block_id * ROWS, ROWS)
    own_wpo = wpo.at[:, pl.ds(768, 1536)]
    got_wo = net.land()
    net.local(wr.at[:, pl.ds(PATCH_AT, 1536)], own_wpo, got_wpo)
    net.local(gl_in, pool0, got_gl)
    net.local(slope_in, pool1, got_sl)

    def load(i):
        net.local(wd.at[pl.ds(PANEL * i, PANEL)], wds.at[i % 2], got_wd + i)
        net.local(wr.at[:, pl.ds(UP_AT + PANEL * i, PANEL)], wus.at[i % 2], got_wu + i)

    early = ((znt_in, znt), (h_in, h_f), (inv_in, inv), (att_in, att))
    got_early = net.land(len(early))
    net.local(znt_in, znt, got_early)
    load(0)
    load(1)
    for i, (src, dst) in enumerate(early):
        if i:
            net.local(src, dst, got_early + i)
    net.local(wr.at[:, pl.ds(OUT_AT, 768)], wpo.at[:, pl.ds(0, 768)], got_wo)
    net.local(xs_in.at[own_rows], back, got_xb)
    kept = ((kr_in, kr), (vr_in, vr), (qr_in, qr), (out_in, out), (stats_in, stats), (wp_in, wp))
    got_kept = net.land(len(kept))
    for i, (src, dst) in enumerate(kept):
        net.local(src, dst, got_kept + i)
    enter(y, x, c, z)
    sib, xdev, ydev = device(y, x, 1 - c, z), device(y, 1 - x, c, z), device(1 - y, x, c, z)
    peers = [(device(y, x, c, lax.rem(z + s, 4)), lax.rem(z + s, 4)) for s in (1, 3, 2)]
    group = group_of(y, x, c, z)

    def tok_of(b, core):
        return (b // 2) * 4 + (b % 2) * 2 + core

    def tok_of2(q, core):
        return lax.div(q, 2) * 4 + lax.rem(q, 2) * 2 + core

    def blk(t):
        return rows_of(t * 96, 96)

    def big(t):
        return rows_of(t * 384, 384)

    chunks = [
        (PATCH_AT, 1536, 0),
        (UP_AT, 1536, 1),
        (UP_AT + 1536, 1536, 1),
        ("d", 0, 1),
        ("d", 256, 1),
        ("d", 512, 0),
        (OUT_AT, 768, 0),
    ]
    count = len(chunks)
    sib_in = [net.land(4) for _ in chunks]
    a_in = [net.land(2) for _ in chunks]
    b_in = [net.land() for _ in chunks]
    z_in = [net.land(4) for _ in chunks]

    def parts(k):
        at, size, y_first = chunks[k]
        if at == "d":
            cols = pl.ds(size, 256)
            grad, rows, width = gd, big, 256
            views = [ref.at[:, :, cols] for ref in (rd, ra_d)] + [rb_d.at[:, cols]]
        else:
            cols = pl.ds(at, size)
            grad, rows, width = gr, blk, 384
            views = [ref.at[:, :, cols] for ref in (rr, ra_r)] + [rb_r.at[:, cols]]

        def mine(a, b):
            return grad.at[rows(a * 4 + b * 2 + c), cols]

        return cols, mine, views, width, y_first

    def core_send(k):
        at = chunks[k][0]
        cols, mine, (new, _, _), _, _ = parts(k)
        for b in range(4):
            t = tok_of(b, 1 - c)
            src = gd.at[big(t), cols] if at == "d" else gr.at[blk(t), cols]
            net.send(src, new.at[b], sib, sib_in[k] + b)

    def stage_core(k):
        def step():
            cols, mine, (new, ra, rb), width, y_first = parts(k)
            for b in range(4):
                net.wait(new.at[b], sib_in[k] + b)
                add_into(mine(b // 2, b % 2), new.at[b], width)
            for i in range(2):
                far, to = (mine(1 - y, i), ydev) if y_first else (mine(i, 1 - x), xdev)
                net.send(far, ra.at[i], to, a_in[k] + i)

        return step

    def stage_one(k):
        def step():
            cols, mine, (new, ra, rb), width, y_first = parts(k)
            for i in range(2):
                net.wait(ra.at[i], a_in[k] + i)
                add_into(mine(y, i) if y_first else mine(i, x), ra.at[i], width)
            last, to = (mine(y, 1 - x), xdev) if y_first else (mine(1 - y, x), ydev)
            net.send(last, rb, to, b_in[k])

        return step

    def stage_two(k):
        def step():
            cols, mine, (new, ra, rb), width, y_first = parts(k)
            net.wait(rb, b_in[k])
            add_into(mine(y, x), rb, width)
            if chunks[k][0] == "d":
                base = (y * 4 + x * 2 + c) * 384
                for peer, pz in peers:
                    net.send(
                        gd.at[rows_of(base + 96 * pz, 96), cols], rzd.at[z, :, cols], peer, z_in[k] + z
                    )
                net.local(gd.at[rows_of(base + 96 * z, 96), cols], rzd.at[z, :, cols], z_in[k] + z)
            else:
                split_rows(mine(y, x), sp.at[:, :, cols], width)
                for peer, pz in peers:
                    net.send(sp.at[pz, :, cols], rz.at[z, :, cols], peer, z_in[k] + z)
                net.local(sp.at[z, :, cols], rz.at[z, :, cols], z_in[k] + z)

        return step

    def stage_sum(k):
        def step():
            cols, _, _, width, _ = parts(k)
            if chunks[k][0] == "d":
                stage, total = rzd, sum_d
            else:
                stage, total = rz, sum_r
            for part in range(4):
                net.wait(stage.at[part, :, cols], z_in[k] + part)
            sum_parts(stage.at[:, :, cols], total.at[:, cols], width)

        return step

    pump = Pump()
    c_, o_, t_, s_ = stage_core, stage_one, stage_two, stage_sum
    order = [
        [c_(0)],
        [c_(1)],
        [],
        [o_(0), c_(5), c_(4)],
        [],
        [],
        [o_(1)],
        [],
        [c_(6), c_(3)],
        [t_(0), t_(1)],
        [o_(4)],
        [o_(5), o_(6)],
        [c_(2), o_(3), t_(4)],
        [],
        [t_(5), t_(3), t_(6)],
        [],
        [o_(2), t_(2)],
        [s_(5)],
        [s_(2), s_(0), s_(1), s_(3), s_(4), s_(6)],
    ]
    for steps in order:
        pump.add(lambda steps=steps: [step() for step in steps])

    got_mask, got_back = net.land(), net.land(2)
    owner = device(y, lax.rem(z, 2), lax.div(z, 2), block_id)
    is_owner = block_id == z
    net.send(masks, mask_rows, owner, got_mask, is_owner)
    gz_in = net.land(4)
    for peer, pz in peers:
        net.send(gain_part, gz.at[z], peer, gz_in + z)
    net.local(gain_part, gz.at[z], gz_in + z)
    gh_in = net.land(3)

    def gain_first():
        for part in range(4):
            net.wait(gz.at[part], gz_in + part)
        gain_sum[...] = gz[0] + gz[1] + gz[2] + gz[3]
        gh[0] = gain_sum[...]
        net.send(gh.at[0], gh.at[3], xdev, gh_in)

    def gain_next(i, to):
        net.wait(gh.at[2 + i], gh_in + i - 1)
        gain_sum[...] += gh[2 + i]
        if to is not None:
            gh[i] = gain_sum[...]
            net.send(gh.at[i], gh.at[3 + i], to, gh_in + i)

    net.wait(own_wpo, got_wpo)
    z2p, z2c = z2[0:PATCH, :], z2[PATCH:ROWS, :]
    d_pp, d_cc = dpc[0:PATCH, :], dpc[PATCH:ROWS, :]
    gr[:, PATCH_AT : PATCH_AT + 768] = tn(z2p, d_pp).astype(BF)
    gr[:, CLASS_AT : CLASS_AT + 768] = tn(z2c, d_cc).astype(BF)
    core_send(0)
    dz_f[0:PATCH, :] = nt(d_pp, wpo[:, 768:1536])
    dz_f[PATCH:ROWS, :] = nt(d_cc, wpo[:, 1536:2304])
    dzb[...] = dz_f[...].astype(BF)
    net.wait(znt, got_early)
    net.wait(pool0, got_gl)
    net.wait(pool1, got_sl)
    for i in range(8):
        net.wait(wds.at[i % 2], got_wd + i)
        net.wait(wus.at[i % 2], got_wu + i)
        rows = pl.ds(ROWS * (i // 2), ROWS)
        cols = pl.ds(PANEL * (i % 2), PANEL)
        d_u = (nt(dzb[...], wds[i % 2]) * pool1[rows, cols].astype(F32)).astype(BF)
        gd[PANEL * i : PANEL * i + PANEL, :] = tn(pool0[rows, cols], dzb[...]).astype(BF)
        gr[:, UP_AT + PANEL * i : UP_AT + PANEL * i + PANEL] = nn(znt[...], d_u).astype(BF)
        part = nt(d_u, wus[i % 2])
        if i == 0:
            dzn[...] = part
        else:
            dzn[...] += part
        if i + 2 < 8:
            load(i + 2)
        if i == 0:
            gain_first()
        if i == 2:
            gain_next(1, ydev)
        if i == 4:
            gain_next(2, sib)
        if i == 6:
            gain_next(3, None)
        if i == 3:
            core_send(1)
            pump.run(1)
        if i == 7:
            core_send(2)
            pump.run(1)
    mark = len(net.open)
    for k in (3, 4, 5):
        core_send(k)
    dsent = net.take(mark)
    for i, (_, dst) in enumerate(early):
        if i:
            net.wait(dst, got_early + i)
    d_zn = dzn[...]
    normed = h_f[...]
    normed = (normed - jnp.mean(normed, axis=-1, keepdims=True)) * inv[:, 0:1]
    d_h = dz_f[...] + inv[:, 0:1] * (
        d_zn
        - jnp.mean(d_zn, axis=-1, keepdims=True)
        - normed * jnp.mean(d_zn * normed, axis=-1, keepdims=True)
    )
    dz_f[...] = d_h
    d_hb = d_h.astype(BF)
    net.wait(wpo.at[:, pl.ds(0, 768)], got_wo)
    dob, dh = dzb, dz_f
    dob[...] = nt(d_hb, wpo[:, 0:768]).astype(BF)

    got_do = net.land(4)

    def piece(q):
        return dob.at[:, lanes_of(384 * lax.div(q, 2) + 128 * lax.rem(q, 2), 256)]

    net.local(piece(quarter), d_out.at[own_rows], got_do + block_id)
    for to, q, _ in group:
        net.send(piece(q), d_out.at[own_rows], to, got_do + block_id)
    gr[:, OUT_AT : OUT_AT + 768] = tn(att[...], d_hb).astype(BF)
    core_send(6)
    pump.run(1)
    for i, (_, dst) in enumerate(kept):
        net.wait(dst, got_kept + i)
    kh, vh = pool0, pool1

    lead_len, tail_len = aux[0:1, 0:1], aux[1:2, 0:1]
    key_col = lax.broadcasted_iota(jnp.int32, (SLOT_ROWS, 1), 0)
    key_seg, key_filler = segments(key_col, lead_len, tail_len)
    key_seg = jnp.where(key_seg < 0, -5, key_seg)
    masked = jnp.where(key_filler, -3e38, -1e30)
    def dqkv(q):
        return gd.at[rows_of(384 * tok_of2(q, 1 - c), ROWS)]

    for head in range(3):
        mine = own_lanes(c, head, (SLOT_ROWS, 256))
        cols = pl.ds(256 * head, 256)
        kh[:, cols] = jnp.where(mine, kr[...], 0.0).astype(BF)
        vh[:, cols] = jnp.where(mine, vr[...], 0.0).astype(BF)
    lane = lax.broadcasted_iota(jnp.int32, (8, 256), 1)
    row8 = lax.broadcasted_iota(jnp.int32, (8, 256), 0)
    picker = jnp.where((row8 < 3) & (lane // 64 - c == row8), 1.0, 0.0)
    for n, q in enumerate([block_id] + [q for _, _, q in group]):
        rows = rows_of(q * ROWS, ROWS)
        net.wait(d_out.at[rows], got_do + q)
        query, d_result = qr[rows, :], d_out[rows, :]
        stat = stats[rows, :].T
        product = d_result.astype(F32) * out[rows, :].astype(F32)
        delta = lax.dot_general(
            picker,
            product,
            (((1,), (1,)), ((), ())),
            precision=lax.Precision.HIGHEST,
            preferred_element_type=F32,
        )
        query_row = lax.broadcasted_iota(jnp.int32, (1, ROWS), 1) + q * ROWS
        query_seg = segments(query_row, lead_len, tail_len)[0]
        d_query = jnp.zeros((ROWS, 256), F32)
        for head in range(3):
            mine = own_lanes(c, head, (ROWS, 256))
            cols = pl.ds(256 * head, 256)
            own_query = jnp.where(mine, query, 0.0).astype(BF)
            own_result = jnp.where(mine, d_result, 0.0).astype(BF)
            for side in range(2):
                low, high = side * SLOT_ROWS // 2, (side + 1) * SLOT_ROWS // 2
                keys = pl.ds(low, SLOT_ROWS // 2)
                key = kh[keys, cols]
                allowed = key_seg[low:high] == query_seg
                scores = jnp.where(allowed, nt(key, query), masked[low:high])
                probs = jnp.exp(scores - stat[head : head + 1, :])
                d_probs = nt(vh[keys, cols], d_result)
                d_scores = jnp.where(allowed, probs * (d_probs - delta[head : head + 1, :]), 0.0)
                d_scores = d_scores.astype(BF)
                d_query = d_query + tn(d_scores, key)
                d_key = nn(d_scores, own_query)
                d_value = nn(probs.astype(BF), own_result)
                if n == 0 and head == 0:
                    dk[keys, :] = d_key
                    dv[keys, :] = d_value
                else:
                    dk[keys, :] += d_key
                    dv[keys, :] += d_value
            pump.run(1)
        if n == 0:
            net.finish_some(dsent)
        dqkv(q)[:, 0:256] = (d_query * 0.125).astype(BF)
    for q in range(4):
        rows = pl.ds(ROWS * q, ROWS)
        dqkv(q)[:, 256:512] = dk[rows, :].astype(BF)
        dqkv(q)[:, 512:768] = dv[rows, :].astype(BF)
    got_xs = net.land()
    net.local(xs_in, pool1, got_xs)

    fb_in, fc_in = net.land(2), net.land(2)
    halves = (pl.ds(0, 176), pl.ds(176, 160))
    (_, _, sib_q), (_, _, cross_q), (_, _, diag_q) = group

    def first(q):
        rows = rows_of(q * ROWS, ROWS)
        pool0[rows, :] = nt(dqkv(q)[...], wp[...]).astype(BF)
        return pool0.at[rows]

    net.send(first(diag_q), fb.at[0], sib, fb_in)
    net.send(first(sib_q), fb.at[1], sib, fb_in + 1)
    far = first(cross_q)
    net.wait(fb.at[0], fb_in)
    for i, part in enumerate(halves):
        add_into(far.at[part], fb.at[0, part], 256)
        net.send(far.at[part], fc.at[part], xdev, fc_in + i)
    near = first(block_id)

    qb_in = [net.land(4) for _ in range(3)]
    qy_in, qx_in, qz_in = net.land(6), net.land(3), [net.land(4) for _ in range(3)]
    first_core = c == 0

    gq = wpo.at[:, pl.ds(0, 768)]

    def hq(b):
        return wpo.at[rows_of(96 * b, 96), pl.ds(768, 1152)]

    def fq(part):
        return wds.at[0, pl.ds(96 * part, 96)]

    def q_make(part):
        cols = pl.ds(256 * part, 256)
        total = tn(pool1[0:ROWS, :], dqkv(0)[:, cols])
        for q in range(1, 4):
            total = total + tn(pool1[ROWS * q : ROWS * q + ROWS, :], dqkv(q)[:, cols])
        gq[:, cols] = total.astype(BF)
        for b in range(4):
            net.send(gq.at[blk(tok_of(b, 1 - c)), cols], rq.at[b, :, cols], sib, qb_in[part] + b)

    def q_core(part):
        cols = pl.ds(256 * part, 256)
        half = pl.ds(384 * part, 384)
        base = 384 * part
        for b in range(4):
            net.wait(rq.at[b, :, cols], qb_in[part] + b)
            own = gq[blk(tok_of(b, c)), cols].astype(F32)
            new = rq[b, :, cols].astype(F32)
            left, right = jnp.where(first_core, own, new), jnp.where(first_core, new, own)
            hq(b)[:, base : base + 128] = left[:, 0:128].astype(BF)
            hq(b)[:, base + 128 : base + 256] = (left[:, 128:256] + right[:, 0:128]).astype(BF)
            hq(b)[:, base + 256 : base + 384] = right[:, 128:256].astype(BF)
        for side in range(2):
            net.send(
                hq(2 * (1 - y) + side).at[:, half], ryq.at[side, :, half], ydev, qy_in + 2 * part + side
            )

    def q_one(part):
        half = pl.ds(384 * part, 384)
        for side in range(2):
            net.wait(ryq.at[side, :, half], qy_in + 2 * part + side)
            add_into(hq(2 * y + side).at[:, half], ryq.at[side, :, half], 384)
        net.send(hq(2 * y + 1 - x).at[:, half], rxq.at[:, half], xdev, qx_in + part)

    def q_two(part):
        half = pl.ds(384 * part, 384)
        both = pl.ds(768 * part, 768)
        net.wait(rxq.at[:, half], qx_in + part)
        fq(part)[:, lanes_of(384 * x, 384)] = hq(2 * y + x)[:, half]
        fq(part)[:, lanes_of(384 * (1 - x), 384)] = rxq[:, half]
        split_rows(fq(part), spq.at[:, :, both], 384)
        for peer, pz in peers:
            net.send(spq.at[pz, :, both], rzq.at[z, :, both], peer, qz_in[part] + z)
        net.local(spq.at[z, :, both], rzq.at[z, :, both], qz_in[part] + z)

    def q_sum(part):
        both = pl.ds(768 * part, 768)
        for src in range(4):
            net.wait(rzq.at[src, :, both], qz_in[part] + src)
        sum_parts(rzq.at[:, :, both], sum_q.at[:, both], 384)

    def finish_rows(i):
        part = halves[i]
        net.wait(fc.at[part], fc_in + i)
        d_zn = near[part, :].astype(F32) + fc[part, :].astype(F32)
        normed, scale = normalise(back[part, :].astype(F32))
        d_x = dh[part, :] + scale * (
            d_zn
            - jnp.mean(d_zn, axis=-1, keepdims=True)
            - normed * jnp.mean(d_zn * normed, axis=-1, keepdims=True)
        )
        back[part, :] = d_x.astype(BF)
        net.send(back.at[part], d_rows.at[part], owner, got_back + i, is_owner)

    net.wait(pool1, got_xs)

    def norm_step(i, carry):
        rows = rows_of(i * ROWS, ROWS)
        pool1[rows, :] = normalise(pool1[rows, :].astype(F32))[0].astype(BF)
        return carry

    lax.fori_loop(0, 4, norm_step, 0)
    q_make(0)
    q_make(1)
    q_core(0)
    q_make(2)
    q_core(1)
    q_core(2)
    net.wait(back, got_xb)
    net.wait(fb.at[1], fb_in + 1)
    add_into(near, fb.at[1], 256)
    pump.run(1)
    finish_rows(0)
    finish_rows(1)
    pump.run(1)
    for part in range(3):
        q_one(part)
    pump.run(1)
    for part in range(3):
        q_two(part)
    pump.run()
    for part in range(3):
        q_sum(part)
    net.wait(mask_rows, got_mask)
    for i, part in enumerate(halves):
        net.wait(d_rows.at[part], got_back + i)
    net.finish()


def last_kernel(
    d_rows, mask_rows, sum_q, sum_r, sum_d, gain_sum, w_qkv, w_up, g1, g2,
    masks, d_patches, d_classes, d_qkv, d_out, d_up, d_down, d_patch, d_class, d_one, d_two, d_gain,
):
    masks[...] = nt(spread_matrix(BF, (2 * REAL, 256), 1), mask_rows[...])
    d_patches[...] = d_rows[0:PATCH, :].astype(F32)
    d_classes[...] = d_rows[PATCH : PATCH + REAL, :].astype(F32)
    total = sum_q[...]
    d_qkv[...] = total * column(g1)
    ones = jnp.ones((8, total.shape[1]), F32)
    d_one[...] = exact(ones, total * w_qkv[...].astype(F32), ((1,), (1,)))[0:1, :]
    total = sum_r[:, UP_AT : UP_AT + 3072]
    d_up[...] = total * column(g2)
    ones = jnp.ones((8, total.shape[1]), F32)
    d_two[...] = exact(ones, total * w_up[...].astype(F32), ((1,), (1,)))[0:1, :]
    d_out[...] = sum_r[:, OUT_AT : OUT_AT + 768]
    d_down[...] = sum_d[...]
    d_patch[...] = sum_r[:, PATCH_AT : PATCH_AT + 768]
    d_class[...] = sum_r[:, CLASS_AT : CLASS_AT + 768]
    d_gain[...] = exact(gain_sum[...], spread_matrix(F32, (256, 2 * REAL), 0), ((1,), (0,)))[0:1, :]


VMEM_SPEC = pl.BlockSpec(memory_space=pltpu.VMEM)
ANY_SPEC = pl.BlockSpec(memory_space=pl.ANY)


def call(body, ident, specs, outs, scratch, sems, args, cost):
    out_shape = tuple(jax.ShapeDtypeStruct(shape, kind) for shape, kind, _ in outs)
    scratch_shapes = [pltpu.VMEM(shape, kind) for shape, kind in scratch]
    if sems:
        scratch_shapes += [pltpu.SemaphoreType.DMA((n,)) for n in sems]
    extra = {} if ident is None else dict(collective_id=ident, has_side_effects=True)
    return pl.pallas_call(
        body,
        out_shape=out_shape,
        in_specs=list(specs),
        out_specs=tuple(spec for _, _, spec in outs),
        scratch_shapes=scratch_shapes,
        compiler_params=pltpu.CompilerParams(vmem_limit_bytes=63 * 2**20, **extra),
        cost_estimate=pl.CostEstimate(flops=cost, bytes_accessed=2**24, transcendentals=0),
    )(*args)


def home_plan(
    patches,
    classes,
    slot_lengths,
    w_qkv,
    w_out,
    w_up,
    w_down,
    w_patch,
    w_class,
    norm1,
    norm2,
    mask_gain,
    d_masks,
):
    V, A = VMEM_SPEC, ANY_SPEC
    wide = 3 * w_out.shape[1] + w_up.shape[1]
    rows = w_qkv.shape[0]
    g1, g2 = norm1.reshape(1, rows), norm2.reshape(1, rows)
    slot, part = (SLOT_ROWS, 768), (SLOT_ROWS, 256)
    row_shape = (ROWS, 768)
    kept = call(
        front_kernel,
        1,
        [V] * 13,
        [
            (row_shape, BF, V),
            (row_shape, BF, V),
            ((768, ROWS), BF, A),
            (row_shape, F32, A),
            ((ROWS, 128), F32, A),
            (row_shape, BF, A),
            ((PATCH, 256), BF, V),
            ((8, 256), F32, V),
            (slot, BF, A),
            (slot, BF, A),
            ((768, wide), BF, A),
            ((3072, 768), BF, A),
            (slot, BF, A),
            (part, BF, A),
            (part, BF, A),
            (part, BF, A),
            (part, BF, A),
            ((SLOT_ROWS, 128), F32, A),
            ((768, 768), BF, A),
            ((8, 128), jnp.int32, A),
        ],
        [
            (slot, BF),
            (slot, BF),
            (part, BF),
            (part, BF),
            (part, BF),
            (part, BF),
            ((SLOT_ROWS, 128), F32),
            ((768, 768), BF),
            ((768, 1152), BF),
            ((768, wide), BF),
            ((3072, 768), BF),
            ((4, 24, 2304), BF),
            ((4, 24, wide), BF),
            ((96, 2304), BF),
            (slot, BF),
            (slot, BF),
            ((PATCH, 256), BF),
            ((8, 128), jnp.int32),
            ((CLS, 768), BF),
            ((PATCH, 256), BF),
            ((8, 128), jnp.int32),
            ((24, 2304), BF),
            ((24, wide), BF),
            ((4, ROWS, 256), BF),
            (row_shape, BF),
            ((PATCH, 768), F32),
            ((4 * CLS, 768), BF),
            ((4 * CLS, 768), BF),
            ((4, CLS, 768), BF),
            ((768, ROWS), BF),
            (row_shape, F32),
            ((ROWS, 128), F32),
            (row_shape, BF),
        ],
        (200, 260),
        (
            patches,
            classes,
            slot_lengths,
            w_qkv,
            w_out,
            w_up,
            w_down,
            w_patch,
            w_class,
            g1,
            g2,
            mask_gain.reshape(1, -1),
            d_masks.T,
        ),
        10**10,
    )
    d_rows, mask_rows, sum_q, sum_r, sum_d, gain_sum = call(
        back_kernel,
        2,
        [V, V] + [A] * 5 + [V] + [A] * 11 + [V],
        [
            (row_shape, BF, A),
            ((PATCH, 256), BF, A),
            ((24, 2304), F32, V),
            ((24, wide), F32, V),
            ((96, 768), F32, V),
            ((8, 256), F32, V),
        ],
        [
            (slot, BF),
            (slot, BF),
            ((768, 2304), BF),
            ((2, PANEL, 768), BF),
            ((2, 768, PANEL), BF),
            ((768, wide), BF),
            ((3072, 768), BF),
            ((4, 96, wide), BF),
            ((4, 384, 768), BF),
            ((2, 96, wide), BF),
            ((96, wide), BF),
            ((2, 384, 768), BF),
            ((384, 768), BF),
            ((4, 24, wide), BF),
            ((4, 24, wide), BF),
            ((4, 96, 768), BF),
            ((4, 96, 768), BF),
            ((2, 96, 1152), BF),
            ((96, 1152), BF),
            ((4, 24, 2304), BF),
            ((4, 24, 2304), BF),
            ((2, ROWS, 768), BF),
            (row_shape, BF),
            (row_shape, BF),
            ((4, 8, 256), F32),
            ((6, 8, 256), F32),
            (part, F32),
            (part, F32),
            (part, BF),
            (row_shape, F32),
            (row_shape, BF),
            (row_shape, F32),
            (part, BF),
            (part, BF),
            (part, BF),
            (part, BF),
            ((SLOT_ROWS, 128), F32),
            ((768, 768), BF),
            ((768, ROWS), BF),
            (row_shape, F32),
            ((ROWS, 128), F32),
            (row_shape, BF),
        ],
        (160, 240),
        kept,
        10**10,
    )
    square = ((rows, 768), F32, V)
    masks, d_patches, d_classes, d_qkv, d_w_out, d_up, d_down, d_patch, d_class, d_one, d_two, d_gain = call(
        last_kernel,
        None,
        [V] * 10,
        [
            (d_masks.shape[::-1], F32, V),
            (patches.shape, F32, V),
            (classes.shape, F32, V),
            (w_qkv.shape, F32, V),
            square,
            (w_up.shape, F32, V),
            (w_down.shape, F32, V),
            square,
            square,
            ((1, rows), F32, V),
            ((1, rows), F32, V),
            ((1, 2 * REAL), F32, V),
        ],
        [],
        (),
        (d_rows, mask_rows, sum_q, sum_r, sum_d, gain_sum, w_qkv, w_up, g1, g2),
        10**7,
    )
    return (
        masks.T,
        d_patches,
        d_classes,
        d_qkv,
        d_w_out,
        d_up,
        d_down,
        d_patch,
        d_class,
        d_one.reshape(-1),
        d_two.reshape(-1),
        d_gain.reshape(-1),
    )


def solution(mesh):
    placed = (
        P(("tok", "head"), None),
        P(("tok", "head"), None),
        P("tok", None),
        P(("tok", "head"), None),
        P(("tok", "head"), None),
        P(("tok", "head"), None),
        P(("tok", "head"), None),
        P(("tok", "head"), None),
        P(("tok", "head"), None),
        P(("tok", "head")),
        P(("tok", "head")),
        P(),
        P(("tok", "head"), None),
    )
    fits = mesh.shape["tok"] == 8 and mesh.shape["head"] == 4
    return jax.shard_map(
        home_plan if fits else per_device,
        mesh=mesh,
        in_specs=placed,
        out_specs=(
            P(("tok", "head"), None),
            P(("tok", "head"), None),
            P(("tok", "head"), None),
            P(("tok", "head"), None),
            P(("tok", "head"), None),
            P(("tok", "head"), None),
            P(("tok", "head"), None),
            P(("tok", "head"), None),
            P(("tok", "head"), None),
            P(("tok", "head")),
            P(("tok", "head")),
            P(),
        ),
        check_vma=False,
    )
```
